32 devices in a mesh: req: 4 (over y, x), blk: 8 (over z, core).
Axes of the slice: x: 2, y: 2, z: 4, core: 2. Of those that a mesh axis runs over, the one named last changes fastest.
Arguments:
- tokens: bfloat16 [4, 1024, 2048], P('req', 'blk'), may hold values from -6 to 6
- block_ids: int32 [4, 16], P('req', 'blk'), may hold values from 0 to 15, as said below
- lengths: int32 [4], P('req'), may hold values from 513 to 1024, as said below
- page_table: int32 [4, 2, 16], P('req'), may hold values from 0 to 31, as said below
- qkv_weight: bfloat16 [2048, 3072], P(('req', 'blk')), may hold values from -0.125 to 0.125
- q_gain: float32 [256], replicated
- k_gain: float32 [256], replicated
Outputs:
- attended: bfloat16 [4, 1024, 2048], P('req', 'blk')
- kv_cache: bfloat16 [4, 32, 64, 512], P('req', 'blk')
The draws below stay inside these ranges and needn't reach their ends.
Inputs may be any that keep to these rules, and one draw needn't show every extreme that they name: `lengths`: one prompt has length exactly 1024. `block_ids`: the two entries of one device are b and 15 - b; over a prompt the first entries are a permutation of 0 to 7. `page_table`: each prompt's entries are a permutation of 0 to 31.
All inputs are finite; a program needn't handle non-finite values.
Results may differ from the reference program's by a relative error of at most 0.013.
The reference program's roundings to bfloat16 on the way count: a program that leaves them out, or rounds other values in their place, can miss the bound.
Values may be sent and summed in bfloat16 or wider, within the bound.
No kernel may reach another device: no remote copies, remote signals or barrier semaphores. Data moves between devices by JAX's collectives and lax.ppermute only.
A program may use at most 128 MiB of HBM per device.

```python
import math
import jax
import jax.numpy as jnp
from jax import lax

D = 2048
H = 8
KVH = 2
HD = 256
BLK_ROWS = 64
SEQ = 1024
QKV = 3072
N_REQ = 4
N_BLK = 8


def draw_lengths(key, part):
    first_key = jax.random.fold_in(key, 101)
    second_key = jax.random.fold_in(key, 102)
    drawn = jax.random.randint(first_key, (N_REQ,), SEQ // 2 + 1, SEQ + 1)
    longest = jax.random.randint(second_key, (), 0, N_REQ)
    return jnp.where(jnp.arange(N_REQ) == longest, SEQ, drawn).astype(jnp.int32)


def draw_block_ids(key, part):
    base_key = jax.random.fold_in(key, 201)
    orders = jnp.stack([jax.random.permutation(jax.random.fold_in(base_key, request), N_BLK) for request in range(N_REQ)])
    paired = jnp.stack([orders, 2 * N_BLK - 1 - orders], -1)
    return paired.reshape(N_REQ, 2 * N_BLK).astype(jnp.int32)


def draw_page_table(key, part):
    base_key = jax.random.fold_in(key, 301)
    orders = jnp.stack([jax.random.permutation(jax.random.fold_in(base_key, request), KVH * 2 * N_BLK) for request in range(N_REQ)])
    return orders.reshape(N_REQ, KVH, 2 * N_BLK).astype(jnp.int32)


def gain_values(key):
    return jnp.exp(jax.random.uniform(key, (HD,), jnp.float32, jnp.log(0.28), jnp.log(0.56)))


def draw_q_gain(key, part):
    return gain_values(jax.random.fold_in(key, 401))


def draw_k_gain(key, part):
    return gain_values(jax.random.fold_in(key, 402))


def level_of(own_key, dims, pieces, least, top_value):
    loudness, own = 1.0, jax.random.fold_in(own_key, 6)
    for dim, parts in pieces:
        steps = jnp.exp(jax.random.uniform(jax.random.fold_in(own, dim), (parts,), jnp.float32, least / len(pieces), top_value / len(pieces)))
        loudness = loudness * jnp.repeat(steps, dims[dim] // parts).reshape([-1 if axis == dim else 1 for axis in range(len(dims))])
    return loudness


def bell_draw(key, extent, width, limit, split=(), held_as=jnp.bfloat16):
    values = width * jax.random.normal(key, extent, jnp.float32)
    if split:
        values = values * level_of(key, extent, split, -0.22, 0.18)
    return jnp.clip(values, -limit, limit).astype(held_as)


def setup_inputs(seed: int = 0) -> dict:
    splits = jax.random.split(jax.random.key(seed), 8)
    return {
        "tokens": bell_draw(splits[0], (N_REQ, SEQ, D), 1.0, 6.0, ((0, 4), (1, 8))),
        "block_ids": draw_block_ids(jax.random.fold_in(splits[7], 71), 0),
        "lengths": draw_lengths(jax.random.fold_in(splits[7], 71), 0),
        "page_table": draw_page_table(jax.random.fold_in(splits[7], 71), 0),
        "qkv_weight": bell_draw(splits[4], (D, QKV), D ** -0.5, 0.125, ((0, 32),)),
        "q_gain": draw_q_gain(jax.random.fold_in(splits[7], 71), 0),
        "k_gain": draw_k_gain(jax.random.fold_in(splits[7], 71), 0),
    }


ROPE_BASE = 1000000.0
NORM_EPS = 1e-06
FLOOR_SCORE = -1e+30

def head_norm(tensor, scale_gain):
    return tensor * lax.rsqrt(lax.optimization_barrier(jnp.mean(tensor * tensor, axis=-1, keepdims=True)) + NORM_EPS) * scale_gain

def rotary(tensor, positions):
    half_dim = tensor.shape[-1] // 2
    channel = jnp.arange(half_dim).astype(jnp.float32)
    inverse = jnp.power(jnp.float32(ROPE_BASE), -2.0 * channel / tensor.shape[-1])
    angles = positions.astype(jnp.float32)[:, None] * inverse[None, :]
    cosine = jnp.cos(angles)[:, None, :]
    sine_part = jnp.sin(angles)[:, None, :]
    front_half = tensor[..., :half_dim]
    second = tensor[..., half_dim:]
    return jnp.concatenate([front_half * cosine - second * sine_part, second * cosine + front_half * sine_part], -1)

def reference(tokens, block_ids, lengths, page_table, qkv_weight, q_gain, k_gain):
    groups = H // KVH
    query_block = math.gcd(SEQ, 512)
    block_total = SEQ // query_block
    attended_list = []
    cache_list = []
    for request in range(N_REQ):
        positions = (block_ids[request][:, None] * BLK_ROWS + jnp.arange(BLK_ROWS, dtype=jnp.int32)[None, :]).reshape(SEQ).astype(jnp.int32)
        projected = jnp.dot(tokens[request], qkv_weight, preferred_element_type=jnp.float32)
        query_raw = projected[:, :H * HD].reshape(SEQ, H, HD)
        key_raw = projected[:, H * HD:(H + KVH) * HD].reshape(SEQ, KVH, HD)
        value_raw = projected[:, (H + KVH) * HD:].reshape(SEQ, KVH, HD)
        queries = rotary(head_norm(query_raw, q_gain), positions).astype(jnp.bfloat16)
        key_rows = rotary(head_norm(key_raw, k_gain), positions).astype(jnp.bfloat16)
        values = head_norm(value_raw, 1.0).astype(jnp.bfloat16)
        length = lengths[request]
        grouped = lax.optimization_barrier(queries).astype(jnp.float32).reshape(SEQ, KVH, groups, HD)
        key_wide = lax.optimization_barrier(key_rows).astype(jnp.float32)
        value_wide = lax.optimization_barrier(values).astype(jnp.float32)
        key_live = positions < length

        def attend(block_number):
            query_rows = lax.dynamic_slice_in_dim(grouped, block_number * query_block, query_block, 0)
            query_pos = lax.dynamic_slice_in_dim(positions, block_number * query_block, query_block, 0)
            scores = jnp.einsum('rgad,kgd->rgak', query_rows, key_wide)
            allowed = ((positions[None, :] <= query_pos[:, None]) & key_live[None, :])[:, None, None, :]
            row_max = lax.optimization_barrier(jnp.max(jnp.where(allowed, scores, FLOOR_SCORE), -1, keepdims=True))
            weights = jnp.where(allowed, jnp.exp(scores - row_max), 0.0)
            row_sum = lax.optimization_barrier(jnp.sum(weights, -1))
            rounded = lax.optimization_barrier(weights.astype(jnp.bfloat16)).astype(jnp.float32)
            summed = jnp.einsum('rgak,kgd->rgad', rounded, value_wide)
            query_live = query_pos < length
            divisor = jnp.where(query_live[:, None, None], row_sum, 1.0)
            result = jnp.where(query_live[:, None, None, None], summed / divisor[..., None], 0.0)
            return result.reshape(query_block, H * HD).astype(jnp.bfloat16)
        attended_list.append(lax.map(attend, jnp.arange(block_total)).reshape(SEQ, H * HD))
        kv_rows = jnp.concatenate([key_rows, values], -1)
        kv_rows = jnp.where(key_live[:, None, None], kv_rows, jnp.zeros_like(kv_rows))
        ordered = jnp.zeros_like(kv_rows).at[positions].set(kv_rows)
        page_rows = ordered.reshape(2 * N_BLK, BLK_ROWS, KVH, 2 * HD).transpose(2, 0, 1, 3).reshape(KVH * 2 * N_BLK, BLK_ROWS, 2 * HD)
        cache_list.append(jnp.zeros_like(page_rows).at[page_table[request].reshape(-1).astype(jnp.int32)].set(page_rows))
    return (jnp.stack(attended_list), jnp.stack(cache_list))
```

```python
import functools

import jax
import jax.numpy as jnp
from jax import lax
from jax.experimental import pallas as pl
from jax.experimental.pallas import tpu as pltpu
from jax.sharding import PartitionSpec as P

H = 8
KVH = 2
HD = 256
GROUPS = H // KVH
TEAM = 4
ROPE_BASE = 1000000.0
NORM_EPS = 1e-06
FLOOR_SCORE = -1e30
VMEM_LIMIT = 56 * 1024 * 1024

ANY = pl.BlockSpec(memory_space=pl.ANY)
VMEM = pl.BlockSpec(memory_space=pltpu.VMEM)
SMEM = pl.BlockSpec(memory_space=pltpu.SMEM)


def params():
    return pltpu.CompilerParams(vmem_limit_bytes=VMEM_LIMIT)


def place():
    blk = lax.axis_index("blk")
    return lax.axis_index("req"), blk // TEAM, (blk // 2) % 2, blk % 2


def q_start(pair, core):
    return pl.multiple_of((pair * 2 + core) * 2 * HD, 2 * HD)


def kv_start(pair, core):
    return pl.multiple_of(H * HD + core * KVH * HD + pair * HD, HD)


def pack_kernel(w_ref, *outs):
    _, _, pair, core = place()
    for k in range(1, TEAM):
        to_pair, to_core = pair ^ (k // 2), core ^ (k % 2)
        outs[k - 1][...] = w_ref[:, pl.ds(kv_start(to_pair, to_core), HD)]
        outs[TEAM - 2 + k][...] = w_ref[:, pl.ds(q_start(to_pair, to_core), 2 * HD)]


def team_kernel(is_kv, w_ref, *refs):
    _, _, pair, core = place()
    out = refs[-1]
    rows = w_ref.shape[0]
    width = out.shape[1]
    start = kv_start(pair, core) if is_kv else q_start(pair, core)
    member = pair * 2 + core
    out[pl.ds(pl.multiple_of(member * rows, rows), rows), :] = w_ref[:, pl.ds(start, width)]
    for k in range(1, TEAM):
        out[pl.ds(pl.multiple_of((member ^ k) * rows, rows), rows), :] = refs[k - 1][...]


def project_kernel(n_out, pieces, is_kv, *refs):
    tokens = refs[:TEAM]
    weights = refs[TEAM : TEAM + len(pieces)]
    gain_ref, cos_ref, sin_ref, out, x_all, w_all, x_sem, w_sem = refs[TEAM + len(pieces) :]
    req, outer, _, core = place()
    rows = tokens[0].shape[0]
    copies = []
    for k in range(TEAM):
        slot = (core ^ (k % 2)) + (k // 2) * 2
        copies.append(
            pltpu.make_async_copy(
                tokens[k], x_all.at[pl.ds(pl.multiple_of(slot * rows, rows), rows), :], x_sem.at[k]
            )
        )
    depth = weights[0].shape[0]
    for i, (dr, ko) in enumerate(pieces):
        from_outer = lax.rem(outer + n_out - ko, n_out)
        index = (req ^ dr) * n_out + from_outer
        copies.append(
            pltpu.make_async_copy(
                weights[i], w_all.at[pl.ds(pl.multiple_of(index * depth, depth), depth), :], w_sem.at[i]
            )
        )
    for copy in copies:
        copy.start()
    for copy in copies:
        copy.wait()
    half = HD // 2
    for j in range(TEAM):
        mine = slice(j * rows, (j + 1) * rows)
        product = jnp.dot(x_all[mine, :], w_all[...], preferred_element_type=jnp.float32)
        cosine, sine = cos_ref[mine, :], sin_ref[mine, :]
        gain = gain_ref[...]
        if is_kv:
            is_key = core == 0
            cosine = jnp.where(is_key, cosine, 1.0)
            sine = jnp.where(is_key, sine, 0.0)
            gain = jnp.where(is_key, gain, 1.0)
        for h in range(out.shape[1] // HD):
            head = product[:, h * HD : (h + 1) * HD]
            mean = jnp.mean(head * head, axis=-1, keepdims=True)
            head = head * lax.rsqrt(mean + NORM_EPS) * gain
            front, second = head[:, :half], head[:, half:]
            out[mine, h * HD : h * HD + half] = (front * cosine - second * sine).astype(jnp.bfloat16)
            out[mine, h * HD + half : (h + 1) * HD] = (second * cosine + front * sine).astype(jnp.bfloat16)


def load_kv(n_out, mine, other, store, sems, core):
    rows = mine[0].shape[0]
    copies = []
    for k in range(n_out):
        here = pl.ds(k * rows, rows)
        copies.append(pltpu.make_async_copy(mine[k], store.at[core, here, :], sems.at[0, k]))
        copies.append(pltpu.make_async_copy(other[k], store.at[1 - core, here, :], sems.at[1, k]))
    for copy in copies:
        copy.start()
    for copy in copies:
        copy.wait()


def attend_kernel(n_out, parts, *refs):
    mine, other = refs[:n_out], refs[n_out : 2 * n_out]
    q_ref, qpos_ref, kpos_ref, length_ref = refs[2 * n_out : 2 * n_out + 4]
    outs = refs[2 * n_out + 4 : 2 * n_out + 4 + len(parts)]
    store, sems = refs[2 * n_out + 4 + len(parts) :]
    _, _, _, core = place()
    load_kv(n_out, mine, other, store, sems, core)
    length = length_ref[0]
    rows = outs[0].shape[0]
    key_pos = kpos_ref[...]
    key_pos = jnp.where(key_pos < length, key_pos, jnp.iinfo(jnp.int32).max)
    for part, out in zip(parts, outs):
        slot = (core ^ (part % 2)) + (part // 2) * 2
        here = pl.ds(pl.multiple_of(slot * rows, rows), rows)
        query_pos = qpos_ref[here, :]
        allowed = key_pos <= query_pos
        live = query_pos < length
        for h in range(2):
            cols = slice(h * HD, (h + 1) * HD)
            scores = lax.dot_general(
                q_ref[here, cols], store[0], (((1,), (1,)), ((), ())), preferred_element_type=jnp.float32
            )
            scores = jnp.where(allowed, scores, FLOOR_SCORE)
            row_max = jnp.max(scores, axis=-1, keepdims=True)
            weights = jnp.where(allowed, jnp.exp(scores - row_max), 0.0)
            row_sum = jnp.sum(weights, axis=-1, keepdims=True)
            summed = jnp.dot(weights.astype(jnp.bfloat16), store[1], preferred_element_type=jnp.float32)
            divisor = jnp.where(live, row_sum, 1.0)
            out[:, cols] = jnp.where(live, summed / divisor, 0.0).astype(jnp.bfloat16)


def pages_kernel(n_out, blk_rows, *refs):
    mine, other = refs[:n_out], refs[n_out : 2 * n_out]
    info_ref, own, away, store, sems = refs[2 * n_out :]
    _, _, _, core = place()
    load_kv(n_out, mine, other, store, sems, core)
    slots = own.shape[0]
    row = lax.broadcasted_iota(jnp.int32, (blk_rows, HD), 0)
    for target, base in ((own, 0), (away, slots)):
        for i in range(slots):
            start = pl.multiple_of(info_ref[1, base + i] * blk_rows, blk_rows)
            live = row < info_ref[2, base + i]
            for half in range(2):
                page = store[half, pl.ds(start, blk_rows), :].astype(jnp.float32)
                page = jnp.where(live, page, 0.0).astype(jnp.bfloat16)
                target[i, :, half * HD : (half + 1) * HD] = page


def finish_kernel(a0, a1, a2, a3, own_pages, got_pages, info_ref, att_out, page_out):
    _, _, pair, core = place()
    member = pair * 2 + core
    for k, part in enumerate((a0, a1, a2, a3)):
        att_out[:, pl.ds(pl.multiple_of((member ^ k) * 2 * HD, 2 * HD), 2 * HD)] = part[...]
    for i in range(page_out.shape[0]):
        here = info_ref[0, i] == pair

        @pl.when(here)
        def _():
            page_out[i] = own_pages[i]

        @pl.when(jnp.logical_not(here))
        def _():
            page_out[i] = got_pages[i]


def body(tokens, block_ids, lengths, page_table, qkv_weight, q_gain, k_gain):
    n_req, n_blk = lax.axis_size("req"), lax.axis_size("blk")
    n_out = n_blk // TEAM
    bf16 = jnp.bfloat16
    shape = jax.ShapeDtypeStruct
    blk = lax.axis_index("blk")
    pair = (blk // 2) % 2

    def in_team(array, k):
        return lax.ppermute(array, "blk", [(i, i ^ k) for i in range(n_blk)])

    def in_req(array, k):
        return lax.ppermute(array, "req", [(i, i ^ k) for i in range(n_req)])

    def across(array, k):
        return lax.ppermute(array, "blk", [(i, (i + TEAM * k) % n_blk) for i in range(n_blk)])

    w_rows = qkv_weight.shape[0]
    packed = pl.pallas_call(
        pack_kernel,
        out_shape=[shape((w_rows, HD), bf16)] * 3 + [shape((w_rows, 2 * HD), bf16)] * 3,
        in_specs=[VMEM],
        out_specs=[VMEM] * 6,
        compiler_params=params(),
        name="pack",
    )(qkv_weight)

    def gather_weight(parts, is_kv):
        width = HD if is_kv else 2 * HD
        got = [in_team(part, k + 1) for k, part in enumerate(parts)]
        team = pl.pallas_call(
            functools.partial(team_kernel, is_kv),
            out_shape=shape((TEAM * w_rows, width), bf16),
            in_specs=[VMEM] * TEAM,
            out_specs=VMEM,
            compiler_params=params(),
            name="team",
        )(qkv_weight, *got)
        pieces = {}
        for ko in range(n_out):
            piece = team if ko == 0 else across(team, ko)
            pieces[(0, ko)] = piece
            for dr in (1, 2):
                pieces[(dr, ko)] = in_req(piece, dr)
            first = 1 + ko % 2
            pieces[(3, ko)] = in_req(pieces[(first, ko)], 3 - first)
        return pieces

    kv_pieces = gather_weight(packed[:3], True)
    own = tokens[0]
    rows = own.shape[0]
    far = in_team(own, 2)
    team_tokens = [own, in_team(own, 1), far, in_team(far, 1)]
    q_pieces = gather_weight(packed[3:], False)

    blk_rows = rows // block_ids.shape[1]
    near_ids = in_team(block_ids, 1)
    is_first = blk % 2 == 0
    chip_ids = jnp.where(
        is_first, jnp.concatenate([block_ids, near_ids], 1), jnp.concatenate([near_ids, block_ids], 1)
    )
    team_ids = jnp.concatenate([chip_ids, in_team(chip_ids, 2)], 1)
    all_ids = jnp.concatenate([team_ids] + [across(team_ids, k) for k in range(1, n_out)], 1)[0]
    offsets = jnp.arange(blk_rows, dtype=jnp.int32)
    key_pos = (all_ids[:, None] * blk_rows + offsets[None, :]).reshape(1, -1)
    query_pos = (team_ids[0][:, None] * blk_rows + offsets[None, :]).reshape(-1, 1)
    half = HD // 2
    inverse = jnp.power(jnp.float32(ROPE_BASE), -2.0 * jnp.arange(half).astype(jnp.float32) / HD)
    angles = query_pos.astype(jnp.float32) * inverse[None, :]
    cosine, sine = jnp.cos(angles), jnp.sin(angles)

    def project(pieces, is_kv, gain):
        keys = sorted(pieces)
        width = HD if is_kv else 2 * HD
        depth = TEAM * w_rows
        return pl.pallas_call(
            functools.partial(project_kernel, n_out, keys, is_kv),
            out_shape=shape((TEAM * rows, width), bf16),
            in_specs=[ANY] * (TEAM + len(keys)) + [VMEM] * 3,
            out_specs=VMEM,
            scratch_shapes=[
                pltpu.VMEM((TEAM * rows, own.shape[1]), bf16),
                pltpu.VMEM((depth * len(keys), width), bf16),
                pltpu.SemaphoreType.DMA((TEAM,)),
                pltpu.SemaphoreType.DMA((len(keys),)),
            ],
            cost_estimate=pl.CostEstimate(
                flops=2 * TEAM * rows * own.shape[1] * width, bytes_accessed=6 << 20, transcendentals=0
            ),
            compiler_params=params(),
            name="project_kv" if is_kv else "project_q",
        )(*team_tokens, *[pieces[k] for k in keys], gain[None, :], cosine, sine)

    made = project(kv_pieces, True, k_gain)
    mine = [made] + [across(made, k) for k in range(1, n_out)]
    other = [in_team(part, 1) for part in mine]

    table = page_table[0].reshape(-1)
    per_head = page_table.shape[2]
    slot_count = page_table.shape[1] * per_head // n_blk
    wanted = jnp.concatenate(
        [b * slot_count + jnp.arange(slot_count, dtype=jnp.int32) for b in (blk, blk ^ 2)]
    )
    flat = jnp.sum(
        jnp.where(wanted[:, None] == table[None, :], jnp.arange(table.shape[0], dtype=jnp.int32)[None, :], 0), 1
    )
    block = flat % per_head
    where = jnp.sum(
        jnp.where(block[:, None] == all_ids[None, :], jnp.arange(per_head, dtype=jnp.int32)[None, :], 0), 1
    )
    info = jnp.stack([flat // per_head, where, lengths[0] - block * blk_rows])

    total = TEAM * rows * n_out
    store = [pltpu.VMEM((2, total, HD), bf16), pltpu.SemaphoreType.DMA((2, n_out))]
    page_shape = shape((slot_count, blk_rows, 2 * HD), bf16)
    own_pages, away_pages = pl.pallas_call(
        functools.partial(pages_kernel, n_out, blk_rows),
        out_shape=[page_shape, page_shape],
        in_specs=[ANY] * (2 * n_out) + [SMEM],
        out_specs=[VMEM, VMEM],
        scratch_shapes=store,
        cost_estimate=pl.CostEstimate(flops=0, bytes_accessed=4 << 20, transcendentals=0),
        compiler_params=params(),
        name="pages",
    )(*mine, *other, info)
    got_pages = in_team(away_pages, 2)

    queries = project(q_pieces, False, q_gain)

    def attend(parts):
        return pl.pallas_call(
            functools.partial(attend_kernel, n_out, parts),
            out_shape=[shape((rows, 2 * HD), bf16)] * len(parts),
            in_specs=[ANY] * (2 * n_out) + [VMEM] * 3 + [SMEM],
            out_specs=[VMEM] * len(parts),
            scratch_shapes=store,
            cost_estimate=pl.CostEstimate(
                flops=8 * HD * rows * total * len(parts), bytes_accessed=4 << 20, transcendentals=0
            ),
            compiler_params=params(),
            name="attend",
        )(*mine, *other, queries, query_pos, key_pos, lengths)

    to_far, to_diag = attend((2, 3))
    from_far, from_diag = in_team(to_far, 2), in_team(to_diag, 3)
    kept, to_near = attend((0, 1))
    from_near = in_team(to_near, 1)

    attended, pages = pl.pallas_call(
        finish_kernel,
        out_shape=[shape((rows, H * HD), bf16), page_shape],
        in_specs=[VMEM] * 6 + [SMEM],
        out_specs=[VMEM] * 2,
        compiler_params=params(),
        name="finish",
    )(kept, from_near, from_far, from_diag, own_pages, got_pages, info)
    return attended[None], pages[None]


def solution(mesh):
    in_specs = (
        P("req", "blk", None),
        P("req", "blk"),
        P("req"),
        P("req", None, None),
        P(("req", "blk"), None),
        P(),
        P(),
    )
    out_specs = (P("req", "blk", None), P("req", "blk", None, None))
    return jax.shard_map(body, mesh=mesh, in_specs=in_specs, out_specs=out_specs, check_vma=False)
```

```python
import functools

import jax
import jax.numpy as jnp
from jax import lax
from jax.experimental import pallas as pl
from jax.experimental.pallas import tpu as pltpu
from jax.sharding import PartitionSpec as P

H = 8
KVH = 2
HD = 256
TEAM = 4
ROPE_BASE = 1000000.0
NORM_EPS = 1e-06
MIB = 1024 * 1024

ANY = pl.BlockSpec(memory_space=pl.ANY)
VMEM = pl.BlockSpec(memory_space=pltpu.VMEM)
SMEM = pl.BlockSpec(memory_space=pltpu.SMEM)


def params(mib):
    return pltpu.CompilerParams(vmem_limit_bytes=mib * MIB)


def place():
    blk = lax.axis_index("blk")
    return lax.axis_index("req"), (blk // 2) % 2, blk % 2


def run(copies):
    for copy in copies:
        copy.start()
    for copy in copies:
        copy.wait()


def aligned(index, size):
    return pl.ds(pl.multiple_of(index * size, size), size)


def project_kernel(steps, n_pieces, is_kv, *refs):
    tokens, refs = refs[: len(steps)], refs[len(steps) :]
    weights, refs = refs[:n_pieces], refs[n_pieces:]
    gain_ref, cos_ref, sin_ref, out, x_all, w_all, x_sem, w_sem = refs
    req, pair, core = place()
    member = pair * 2 + core
    rows = tokens[0].shape[0]
    copies = []
    for i, k in enumerate(steps):
        slot = member ^ k if is_kv else i
        copies.append(pltpu.make_async_copy(tokens[i], x_all.at[aligned(slot, rows), :], x_sem.at[i]))
    depth = weights[0].shape[0]
    n_req = w_all.shape[0] // depth
    for i in range(n_pieces):
        part = slice(i // n_req * HD, (i // n_req + 1) * HD)
        copies.append(
            pltpu.make_async_copy(
                weights[i], w_all.at[aligned(req ^ (i % n_req), depth), part], w_sem.at[i]
            )
        )
    run(copies)
    half = HD // 2
    gain = gain_ref[...]
    if is_kv:
        cosine, sine = cos_ref[...], sin_ref[...]
        is_key = core == 0
        cosine = jnp.where(is_key, cosine, 1.0)
        sine = jnp.where(is_key, sine, 0.0)
        gain = jnp.where(is_key, gain, 1.0)
    else:
        cosine = jnp.concatenate([cos_ref[aligned(member ^ k, rows), :] for k in steps], 0)
        sine = jnp.concatenate([sin_ref[aligned(member ^ k, rows), :] for k in steps], 0)
    product = jnp.dot(x_all[...], w_all[...], preferred_element_type=jnp.float32)
    for h in range(out.shape[1] // HD):
        head = product[:, h * HD : (h + 1) * HD]
        mean = jnp.mean(head * head, axis=-1, keepdims=True)
        head = head * lax.rsqrt(mean + NORM_EPS) * gain
        front, second = head[:, :half], head[:, half:]
        out[:, h * HD : h * HD + half] = (front * cosine - second * sine).astype(jnp.bfloat16)
        out[:, h * HD + half : (h + 1) * HD] = (second * cosine + front * sine).astype(jnp.bfloat16)


def load_kv(n_out, blk_rows, mine, other, ids_ref, store, sems, core):
    per_piece = mine[0].shape[0] // blk_rows
    copies = []
    for k in range(n_out):
        for j in range(per_piece):
            n = k * per_piece + j
            there = aligned(ids_ref[n], blk_rows)
            here = pl.ds(j * blk_rows, blk_rows)
            copies.append(pltpu.make_async_copy(mine[k].at[here, :], store.at[core, there, :], sems.at[0, n]))
            copies.append(pltpu.make_async_copy(other[k].at[here, :], store.at[1 - core, there, :], sems.at[1, n]))
    run(copies)


def attend_kernel(n_out, blk_rows, step, *refs):
    mine, other = refs[:n_out], refs[n_out : 2 * n_out]
    q_ref, near_ref, ids_ref, length_ref, out, store, sems = refs[2 * n_out :]
    _, pair, core = place()
    load_kv(n_out, blk_rows, mine, other, ids_ref, store, sems, core)
    length = length_ref[0]
    rows = out.shape[0]
    member = (pair * 2 + core) ^ step
    total = store.shape[1]
    quarter = total // 4
    heads = 2 * (out.shape[1] // (2 * HD))
    first = step // 2 * rows
    for j in range(rows // blk_rows):
        block = ids_ref[member * (rows // blk_rows) + j]
        here = slice(first + j * blk_rows, first + (j + 1) * blk_rows)
        there = slice(j * blk_rows, (j + 1) * blk_rows)
        for variant in range(4):
            seen = (variant + 1) * quarter

            @pl.when((block * blk_rows) // quarter == variant)
            def _():
                queries = jnp.concatenate(
                    [ref[here, h * HD : (h + 1) * HD] for ref in (q_ref, near_ref) for h in range(heads // 2)], 0
                )
                shape = (heads * blk_rows, 1)
                query_pos = block * blk_rows + lax.rem(lax.broadcasted_iota(jnp.int32, shape, 0), blk_rows)
                limit = jnp.minimum(query_pos, length - 1)
                key_pos = lax.broadcasted_iota(jnp.int32, (1, seen), 1)
                scores = lax.dot_general(
                    queries,
                    store[0, :seen, :],
                    (((1,), (1,)), ((), ())),
                    preferred_element_type=jnp.float32,
                )
                scores = jnp.where(key_pos <= limit, scores, jnp.finfo(jnp.float32).min)
                weights = jnp.exp(scores - jnp.max(scores, axis=-1, keepdims=True))
                row_sum = jnp.sum(weights, axis=-1, keepdims=True)
                summed = jnp.dot(
                    weights.astype(jnp.bfloat16), store[1, :seen, :], preferred_element_type=jnp.float32
                )
                result = jnp.where(query_pos < length, summed / row_sum, 0.0).astype(jnp.bfloat16)
                for n in range(heads):
                    side = core if n < heads // 2 else 1 - core
                    column = side * (heads // 2) + n % (heads // 2)
                    out[there, aligned(column, HD)] = result[n * blk_rows : (n + 1) * blk_rows]


def pages_kernel(n_out, blk_rows, *refs):
    mine, other = refs[:n_out], refs[n_out : 2 * n_out]
    ids_ref, info_ref, own, away, store, sems = refs[2 * n_out :]
    _, _, core = place()
    load_kv(n_out, blk_rows, mine, other, ids_ref, store, sems, core)
    slots = own.shape[0]
    row = lax.broadcasted_iota(jnp.int32, (blk_rows, HD), 0)
    for target, base in ((own, 0), (away, slots)):
        for i in range(slots):
            here = aligned(info_ref[1, base + i], blk_rows)
            live = row < info_ref[2, base + i]
            for half in range(2):
                page = store[half, here, :]
                target[i, :, half * HD : (half + 1) * HD] = jnp.where(live, page, jnp.zeros_like(page))


def finish_kernel(kept, from_far, own_pages, got_pages, info_ref, att_out, page_out, sems):
    _, pair, _ = place()
    width = kept.shape[1]
    copies = [
        pltpu.make_async_copy(kept, att_out.at[:, aligned(pair, width)], sems.at[0]),
        pltpu.make_async_copy(from_far, att_out.at[:, aligned(1 - pair, width)], sems.at[1]),
    ]
    for copy in copies:
        copy.start()
    for i in range(page_out.shape[0]):
        here = info_ref[0, i] == pair
        ours = pltpu.make_async_copy(own_pages.at[i], page_out.at[i], sems.at[2 + i])
        theirs = pltpu.make_async_copy(got_pages.at[i], page_out.at[i], sems.at[2 + i])
        copies.append(ours)

        @pl.when(here)
        def _():
            ours.start()

        @pl.when(jnp.logical_not(here))
        def _():
            theirs.start()

    for copy in copies:
        copy.wait()


def body(tokens, block_ids, lengths, page_table, qkv_weight, q_gain, k_gain):
    n_req, n_blk = lax.axis_size("req"), lax.axis_size("blk")
    n_out = n_blk // TEAM
    bf16 = jnp.bfloat16
    shape = jax.ShapeDtypeStruct
    blk = lax.axis_index("blk")
    member = blk % TEAM

    def in_team(array, k):
        return lax.ppermute(array, "blk", [(i, i ^ k) for i in range(n_blk)])

    def in_req(array, k):
        return lax.ppermute(array, "req", [(i, i ^ k) for i in range(n_req)])

    def across(array, k):
        return lax.ppermute(array, "blk", [(i, (i + TEAM * k) % n_blk) for i in range(n_blk)])

    blk_rows = tokens.shape[1] // block_ids.shape[1]

    def join(array, bit):
        got = in_team(array, bit)
        low = member & bit == 0
        return jnp.where(low, jnp.concatenate([array, got], 1), jnp.concatenate([got, array], 1))

    team_ids = join(join(block_ids, 1), 2)
    all_ids = jnp.concatenate([team_ids] + [across(team_ids, k) for k in range(1, n_out)], 1)[0]

    w_rows = qkv_weight.shape[0]
    q_part = qkv_weight[:, : H * HD].reshape(w_rows, 2, 2, 2, HD).transpose(3, 1, 2, 0, 4)
    kv_part = qkv_weight[:, H * HD :].reshape(w_rows, 2, 2, HD).transpose(2, 1, 0, 3)

    def to_columns(part):
        part = jnp.broadcast_to(part[None], (n_out,) + part.shape).reshape(n_blk * w_rows, HD)
        return lax.all_to_all(part, "blk", split_axis=0, concat_axis=0, tiled=True)

    def to_prompts(piece, share):
        rows = piece.shape[0]
        cut = rows * share // 4
        one, two = in_req(piece, 1), in_req(piece, 2)
        if cut == rows:
            return [piece, one, two, in_req(one, 2)]
        if cut == 0:
            return [piece, one, two, in_req(two, 1)]
        return [piece, one, two, jnp.concatenate([in_req(one[:cut], 2), in_req(two[cut:], 1)], 0)]

    kv_pieces = to_prompts(to_columns(kv_part), 4)
    q_pieces = to_prompts(to_columns(q_part[0]), 0) + to_prompts(to_columns(q_part[1]), 2)

    own = tokens[0]
    rows = own.shape[0]
    own, all_ids = lax.optimization_barrier((own, all_ids))
    far = in_team(own, 2)
    team_tokens = [own, in_team(own, 1), far, in_team(far, 1)]

    offsets = jnp.arange(blk_rows, dtype=jnp.int32)
    positions = (team_ids[0][:, None] * blk_rows + offsets[None, :]).reshape(-1, 1)
    inverse = jnp.power(jnp.float32(ROPE_BASE), -2.0 * jnp.arange(HD // 2).astype(jnp.float32) / HD)
    angles = positions.astype(jnp.float32) * inverse[None, :]
    cosine, sine = jnp.cos(angles), jnp.sin(angles)

    def project(steps, pieces, is_kv, gain):
        width = len(pieces) // n_req * HD
        depth = own.shape[1]
        return pl.pallas_call(
            functools.partial(project_kernel, steps, len(pieces), is_kv),
            out_shape=shape((len(steps) * rows, width), bf16),
            in_specs=[ANY] * (len(steps) + len(pieces)) + [VMEM] * 3,
            out_specs=VMEM,
            scratch_shapes=[
                pltpu.VMEM((len(steps) * rows, depth), bf16),
                pltpu.VMEM((depth, width), bf16),
                pltpu.SemaphoreType.DMA((len(steps),)),
                pltpu.SemaphoreType.DMA((len(pieces),)),
            ],
            cost_estimate=pl.CostEstimate(
                flops=2 * len(steps) * rows * depth * width, bytes_accessed=6 * MIB, transcendentals=0
            ),
            compiler_params=params(12),
            name="project_kv" if is_kv else "project_q",
        )(*[team_tokens[k] for k in steps], *pieces, gain[None, :], cosine, sine)

    made = project((0, 1, 2, 3), kv_pieces, True, k_gain)
    mine = [made] + [across(made, k) for k in range(1, n_out)]
    other = [in_team(part, 1) for part in mine]

    from_near = in_team(project((1, 3), q_pieces, False, q_gain), 1)
    queries = project((0, 2), q_pieces, False, q_gain)

    table = page_table[0].reshape(-1)
    per_head = page_table.shape[2]
    slot_count = page_table.shape[1] * per_head // n_blk
    wanted = jnp.concatenate(
        [b * slot_count + jnp.arange(slot_count, dtype=jnp.int32) for b in (blk, blk ^ 2)]
    )
    flat = jnp.sum(
        jnp.where(wanted[:, None] == table[None, :], jnp.arange(table.shape[0], dtype=jnp.int32)[None, :], 0), 1
    )
    block = flat % per_head
    info = jnp.stack([flat // per_head, block, lengths[0] - block * blk_rows])

    total = TEAM * rows * n_out
    store = [pltpu.VMEM((2, total, HD), bf16), pltpu.SemaphoreType.DMA((2, total // blk_rows))]
    store_mib = -(-2 * total * HD * 2 // MIB)
    page_shape = shape((slot_count, blk_rows, 2 * HD), bf16)
    own_pages, away_pages = pl.pallas_call(
        functools.partial(pages_kernel, n_out, blk_rows),
        out_shape=[page_shape, page_shape],
        in_specs=[ANY] * (2 * n_out) + [SMEM] * 2,
        out_specs=[VMEM, VMEM],
        scratch_shapes=store,
        cost_estimate=pl.CostEstimate(flops=0, bytes_accessed=4 * MIB, transcendentals=0),
        compiler_params=params(store_mib + 4),
        name="pages",
    )(*mine, *other, all_ids, info)
    got_pages = in_team(away_pages, 2)

    def attend(step):
        return pl.pallas_call(
            functools.partial(attend_kernel, n_out, blk_rows, step),
            out_shape=shape((rows, H // 2 * HD), bf16),
            in_specs=[ANY] * (2 * n_out) + [VMEM] * 2 + [SMEM] * 2,
            out_specs=VMEM,
            scratch_shapes=store,
            cost_estimate=pl.CostEstimate(
                flops=2 * H * HD * rows * total, bytes_accessed=4 * MIB, transcendentals=0
            ),
            compiler_params=params(store_mib + 4 + 4 * total // 1024),
            name="attend",
        )(*mine, *other, queries, from_near, all_ids, lengths)

    from_far = in_team(attend(2), 2)
    kept = attend(0)

    attended, pages = pl.pallas_call(
        finish_kernel,
        out_shape=[shape((rows, H * HD), bf16), page_shape],
        in_specs=[ANY] * 4 + [SMEM],
        out_specs=[ANY] * 2,
        scratch_shapes=[pltpu.SemaphoreType.DMA((2 + slot_count,))],
        compiler_params=params(1),
        name="finish",
    )(kept, from_far, own_pages, got_pages, info)
    return attended[None], pages[None]


def solution(mesh):
    in_specs = (
        P("req", "blk", None),
        P("req", "blk"),
        P("req"),
        P("req", None, None),
        P(("req", "blk"), None),
        P(),
        P(),
    )
    out_specs = (P("req", "blk", None), P("req", "blk", None, None))
    return jax.shard_map(body, mesh=mesh, in_specs=in_specs, out_specs=out_specs, check_vma=False)
```

```python
import functools

import jax
import jax.numpy as jnp
from jax import lax
from jax.experimental import pallas as pl
from jax.experimental.pallas import tpu as pltpu
from jax.sharding import PartitionSpec as P

H = 8
KVH = 2
HD = 256
TEAM = 4
ROPE_BASE = 1000000.0
NORM_EPS = 1e-06
MIB = 1024 * 1024

ANY = pl.BlockSpec(memory_space=pl.ANY)
VMEM = pl.BlockSpec(memory_space=pltpu.VMEM)
SMEM = pl.BlockSpec(memory_space=pltpu.SMEM)


def params(mib):
    return pltpu.CompilerParams(vmem_limit_bytes=mib * MIB)


def place():
    blk = lax.axis_index("blk")
    return lax.axis_index("req"), (blk // 2) % 2, blk % 2


def run(copies):
    for copy in copies:
        copy.start()
    for copy in copies:
        copy.wait()


def aligned(index, size):
    return pl.ds(pl.multiple_of(index * size, size), size)


def q_start(pair, core):
    return pl.multiple_of((pair * 2 + core) * 2 * HD, 2 * HD)


def kv_start(pair, core):
    return pl.multiple_of(H * HD + core * KVH * HD + pair * HD, HD)


def pack_kernel(w_ref, *refs):
    outs, sems = refs[:-1], refs[-1]
    _, pair, core = place()
    copies = []
    for k in range(1, TEAM):
        to_pair, to_core = pair ^ (k // 2), core ^ (k % 2)
        kv_part = w_ref.at[:, pl.ds(kv_start(to_pair, to_core), HD)]
        q_part = w_ref.at[:, pl.ds(q_start(to_pair, to_core), 2 * HD)]
        copies.append(pltpu.make_async_copy(kv_part, outs[k - 1], sems.at[k - 1]))
        copies.append(pltpu.make_async_copy(q_part, outs[TEAM - 2 + k], sems.at[TEAM - 2 + k]))
    run(copies)


def team_kernel(is_kv, w_ref, *refs):
    _, pair, core = place()
    got, out, sems = refs[:-2], refs[-2], refs[-1]
    rows, width = w_ref.shape[0], out.shape[1]
    start = kv_start(pair, core) if is_kv else q_start(pair, core)
    member = pair * 2 + core
    copies = [pltpu.make_async_copy(w_ref.at[:, pl.ds(start, width)], out.at[aligned(member, rows), :], sems.at[0])]
    for k in range(1, TEAM):
        copies.append(pltpu.make_async_copy(got[k - 1], out.at[aligned(member ^ k, rows), :], sems.at[k]))
    run(copies)


def project_kernel(steps, is_kv, *refs):
    tokens, refs = refs[: len(steps)], refs[len(steps) :]
    w_all, gain_ref, cos_ref, sin_ref, out, x_all, x_sem = refs
    _, pair, core = place()
    member = pair * 2 + core
    rows = tokens[0].shape[0]
    copies = []
    for i, k in enumerate(steps):
        slot = member ^ k if is_kv else i
        copies.append(pltpu.make_async_copy(tokens[i], x_all.at[aligned(slot, rows), :], x_sem.at[i]))
    run(copies)
    half = HD // 2
    gain = gain_ref[...]
    if is_kv:
        cosine, sine = cos_ref[...], sin_ref[...]
        is_key = core == 0
        cosine = jnp.where(is_key, cosine, 1.0)
        sine = jnp.where(is_key, sine, 0.0)
        gain = jnp.where(is_key, gain, 1.0)
    else:
        cosine = jnp.concatenate([cos_ref[aligned(member ^ k, rows), :] for k in steps], 0)
        sine = jnp.concatenate([sin_ref[aligned(member ^ k, rows), :] for k in steps], 0)
    product = jnp.dot(x_all[...], w_all[...], preferred_element_type=jnp.float32)
    for h in range(out.shape[1] // HD):
        head = product[:, h * HD : (h + 1) * HD]
        mean = jnp.mean(head * head, axis=-1, keepdims=True)
        head = head * lax.rsqrt(mean + NORM_EPS) * gain
        front, second = head[:, :half], head[:, half:]
        out[:, h * HD : h * HD + half] = (front * cosine - second * sine).astype(jnp.bfloat16)
        out[:, h * HD + half : (h + 1) * HD] = (second * cosine + front * sine).astype(jnp.bfloat16)


def load_kv(n_out, blk_rows, mine, other, ids_ref, store, sems, core):
    per_piece = mine[0].shape[0] // blk_rows
    copies = []
    for k in range(n_out):
        for j in range(per_piece):
            n = k * per_piece + j
            there = aligned(ids_ref[n], blk_rows)
            here = pl.ds(j * blk_rows, blk_rows)
            copies.append(pltpu.make_async_copy(mine[k].at[here, :], store.at[core, there, :], sems.at[0, n]))
            copies.append(pltpu.make_async_copy(other[k].at[here, :], store.at[1 - core, there, :], sems.at[1, n]))
    run(copies)


def attend_kernel(blk_rows, step, store, q_ref, near_ref, ids_ref, length_ref, out):
    _, pair, core = place()
    length = length_ref[0]
    rows = out.shape[0]
    member = (pair * 2 + core) ^ step
    total = store.shape[1]
    quarter = total // 4
    heads = 2 * (out.shape[1] // (2 * HD))
    first = step // 2 * rows
    for j in range(rows // blk_rows):
        block = ids_ref[member * (rows // blk_rows) + j]
        here = slice(first + j * blk_rows, first + (j + 1) * blk_rows)
        there = slice(j * blk_rows, (j + 1) * blk_rows)
        for variant in range(4):
            seen = (variant + 1) * quarter

            @pl.when((block * blk_rows) // quarter == variant)
            def _():
                queries = jnp.concatenate(
                    [ref[here, h * HD : (h + 1) * HD] for ref in (q_ref, near_ref) for h in range(heads // 2)], 0
                )
                shape = (heads * blk_rows, 1)
                query_pos = block * blk_rows + lax.rem(lax.broadcasted_iota(jnp.int32, shape, 0), blk_rows)
                limit = jnp.minimum(query_pos, length - 1)
                key_pos = lax.broadcasted_iota(jnp.int32, (1, seen), 1)
                scores = lax.dot_general(
                    queries,
                    store[0, :seen, :],
                    (((1,), (1,)), ((), ())),
                    preferred_element_type=jnp.float32,
                )
                scores = jnp.where(key_pos <= limit, scores, jnp.finfo(jnp.float32).min)
                weights = jnp.exp(scores - jnp.max(scores, axis=-1, keepdims=True))
                row_sum = jnp.sum(weights, axis=-1, keepdims=True)
                summed = jnp.dot(
                    weights.astype(jnp.bfloat16), store[1, :seen, :], preferred_element_type=jnp.float32
                )
                result = jnp.where(query_pos < length, summed / row_sum, 0.0).astype(jnp.bfloat16)
                for n in range(heads):
                    side = core if n < heads // 2 else 1 - core
                    column = side * (heads // 2) + n % (heads // 2)
                    out[there, aligned(column, HD)] = result[n * blk_rows : (n + 1) * blk_rows]


def pages_kernel(n_out, blk_rows, *refs):
    mine, other = refs[:n_out], refs[n_out : 2 * n_out]
    ids_ref, info_ref, own, away, store, sems = refs[2 * n_out :]
    _, _, core = place()
    load_kv(n_out, blk_rows, mine, other, ids_ref, store, sems, core)
    slots = own.shape[0]
    row = lax.broadcasted_iota(jnp.int32, (blk_rows, HD), 0)
    for target, base in ((own, 0), (away, slots)):
        for i in range(slots):
            here = aligned(info_ref[1, base + i], blk_rows)
            live = row < info_ref[2, base + i]
            for half in range(2):
                page = store[half, here, :]
                target[i, :, half * HD : (half + 1) * HD] = jnp.where(live, page, jnp.zeros_like(page))


def finish_kernel(kept, from_far, own_pages, got_pages, info_ref, att_out, page_out, sems):
    _, pair, _ = place()
    width = kept.shape[1]
    copies = [
        pltpu.make_async_copy(kept, att_out.at[:, aligned(pair, width)], sems.at[0]),
        pltpu.make_async_copy(from_far, att_out.at[:, aligned(1 - pair, width)], sems.at[1]),
    ]
    for copy in copies:
        copy.start()
    for i in range(page_out.shape[0]):
        here = info_ref[0, i] == pair
        ours = pltpu.make_async_copy(own_pages.at[i], page_out.at[i], sems.at[2 + i])
        theirs = pltpu.make_async_copy(got_pages.at[i], page_out.at[i], sems.at[2 + i])
        copies.append(ours)

        @pl.when(here)
        def _():
            ours.start()

        @pl.when(jnp.logical_not(here))
        def _():
            theirs.start()

    for copy in copies:
        copy.wait()


def body(tokens, block_ids, lengths, page_table, qkv_weight, q_gain, k_gain):
    n_req, n_blk = lax.axis_size("req"), lax.axis_size("blk")
    n_out = n_blk // TEAM
    bf16 = jnp.bfloat16
    shape = jax.ShapeDtypeStruct
    blk = lax.axis_index("blk")
    member = blk % TEAM

    def in_team(array, k):
        return lax.ppermute(array, "blk", [(i, i ^ k) for i in range(n_blk)])

    def in_req(array, k):
        return lax.ppermute(array, "req", [(i, i ^ k) for i in range(n_req)])

    def across(array, k):
        return lax.ppermute(array, "blk", [(i, (i + TEAM * k) % n_blk) for i in range(n_blk)])

    blk_rows = tokens.shape[1] // block_ids.shape[1]

    def join(array, bit):
        got = in_team(array, bit)
        low = member & bit == 0
        return jnp.where(low, jnp.concatenate([array, got], 1), jnp.concatenate([got, array], 1))

    team_ids = join(join(block_ids, 1), 2)
    all_ids = jnp.concatenate([team_ids] + [across(team_ids, k) for k in range(1, n_out)], 1)[0]

    w_rows = qkv_weight.shape[0]
    packed = pl.pallas_call(
        pack_kernel,
        out_shape=[shape((w_rows, HD), bf16)] * 3 + [shape((w_rows, 2 * HD), bf16)] * 3,
        in_specs=[ANY],
        out_specs=[ANY] * 6,
        scratch_shapes=[pltpu.SemaphoreType.DMA((6,))],
        compiler_params=params(1),
        name="pack",
    )(qkv_weight)

    def gather_weight(parts, is_kv):
        got = [in_team(part, k + 1) for k, part in enumerate(parts)]
        team = pl.pallas_call(
            functools.partial(team_kernel, is_kv),
            out_shape=shape((TEAM * w_rows, parts[0].shape[1]), bf16),
            in_specs=[ANY] * TEAM,
            out_specs=ANY,
            scratch_shapes=[pltpu.SemaphoreType.DMA((TEAM,))],
            compiler_params=params(1),
            name="team",
        )(qkv_weight, *got)
        same = [[r * n_blk + o * TEAM + m for r in range(n_req) for o in range(n_out)] for m in range(TEAM)]
        return lax.all_gather(team, ("req", "blk"), axis_index_groups=same, axis=0, tiled=True)

    kv_weight = gather_weight(packed[:3], True)
    q_weight = gather_weight(packed[3:], False)

    own = tokens[0]
    rows = own.shape[0]
    own, all_ids = lax.optimization_barrier((own, all_ids))
    far = in_team(own, 2)
    team_tokens = [own, in_team(own, 1), far, in_team(far, 1)]

    offsets = jnp.arange(blk_rows, dtype=jnp.int32)
    positions = (team_ids[0][:, None] * blk_rows + offsets[None, :]).reshape(-1, 1)
    inverse = jnp.power(jnp.float32(ROPE_BASE), -2.0 * jnp.arange(HD // 2).astype(jnp.float32) / HD)
    angles = positions.astype(jnp.float32) * inverse[None, :]
    cosine, sine = jnp.cos(angles), jnp.sin(angles)

    def project(steps, weight, is_kv, gain):
        depth, width = weight.shape
        return pl.pallas_call(
            functools.partial(project_kernel, steps, is_kv),
            out_shape=shape((len(steps) * rows, width), bf16),
            in_specs=[ANY] * len(steps) + [VMEM] * 4,
            out_specs=VMEM,
            scratch_shapes=[
                pltpu.VMEM((len(steps) * rows, depth), bf16),
                pltpu.SemaphoreType.DMA((len(steps),)),
            ],
            cost_estimate=pl.CostEstimate(
                flops=2 * len(steps) * rows * depth * width, bytes_accessed=6 * MIB, transcendentals=0
            ),
            compiler_params=params(12),
            name="project_kv" if is_kv else "project_q",
        )(*[team_tokens[k] for k in steps], weight, gain[None, :], cosine, sine)

    made = project((0, 1, 2, 3), kv_weight, True, k_gain)
    made, all_ids = lax.optimization_barrier((made, all_ids))
    mine = [made] + [across(made, k) for k in range(1, n_out)]
    other = [in_team(part, 1) for part in mine]

    from_near = in_team(project((1, 3), q_weight, False, q_gain), 1)
    queries = project((0, 2), q_weight, False, q_gain)

    table = page_table[0].reshape(-1)
    per_head = page_table.shape[2]
    slot_count = page_table.shape[1] * per_head // n_blk
    wanted = jnp.concatenate(
        [b * slot_count + jnp.arange(slot_count, dtype=jnp.int32) for b in (blk, blk ^ 2)]
    )
    flat = jnp.sum(
        jnp.where(wanted[:, None] == table[None, :], jnp.arange(table.shape[0], dtype=jnp.int32)[None, :], 0), 1
    )
    block = flat % per_head
    info = jnp.stack([flat // per_head, block, lengths[0] - block * blk_rows])

    total = TEAM * rows * n_out
    store_mib = -(-2 * total * HD * 2 // MIB)
    page_shape = shape((slot_count, blk_rows, 2 * HD), bf16)
    own_pages, away_pages, store = pl.pallas_call(
        functools.partial(pages_kernel, n_out, blk_rows),
        out_shape=[page_shape, page_shape, shape((2, total, HD), bf16)],
        in_specs=[ANY] * (2 * n_out) + [SMEM] * 2,
        out_specs=[VMEM] * 3,
        scratch_shapes=[pltpu.SemaphoreType.DMA((2, total // blk_rows))],
        cost_estimate=pl.CostEstimate(flops=0, bytes_accessed=4 * MIB, transcendentals=0),
        compiler_params=params(store_mib + 4),
        name="pages",
    )(*mine, *other, all_ids, info)
    got_pages = in_team(away_pages, 2)

    def attend(step):
        return pl.pallas_call(
            functools.partial(attend_kernel, blk_rows, step),
            out_shape=shape((rows, H // 2 * HD), bf16),
            in_specs=[VMEM] * 3 + [SMEM] * 2,
            out_specs=VMEM,
            cost_estimate=pl.CostEstimate(
                flops=2 * H * HD * rows * total, bytes_accessed=4 * MIB, transcendentals=0
            ),
            compiler_params=params(store_mib + 4 + 4 * total // 1024),
            name="attend",
        )(store, queries, from_near, all_ids, lengths)

    from_far = in_team(attend(2), 2)
    kept = attend(0)

    attended, pages = pl.pallas_call(
        finish_kernel,
        out_shape=[shape((rows, H * HD), bf16), page_shape],
        in_specs=[ANY] * 4 + [SMEM],
        out_specs=[ANY] * 2,
        scratch_shapes=[pltpu.SemaphoreType.DMA((2 + slot_count,))],
        compiler_params=params(1),
        name="finish",
    )(kept, from_far, own_pages, got_pages, info)
    return attended[None], pages[None]


def solution(mesh):
    in_specs = (
        P("req", "blk", None),
        P("req", "blk"),
        P("req"),
        P("req", None, None),
        P(("req", "blk"), None),
        P(),
        P(),
    )
    out_specs = (P("req", "blk", None), P("req", "blk", None, None))
    return jax.shard_map(body, mesh=mesh, in_specs=in_specs, out_specs=out_specs, check_vma=False)
```

```python
import functools

import jax
import jax.numpy as jnp
from jax import lax
from jax.experimental import pallas as pl
from jax.experimental.pallas import tpu as pltpu
from jax.sharding import PartitionSpec as P

H = 8
KVH = 2
HD = 256
TEAM = 4
ID_ROWS = 16
ROPE_BASE = 1000000.0
NORM_EPS = 1e-06
MIB = 1024 * 1024

ANY = pl.BlockSpec(memory_space=pl.ANY)
VMEM = pl.BlockSpec(memory_space=pltpu.VMEM)
SMEM = pl.BlockSpec(memory_space=pltpu.SMEM)


def params(mib):
    return pltpu.CompilerParams(vmem_limit_bytes=mib * MIB)


def place():
    blk = lax.axis_index("blk")
    return lax.axis_index("req"), (blk // 2) % 2, blk % 2


def run(copies):
    for copy in copies:
        copy.start()
    for copy in copies:
        copy.wait()


def aligned(index, size):
    return pl.ds(pl.multiple_of(index * size, size), size)


def q_start(pair, core):
    return pl.multiple_of((pair * 2 + core) * 2 * HD, 2 * HD)


def kv_start(pair, core):
    return pl.multiple_of(H * HD + core * KVH * HD + pair * HD, HD)


def pack_kernel(w_ref, ids_ref, *outs):
    _, pair, core = place()
    rows = w_ref.shape[0]
    for k in range(TEAM):
        to_pair, to_core = pair ^ (k // 2), core ^ (k % 2)
        outs[k][:rows, :] = w_ref[:, pl.ds(kv_start(to_pair, to_core), HD)]
        outs[k][rows:, :] = ids_ref[...]
        outs[TEAM + k][...] = w_ref[:, pl.ds(q_start(to_pair, to_core), 2 * HD)]


def team_kernel(rows, *refs):
    _, pair, core = place()
    parts, outs = refs[:TEAM], refs[TEAM:]
    member = pair * 2 + core
    for n, out in enumerate(outs):
        cols = slice(n * HD, (n + 1) * HD)
        for k in range(TEAM):
            out[aligned(member ^ k, rows), :] = parts[k][:rows, cols]
        if parts[0].shape[0] > rows:
            below = [part[rows:, cols].astype(jnp.float32) for part in parts]
            out[TEAM * rows :, :] = sum(below[1:], below[0]).astype(out.dtype)


def stack_kernel(*refs):
    _, pair, core = place()
    tokens, out, sems = refs[:TEAM], refs[TEAM], refs[TEAM + 1]
    rows = tokens[0].shape[0]
    member = pair * 2 + core
    run([
        pltpu.make_async_copy(tokens[k], out.at[aligned(member ^ k, rows), :], sems.at[k]) for k in range(TEAM)
    ])


def project_kernel(steps, n_out, depth, is_kv, x_ref, *refs):
    gain_ref, cos_ref, sin_ref, out, w_all, sems = refs[-6:]
    weights = refs[:-6]
    req = lax.axis_index("req")
    outer = lax.axis_index("blk") // TEAM
    _, pair, core = place()
    member = pair * 2 + core
    rows = x_ref.shape[0] // TEAM
    copies = []
    per_chunk = 2 * (w_all.shape[0] // (depth * n_out))
    for at, piece in enumerate(weights):
        i = at % per_chunk
        cols = slice(at // per_chunk * HD, (at // per_chunk + 1) * HD)
        from_req = req ^ (i // 2)
        tall = piece.shape[0] // (n_out - 1 if i % 2 else 1)
        for n in range(n_out - 1 if i % 2 else 1):
            from_outer = lax.rem(outer + n_out - n - i % 2, n_out)
            copies.append(
                pltpu.make_async_copy(
                    piece.at[pl.ds(n * tall, depth), :],
                    w_all.at[aligned(from_req * n_out + from_outer, depth), cols],
                    sems.at[len(copies)],
                )
            )
    run(copies)
    half = HD // 2
    gain = gain_ref[...]
    if is_kv:
        x, cosine, sine = x_ref[...], cos_ref[...], sin_ref[...]
        is_key = core == 0
        cosine = jnp.where(is_key, cosine, 1.0)
        sine = jnp.where(is_key, sine, 0.0)
        gain = jnp.where(is_key, gain, 1.0)
    else:
        x, cosine, sine = (
            jnp.concatenate([ref[aligned(member ^ k, rows), :] for k in steps], 0)
            for ref in (x_ref, cos_ref, sin_ref)
        )
    product = jnp.dot(x, w_all[...], preferred_element_type=jnp.float32)
    for h in range(out.shape[1] // HD):
        head = product[:, h * HD : (h + 1) * HD]
        mean = jnp.mean(head * head, axis=-1, keepdims=True)
        head = head * lax.rsqrt(mean + NORM_EPS) * gain
        front, second = head[:, :half], head[:, half:]
        out[:, h * HD : h * HD + half] = (front * cosine - second * sine).astype(jnp.bfloat16)
        out[:, h * HD + half : (h + 1) * HD] = (second * cosine + front * sine).astype(jnp.bfloat16)


def load_kv(n_out, blk_rows, mine, other, ids_ref, store, sems, core):
    per_piece = mine[0].shape[0] // blk_rows
    copies = []
    for k in range(n_out):
        for j in range(per_piece):
            n = k * per_piece + j
            there = aligned(ids_ref[n], blk_rows)
            here = pl.ds(j * blk_rows, blk_rows)
            copies.append(pltpu.make_async_copy(mine[k].at[here, :], store.at[core, there, :], sems.at[0, n]))
            copies.append(pltpu.make_async_copy(other[k].at[here, :], store.at[1 - core, there, :], sems.at[1, n]))
    run(copies)


def attend_kernel(blk_rows, step, store, q_ref, near_ref, ids_ref, length_ref, out):
    _, pair, core = place()
    length = length_ref[0]
    rows = out.shape[0]
    member = (pair * 2 + core) ^ step
    total = store.shape[1]
    quarter = total // 4
    heads = 2 * (out.shape[1] // (2 * HD))
    first = step // 2 * rows
    for j in range(rows // blk_rows):
        block = ids_ref[member * (rows // blk_rows) + j]
        here = slice(first + j * blk_rows, first + (j + 1) * blk_rows)
        there = slice(j * blk_rows, (j + 1) * blk_rows)
        for variant in range(4):
            seen = (variant + 1) * quarter

            @pl.when((block * blk_rows) // quarter == variant)
            def _():
                queries = jnp.concatenate(
                    [ref[here, h * HD : (h + 1) * HD] for ref in (q_ref, near_ref) for h in range(heads // 2)], 0
                )
                shape = (heads * blk_rows, 1)
                query_pos = block * blk_rows + lax.rem(lax.broadcasted_iota(jnp.int32, shape, 0), blk_rows)
                limit = jnp.minimum(query_pos, length - 1)
                key_pos = lax.broadcasted_iota(jnp.int32, (1, seen), 1)
                scores = lax.dot_general(
                    queries,
                    store[0, :seen, :],
                    (((1,), (1,)), ((), ())),
                    preferred_element_type=jnp.float32,
                )
                scores = jnp.where(key_pos <= limit, scores, jnp.finfo(jnp.float32).min)
                weights = jnp.exp(scores - jnp.max(scores, axis=-1, keepdims=True))
                row_sum = jnp.sum(weights, axis=-1, keepdims=True)
                summed = jnp.dot(
                    weights.astype(jnp.bfloat16), store[1, :seen, :], preferred_element_type=jnp.float32
                )
                result = jnp.where(query_pos < length, summed / row_sum, 0.0).astype(jnp.bfloat16)
                for n in range(heads):
                    side = core if n < heads // 2 else 1 - core
                    column = side * (heads // 2) + n % (heads // 2)
                    out[there, aligned(column, HD)] = result[n * blk_rows : (n + 1) * blk_rows]


def pages_kernel(n_out, blk_rows, *refs):
    mine, other = refs[:n_out], refs[n_out : 2 * n_out]
    ids_ref, info_ref, own, away, store, sems = refs[2 * n_out :]
    _, _, core = place()
    load_kv(n_out, blk_rows, mine, other, ids_ref, store, sems, core)
    slots = own.shape[0]
    row = lax.broadcasted_iota(jnp.int32, (blk_rows, HD), 0)
    for target, base in ((own, 0), (away, slots)):
        for i in range(slots):
            here = aligned(info_ref[1, base + i], blk_rows)
            live = row < info_ref[2, base + i]
            for half in range(2):
                page = store[half, here, :]
                target[i, :, half * HD : (half + 1) * HD] = jnp.where(live, page, jnp.zeros_like(page))


def finish_kernel(kept, from_far, own_pages, got_pages, info_ref, att_out, page_out, sems):
    _, pair, _ = place()
    width = kept.shape[1]
    copies = [
        pltpu.make_async_copy(kept, att_out.at[:, aligned(pair, width)], sems.at[0]),
        pltpu.make_async_copy(from_far, att_out.at[:, aligned(1 - pair, width)], sems.at[1]),
    ]
    for copy in copies:
        copy.start()
    for i in range(page_out.shape[0]):
        here = info_ref[0, i] == pair
        ours = pltpu.make_async_copy(own_pages.at[i], page_out.at[i], sems.at[2 + i])
        theirs = pltpu.make_async_copy(got_pages.at[i], page_out.at[i], sems.at[2 + i])
        copies.append(ours)

        @pl.when(here)
        def _():
            ours.start()

        @pl.when(jnp.logical_not(here))
        def _():
            theirs.start()

    for copy in copies:
        copy.wait()


def body(tokens, block_ids, lengths, page_table, qkv_weight, q_gain, k_gain):
    n_req, n_blk = lax.axis_size("req"), lax.axis_size("blk")
    n_out = n_blk // TEAM
    bf16 = jnp.bfloat16
    shape = jax.ShapeDtypeStruct
    blk = lax.axis_index("blk")
    member = blk % TEAM

    def in_team(array, k):
        return lax.ppermute(array, "blk", [(i, i ^ k) for i in range(n_blk)])

    def in_req(array, k):
        return lax.ppermute(array, "req", [(i, i ^ k) for i in range(n_req)])

    def across(array, k):
        return lax.ppermute(array, "blk", [(i, (i + TEAM * k) % n_blk) for i in range(n_blk)])

    def sync(*arrays):
        return lax.optimization_barrier(arrays)

    w_rows = qkv_weight.shape[0]
    per_device = block_ids.shape[1]
    lane = jnp.arange(HD, dtype=jnp.int32) - member * per_device
    ids_row = jnp.zeros((HD,), jnp.int32)
    for j in range(per_device):
        ids_row = jnp.where(lane == j, block_ids[0, j], ids_row)
    ids_rows = jnp.broadcast_to(ids_row.astype(bf16)[None, :], (ID_ROWS, HD))
    packed = pl.pallas_call(
        pack_kernel,
        out_shape=[shape((w_rows + ID_ROWS, HD), bf16)] * TEAM + [shape((w_rows, 2 * HD), bf16)] * TEAM,
        in_specs=[VMEM] * 2,
        out_specs=[VMEM] * (2 * TEAM),
        compiler_params=params(2),
        name="pack",
    )(qkv_weight, ids_rows)

    def exchange(parts):
        return [parts[0]] + [in_team(part, k) for k, part in enumerate(parts) if k]

    def assemble(parts):
        below = parts[0].shape[0] - w_rows
        return pl.pallas_call(
            functools.partial(team_kernel, w_rows),
            out_shape=[shape((TEAM * w_rows + below, HD), bf16)] * (parts[0].shape[1] // HD),
            in_specs=[VMEM] * TEAM,
            out_specs=[VMEM] * (parts[0].shape[1] // HD),
            compiler_params=params(2),
            name="team",
        )(*parts)

    def from_others(piece):
        got = [across(piece, k) for k in range(1, n_out)]
        return got[0] if len(got) == 1 else jnp.concatenate(got, 0)

    own = tokens[0]
    rows = own.shape[0]
    own_near = in_team(own, 1)
    (kv,) = assemble(exchange(packed[:TEAM]))
    kv, own, *q_parts = sync(kv, own, *packed[TEAM:])
    kv_o, kv_x, kv_y = from_others(kv), in_req(kv, 1), in_req(kv, 2)
    qa, qb = assemble(exchange(q_parts))
    far_a = in_team(own[: rows // 2], 2)
    kv, kv_o, kv_x, kv_y, qa, qb, far_a, own, own_near = sync(kv, kv_o, kv_x, kv_y, qa, qb, far_a, own, own_near)
    kv_ox, kv_oy, kv_d = in_req(kv_o, 1), in_req(kv_o, 2), in_req(kv_x, 2)
    qa_o, qa_x = from_others(qa), in_req(qa, 1)
    far_b = in_team(own[rows // 2 :], 2)
    kv_ox, kv_oy, kv_d, qa, qa_o, qa_x, qb, far_a, far_b = sync(kv_ox, kv_oy, kv_d, qa, qa_o, qa_x, qb, far_a, far_b)
    kv_od = in_req(kv_oy, 1)
    qb_o, qa_y, qa_ox, qa_oy = from_others(qb), in_req(qa, 2), in_req(qa_o, 1), in_req(qa_o, 2)
    far = jnp.concatenate([far_a, far_b], 0)
    far_near = in_team(far, 1)
    stacked = pl.pallas_call(
        stack_kernel,
        out_shape=shape((TEAM * rows, own.shape[1]), bf16),
        in_specs=[ANY] * TEAM,
        out_specs=VMEM,
        scratch_shapes=[pltpu.SemaphoreType.DMA((TEAM,))],
        compiler_params=params(4),
        name="stack",
    )(own, own_near, far, far_near)
    kv_od, qa_y, qa_ox, qa_oy, qb, qb_o, stacked = sync(kv_od, qa_y, qa_ox, qa_oy, qb, qb_o, stacked)
    kv_weight = [kv, kv_o, kv_x, kv_ox, kv_y, kv_oy, kv_d, kv_od]
    qb_x, qb_y, qb_ox, qb_oy = in_req(qb, 1), in_req(qb, 2), in_req(qb_o, 1), in_req(qb_o, 2)
    qa_x, qa_oy, qb_x, qb_y, qb_ox, qb_oy = sync(qa_x, qa_oy, qb_x, qb_y, qb_ox, qb_oy)
    qa_od, qb_od, qa_d, qb_d = in_req(qa_oy, 1), in_req(qb_oy, 1), in_req(qa_x, 2), in_req(qb_x, 2)
    q_weight = [qa, qa_o, qa_x, qa_ox, qa_y, qa_oy, qa_d, qa_od]
    q_weight += [qb, qb_o, qb_x, qb_ox, qb_y, qb_oy, qb_d, qb_od]

    blk_rows = rows // per_device
    tall = kv.shape[0]
    team_ids = kv[tall - ID_ROWS, : TEAM * per_device][None].astype(jnp.int32)
    other_ids = kv_o.reshape(n_out - 1, tall, HD)[:, tall - ID_ROWS, : TEAM * per_device].astype(jnp.int32)
    all_ids = jnp.concatenate([team_ids, other_ids], 0).reshape(-1)

    offsets = jnp.arange(blk_rows, dtype=jnp.int32)
    positions = (team_ids[0][:, None] * blk_rows + offsets[None, :]).reshape(-1, 1)
    inverse = jnp.power(jnp.float32(ROPE_BASE), -2.0 * jnp.arange(HD // 2).astype(jnp.float32) / HD)
    angles = positions.astype(jnp.float32) * inverse[None, :]
    cosine, sine = jnp.cos(angles), jnp.sin(angles)

    def project(steps, weight, is_kv, gain):
        width = len(weight) // (2 * n_req) * HD
        depth = own.shape[1]
        return pl.pallas_call(
            functools.partial(project_kernel, steps, n_out, TEAM * w_rows, is_kv),
            out_shape=shape((len(steps) * rows, width), bf16),
            in_specs=[VMEM] + [ANY] * len(weight) + [VMEM] * 3,
            out_specs=VMEM,
            scratch_shapes=[
                pltpu.VMEM((depth, width), bf16),
                pltpu.SemaphoreType.DMA((n_req * n_out * width // HD,)),
            ],
            cost_estimate=pl.CostEstimate(
                flops=2 * len(steps) * rows * depth * width, bytes_accessed=6 * MIB, transcendentals=0
            ),
            compiler_params=params(12),
            name="project_kv" if is_kv else "project_q",
        )(stacked, *weight, gain[None, :], cosine, sine)

    made = project((0, 1, 2, 3), kv_weight, True, k_gain)
    mine = [made] + [across(made, k) for k in range(1, n_out)]
    other = [in_team(part, 1) for part in mine]

    from_near = in_team(project((1, 3), q_weight, False, q_gain), 1)
    queries = project((0, 2), q_weight, False, q_gain)

    table = page_table[0].reshape(-1)
    per_head = page_table.shape[2]
    slot_count = page_table.shape[1] * per_head // n_blk
    wanted = jnp.concatenate(
        [b * slot_count + jnp.arange(slot_count, dtype=jnp.int32) for b in (blk, blk ^ 2)]
    )
    flat = jnp.sum(
        jnp.where(wanted[:, None] == table[None, :], jnp.arange(table.shape[0], dtype=jnp.int32)[None, :], 0), 1
    )
    block = flat % per_head
    info = jnp.stack([flat // per_head, block, lengths[0] - block * blk_rows])

    total = TEAM * rows * n_out
    store_mib = -(-2 * total * HD * 2 // MIB)
    page_shape = shape((slot_count, blk_rows, 2 * HD), bf16)
    own_pages, away_pages, store = pl.pallas_call(
        functools.partial(pages_kernel, n_out, blk_rows),
        out_shape=[page_shape, page_shape, shape((2, total, HD), bf16)],
        in_specs=[ANY] * (2 * n_out) + [SMEM] * 2,
        out_specs=[VMEM] * 3,
        scratch_shapes=[pltpu.SemaphoreType.DMA((2, total // blk_rows))],
        cost_estimate=pl.CostEstimate(flops=0, bytes_accessed=4 * MIB, transcendentals=0),
        compiler_params=params(store_mib + 4),
        name="pages",
    )(*mine, *other, all_ids, info)
    got_pages = in_team(away_pages, 2)

    def attend(step):
        return pl.pallas_call(
            functools.partial(attend_kernel, blk_rows, step),
            out_shape=shape((rows, H // 2 * HD), bf16),
            in_specs=[VMEM] * 3 + [SMEM] * 2,
            out_specs=VMEM,
            cost_estimate=pl.CostEstimate(
                flops=2 * H * HD * rows * total, bytes_accessed=4 * MIB, transcendentals=0
            ),
            compiler_params=params(store_mib + 4 + 4 * total // 1024),
            name="attend",
        )(store, queries, from_near, all_ids, lengths)

    from_far = in_team(attend(2), 2)
    kept = attend(0)

    attended, pages = pl.pallas_call(
        finish_kernel,
        out_shape=[shape((rows, H * HD), bf16), page_shape],
        in_specs=[ANY] * 4 + [SMEM],
        out_specs=[ANY] * 2,
        scratch_shapes=[pltpu.SemaphoreType.DMA((2 + slot_count,))],
        compiler_params=params(1),
        name="finish",
    )(kept, from_far, own_pages, got_pages, info)
    return attended[None], pages[None]


def solution(mesh):
    in_specs = (
        P("req", "blk", None),
        P("req", "blk"),
        P("req"),
        P("req", None, None),
        P(("req", "blk"), None),
        P(),
        P(),
    )
    out_specs = (P("req", "blk", None), P("req", "blk", None, None))
    return jax.shard_map(body, mesh=mesh, in_specs=in_specs, out_specs=out_specs, check_vma=False)
```

```python
import functools

import jax
import jax.numpy as jnp
from jax import lax
from jax.experimental import pallas as pl
from jax.experimental.pallas import tpu as pltpu
from jax.sharding import PartitionSpec as P

H = 8
KVH = 2
HD = 256
TEAM = 4
ID_ROWS = 16
ROPE_BASE = 1000000.0
NORM_EPS = 1e-06
MIB = 1024 * 1024

ANY = pl.BlockSpec(memory_space=pl.ANY)
VMEM = pl.BlockSpec(memory_space=pltpu.VMEM)
SMEM = pl.BlockSpec(memory_space=pltpu.SMEM)


def params(mib):
    return pltpu.CompilerParams(vmem_limit_bytes=mib * MIB)


def place():
    blk = lax.axis_index("blk")
    return lax.axis_index("req"), (blk // 2) % 2, blk % 2


def run(copies):
    for copy in copies:
        copy.start()
    for copy in copies:
        copy.wait()


def aligned(index, size):
    return pl.ds(pl.multiple_of(index * size, size), size)


def q_start(pair, core):
    return pl.multiple_of((pair * 2 + core) * 2 * HD, 2 * HD)


def kv_start(pair, core):
    return pl.multiple_of(H * HD + core * KVH * HD + pair * HD, HD)


def pack_kernel(w_ref, ids_ref, *outs):
    _, pair, core = place()
    member = pair * 2 + core
    rows = w_ref.shape[0]
    per_device = ids_ref.shape[1]
    lane = lax.broadcasted_iota(jnp.int32, (ID_ROWS, HD), 1) - member * per_device
    ids = jnp.zeros((ID_ROWS, HD), jnp.int32)
    for j in range(per_device):
        ids = jnp.where(lane == j, ids_ref[0, j], ids)
    ids = ids.astype(jnp.float32).astype(jnp.bfloat16)
    for k in range(TEAM):
        to_pair, to_core = pair ^ (k // 2), core ^ (k % 2)
        outs[k][:rows, :HD] = w_ref[:, pl.ds(kv_start(to_pair, to_core), HD)]
        outs[k][:rows, HD:] = w_ref[:, pl.ds(q_start(to_pair, to_core), 2 * HD)]
        outs[k][rows:, :HD] = ids
        outs[k][rows:, HD:] = jnp.zeros((ID_ROWS, 2 * HD), jnp.bfloat16)


def team_kernel(*refs):
    _, pair, core = place()
    parts, kv_out, q_out = refs[:TEAM], refs[TEAM], refs[TEAM + 1]
    rows = q_out.shape[0] // TEAM
    member = pair * 2 + core
    for k in range(TEAM):
        here = aligned(member ^ k, rows)
        kv_out[here, :] = parts[k][:rows, :HD]
        q_out[here, :] = parts[k][:rows, HD:]
    below = [part[rows:, :HD].astype(jnp.float32) for part in parts]
    kv_out[TEAM * rows :, :] = sum(below[1:], below[0]).astype(jnp.bfloat16)


def stack_kernel(*refs):
    _, pair, core = place()
    tokens, out, sems = refs[:TEAM], refs[TEAM], refs[TEAM + 1]
    rows = tokens[0].shape[0]
    member = pair * 2 + core
    run([
        pltpu.make_async_copy(tokens[k], out.at[aligned(member ^ k, rows), :], sems.at[k]) for k in range(TEAM)
    ])


def project_kernel(n_out, depth, is_kv, x_ref, *refs):
    n_outs = 1 if is_kv else 2
    weights, (gain_ref, cos_ref, sin_ref) = refs[: -5 - n_outs], refs[-5 - n_outs : -2 - n_outs]
    outs, (w_all, sems) = refs[-2 - n_outs : -2], refs[-2:]
    req = lax.axis_index("req")
    outer = lax.axis_index("blk") // TEAM
    _, pair, core = place()
    member = pair * 2 + core
    rows = x_ref.shape[0] // TEAM
    copies = []
    for i, piece in enumerate(weights):
        from_req = req ^ (i // 2)
        tall = piece.shape[0] // (n_out - 1 if i % 2 else 1)
        for n in range(n_out - 1 if i % 2 else 1):
            from_outer = lax.rem(outer + n_out - n - i % 2, n_out)
            copies.append(
                pltpu.make_async_copy(
                    piece.at[pl.ds(n * tall, depth), :],
                    w_all.at[aligned(from_req * n_out + from_outer, depth), :],
                    sems.at[len(copies)],
                )
            )
    run(copies)
    half = HD // 2
    gain = gain_ref[...]
    if is_kv:
        gain = jnp.where(core == 0, gain, 1.0)
    for out, steps in zip(outs, [(0, 1, 2, 3)] if is_kv else [(1, 3), (0, 2)]):
        if is_kv:
            x, cosine, sine = x_ref[...], cos_ref[...], sin_ref[...]
            cosine = jnp.where(core == 0, cosine, 1.0)
            sine = jnp.where(core == 0, sine, 0.0)
        else:
            x, cosine, sine = (
                jnp.concatenate([ref[aligned(member ^ k, rows), :] for k in steps], 0)
                for ref in (x_ref, cos_ref, sin_ref)
            )
        product = jnp.dot(x, w_all[...], preferred_element_type=jnp.float32)
        for h in range(out.shape[1] // HD):
            head = product[:, h * HD : (h + 1) * HD]
            mean = jnp.mean(head * head, axis=-1, keepdims=True)
            head = head * lax.rsqrt(mean + NORM_EPS) * gain
            front, second = head[:, :half], head[:, half:]
            out[:, h * HD : h * HD + half] = (front * cosine - second * sine).astype(jnp.bfloat16)
            out[:, h * HD + half : (h + 1) * HD] = (second * cosine + front * sine).astype(jnp.bfloat16)


def load_kv(n_out, blk_rows, mine, other, ids_ref, store, sems, core):
    per_piece = mine[0].shape[0] // blk_rows
    copies = []
    for k in range(n_out):
        for j in range(per_piece):
            n = k * per_piece + j
            there = aligned(ids_ref[n], blk_rows)
            here = pl.ds(j * blk_rows, blk_rows)
            copies.append(pltpu.make_async_copy(mine[k].at[here, :], store.at[core, there, :], sems.at[0, n]))
            copies.append(pltpu.make_async_copy(other[k].at[here, :], store.at[1 - core, there, :], sems.at[1, n]))
    run(copies)


def attend_kernel(blk_rows, step, store, q_ref, near_ref, ids_ref, length_ref, out):
    _, pair, core = place()
    length = length_ref[0]
    rows = out.shape[0]
    member = (pair * 2 + core) ^ step
    total = store.shape[1]
    quarter = total // 4
    heads = 2 * (out.shape[1] // (2 * HD))
    first = step // 2 * rows
    for j in range(rows // blk_rows):
        block = ids_ref[member * (rows // blk_rows) + j]
        here = slice(first + j * blk_rows, first + (j + 1) * blk_rows)
        there = slice(j * blk_rows, (j + 1) * blk_rows)
        for variant in range(4):
            seen = (variant + 1) * quarter

            @pl.when((block * blk_rows) // quarter == variant)
            def _():
                queries = jnp.concatenate(
                    [ref[here, h * HD : (h + 1) * HD] for ref in (q_ref, near_ref) for h in range(heads // 2)], 0
                )
                shape = (heads * blk_rows, 1)
                query_pos = block * blk_rows + lax.rem(lax.broadcasted_iota(jnp.int32, shape, 0), blk_rows)
                limit = jnp.minimum(query_pos, length - 1)
                key_pos = lax.broadcasted_iota(jnp.int32, (1, seen), 1)
                scores = lax.dot_general(
                    queries,
                    store[0, :seen, :],
                    (((1,), (1,)), ((), ())),
                    preferred_element_type=jnp.float32,
                )
                scores = jnp.where(key_pos <= limit, scores, jnp.finfo(jnp.float32).min)
                weights = jnp.exp(scores - jnp.max(scores, axis=-1, keepdims=True))
                row_sum = jnp.sum(weights, axis=-1, keepdims=True)
                summed = jnp.dot(
                    weights.astype(jnp.bfloat16), store[1, :seen, :], preferred_element_type=jnp.float32
                )
                result = jnp.where(query_pos < length, summed / row_sum, 0.0).astype(jnp.bfloat16)
                for n in range(heads):
                    side = core if n < heads // 2 else 1 - core
                    column = side * (heads // 2) + n % (heads // 2)
                    out[there, aligned(column, HD)] = result[n * blk_rows : (n + 1) * blk_rows]


def pages_kernel(n_out, blk_rows, *refs):
    mine, other = refs[:n_out], refs[n_out : 2 * n_out]
    ids_ref, info_ref, own, away, store, sems = refs[2 * n_out :]
    _, _, core = place()
    load_kv(n_out, blk_rows, mine, other, ids_ref, store, sems, core)
    slots = own.shape[0]
    row = lax.broadcasted_iota(jnp.int32, (blk_rows, HD), 0)
    for target, base in ((own, 0), (away, slots)):
        for i in range(slots):
            here = aligned(info_ref[1, base + i], blk_rows)
            live = row < info_ref[2, base + i]
            for half in range(2):
                page = store[half, here, :]
                target[i, :, half * HD : (half + 1) * HD] = jnp.where(live, page, jnp.zeros_like(page))


def finish_kernel(kept, from_far, own_pages, got_pages, info_ref, att_out, page_out, sems):
    _, pair, _ = place()
    width = kept.shape[1]
    copies = [
        pltpu.make_async_copy(kept, att_out.at[:, aligned(pair, width)], sems.at[0]),
        pltpu.make_async_copy(from_far, att_out.at[:, aligned(1 - pair, width)], sems.at[1]),
    ]
    for copy in copies:
        copy.start()
    for i in range(page_out.shape[0]):
        here = info_ref[0, i] == pair
        ours = pltpu.make_async_copy(own_pages.at[i], page_out.at[i], sems.at[2 + i])
        theirs = pltpu.make_async_copy(got_pages.at[i], page_out.at[i], sems.at[2 + i])
        copies.append(ours)

        @pl.when(here)
        def _():
            ours.start()

        @pl.when(jnp.logical_not(here))
        def _():
            theirs.start()

    for copy in copies:
        copy.wait()


def body(tokens, block_ids, lengths, page_table, qkv_weight, q_gain, k_gain):
    n_req, n_blk = lax.axis_size("req"), lax.axis_size("blk")
    n_out = n_blk // TEAM
    bf16 = jnp.bfloat16
    shape = jax.ShapeDtypeStruct
    blk = lax.axis_index("blk")
    member = blk % TEAM

    def in_team(array, k):
        return lax.ppermute(array, "blk", [(i, i ^ k) for i in range(n_blk)])

    def in_req(array, k):
        return lax.ppermute(array, "req", [(i, i ^ k) for i in range(n_req)])

    def across(array, k):
        return lax.ppermute(array, "blk", [(i, (i + TEAM * k) % n_blk) for i in range(n_blk)])

    def sync(*arrays):
        return lax.optimization_barrier(arrays)

    w_rows = qkv_weight.shape[0]
    per_device = block_ids.shape[1]
    parts = pl.pallas_call(
        pack_kernel,
        out_shape=[shape((w_rows + ID_ROWS, 3 * HD), bf16)] * TEAM,
        in_specs=[VMEM, SMEM],
        out_specs=[VMEM] * TEAM,
        compiler_params=params(2),
        name="pack",
    )(qkv_weight, block_ids)
    own = tokens[0]
    rows = own.shape[0]
    own_near = in_team(own, 1)
    kv, q = pl.pallas_call(
        team_kernel,
        out_shape=[shape((TEAM * w_rows + ID_ROWS, HD), bf16), shape((TEAM * w_rows, 2 * HD), bf16)],
        in_specs=[VMEM] * TEAM,
        out_specs=[VMEM] * 2,
        compiler_params=params(2),
        name="team",
    )(parts[0], *[in_team(parts[k], k) for k in range(1, TEAM)])

    def from_others(piece):
        got = [across(piece, k) for k in range(1, n_out)]
        return got[0] if len(got) == 1 else jnp.concatenate(got, 0)

    kv, q, own, own_near = sync(kv, q, own, own_near)
    kv_o, kv_x, kv_y = from_others(kv), in_req(kv, 1), in_req(kv, 2)
    far = in_team(own, 2)
    kv_x, kv_y, q = sync(kv_x, kv_y, q)
    q_x, q_y, kv_d = in_req(q, 1), in_req(q, 2), in_req(kv_x, 2)
    kv_o, kv_d, q = sync(kv_o, kv_d, q)
    q_o, kv_ox, kv_oy = from_others(q), in_req(kv_o, 1), in_req(kv_o, 2)
    q_x, q_y, kv_ox, kv_oy, far = sync(q_x, q_y, kv_ox, kv_oy, far)
    kv_od, q_d, far_near = in_req(kv_oy, 1), in_req(q_x, 2), in_team(far, 1)
    kv_weight = [kv, kv_o, kv_x, kv_ox, kv_y, kv_oy, kv_d, kv_od]
    q_o, q_d, kv_od = sync(q_o, q_d, kv_od)
    q_ox, q_oy = in_req(q_o, 1), in_req(q_o, 2)
    q_od = in_req(q_oy, 1)
    q_weight = [q, q_o, q_x, q_ox, q_y, q_oy, q_d, q_od]
    stacked = pl.pallas_call(
        stack_kernel,
        out_shape=shape((TEAM * rows, own.shape[1]), bf16),
        in_specs=[ANY] * TEAM,
        out_specs=VMEM,
        scratch_shapes=[pltpu.SemaphoreType.DMA((TEAM,))],
        compiler_params=params(4),
        name="stack",
    )(own, own_near, far, far_near)

    blk_rows = rows // per_device
    tall = kv.shape[0]
    team_ids = kv[tall - ID_ROWS, : TEAM * per_device][None].astype(jnp.int32)
    other_ids = kv_o.reshape(n_out - 1, tall, HD)[:, tall - ID_ROWS, : TEAM * per_device].astype(jnp.int32)
    all_ids = jnp.concatenate([team_ids, other_ids], 0).reshape(-1)

    offsets = jnp.arange(blk_rows, dtype=jnp.int32)
    positions = (team_ids[0][:, None] * blk_rows + offsets[None, :]).reshape(-1, 1)
    inverse = jnp.power(jnp.float32(ROPE_BASE), -2.0 * jnp.arange(HD // 2).astype(jnp.float32) / HD)
    angles = positions.astype(jnp.float32) * inverse[None, :]
    cosine, sine = jnp.cos(angles), jnp.sin(angles)

    def project(weight, is_kv, gain):
        width = weight[0].shape[1]
        depth = own.shape[1]
        n_outs = 1 if is_kv else 2
        return pl.pallas_call(
            functools.partial(project_kernel, n_out, TEAM * w_rows, is_kv),
            out_shape=[shape((TEAM * rows // n_outs, width), bf16)] * n_outs,
            in_specs=[VMEM] + [ANY] * len(weight) + [VMEM] * 3,
            out_specs=[VMEM] * n_outs,
            scratch_shapes=[
                pltpu.VMEM((depth, width), bf16),
                pltpu.SemaphoreType.DMA((n_req * n_out,)),
            ],
            cost_estimate=pl.CostEstimate(
                flops=2 * TEAM * rows * depth * width, bytes_accessed=6 * MIB, transcendentals=0
            ),
            compiler_params=params(12),
            name="project_kv" if is_kv else "project_q",
        )(stacked, *weight, gain[None, :], cosine, sine)

    (made,) = project(kv_weight, True, k_gain)
    mine = [made] + [across(made, k) for k in range(1, n_out)]
    other = [in_team(part, 1) for part in mine]

    to_near, queries = project(q_weight, False, q_gain)
    from_near = in_team(to_near, 1)

    table = page_table[0].reshape(-1)
    per_head = page_table.shape[2]
    slot_count = page_table.shape[1] * per_head // n_blk
    wanted = jnp.concatenate(
        [b * slot_count + jnp.arange(slot_count, dtype=jnp.int32) for b in (blk, blk ^ 2)]
    )
    flat = jnp.sum(
        jnp.where(wanted[:, None] == table[None, :], jnp.arange(table.shape[0], dtype=jnp.int32)[None, :], 0), 1
    )
    block = flat % per_head
    info = jnp.stack([flat // per_head, block, lengths[0] - block * blk_rows])

    total = TEAM * rows * n_out
    store_mib = -(-2 * total * HD * 2 // MIB)
    page_shape = shape((slot_count, blk_rows, 2 * HD), bf16)
    own_pages, away_pages, store = pl.pallas_call(
        functools.partial(pages_kernel, n_out, blk_rows),
        out_shape=[page_shape, page_shape, shape((2, total, HD), bf16)],
        in_specs=[ANY] * (2 * n_out) + [SMEM] * 2,
        out_specs=[VMEM] * 3,
        scratch_shapes=[pltpu.SemaphoreType.DMA((2, total // blk_rows))],
        cost_estimate=pl.CostEstimate(flops=0, bytes_accessed=4 * MIB, transcendentals=0),
        compiler_params=params(store_mib + 4),
        name="pages",
    )(*mine, *other, all_ids, info)
    got_pages = in_team(away_pages, 2)

    def attend(step):
        return pl.pallas_call(
            functools.partial(attend_kernel, blk_rows, step),
            out_shape=shape((rows, H // 2 * HD), bf16),
            in_specs=[VMEM] * 3 + [SMEM] * 2,
            out_specs=VMEM,
            cost_estimate=pl.CostEstimate(
                flops=2 * H * HD * rows * total, bytes_accessed=4 * MIB, transcendentals=0
            ),
            compiler_params=params(store_mib + 4 + 4 * total // 1024),
            name="attend",
        )(store, queries, from_near, all_ids, lengths)

    from_far = in_team(attend(2), 2)
    kept = attend(0)

    attended, pages = pl.pallas_call(
        finish_kernel,
        out_shape=[shape((rows, H * HD), bf16), page_shape],
        in_specs=[ANY] * 4 + [SMEM],
        out_specs=[ANY] * 2,
        scratch_shapes=[pltpu.SemaphoreType.DMA((2 + slot_count,))],
        compiler_params=params(1),
        name="finish",
    )(kept, from_far, own_pages, got_pages, info)
    return attended[None], pages[None]


def solution(mesh):
    in_specs = (
        P("req", "blk", None),
        P("req", "blk"),
        P("req"),
        P("req", None, None),
        P(("req", "blk"), None),
        P(),
        P(),
    )
    out_specs = (P("req", "blk", None), P("req", "blk", None, None))
    return jax.shard_map(body, mesh=mesh, in_specs=in_specs, out_specs=out_specs, check_vma=False)
```

```python
import functools

import jax
import jax.numpy as jnp
from jax import lax
from jax.experimental import pallas as pl
from jax.experimental.pallas import tpu as pltpu
from jax.sharding import PartitionSpec as P

H = 8
KVH = 2
HD = 256
TEAM = 4
ID_ROWS = 16
LANES = 128
ROPE_BASE = 1000000.0
NORM_EPS = 1e-06
MIB = 1024 * 1024

ANY = pl.BlockSpec(memory_space=pl.ANY)
VMEM = pl.BlockSpec(memory_space=pltpu.VMEM)
SMEM = pl.BlockSpec(memory_space=pltpu.SMEM)


def params(mib):
    return pltpu.CompilerParams(vmem_limit_bytes=mib * MIB)


def place():
    blk = lax.axis_index("blk")
    return lax.axis_index("req"), (blk // 2) % 2, blk % 2


def run(copies):
    for copy in copies:
        copy.start()
    for copy in copies:
        copy.wait()


def aligned(index, size):
    return pl.ds(pl.multiple_of(index * size, size), size)


def q_start(pair, core):
    return pl.multiple_of((pair * 2 + core) * 2 * HD, 2 * HD)


def kv_start(pair, core):
    return pl.multiple_of(H * HD + core * KVH * HD + pair * HD, HD)


def pack_kernel(w_hbm, ids_hbm, *refs):
    outs, (w_ref, ids_ref, sems) = refs[:TEAM], refs[TEAM:]
    run([pltpu.make_async_copy(w_hbm, w_ref, sems.at[0]), pltpu.make_async_copy(ids_hbm, ids_ref, sems.at[1])])
    _, pair, core = place()
    member = pair * 2 + core
    rows = w_ref.shape[0]
    per_device = ids_ref.shape[1]
    lane = lax.broadcasted_iota(jnp.int32, (ID_ROWS, LANES), 1) - member * per_device
    ids = jnp.zeros((ID_ROWS, LANES), jnp.int32)
    for j in range(per_device):
        ids = jnp.where(lane == j, ids_ref[0, j], ids)
    ids = ids.astype(jnp.float32).astype(jnp.bfloat16)
    for k in range(TEAM):
        to_pair, to_core = pair ^ (k // 2), core ^ (k % 2)
        for n in range(3 * HD // LANES):
            if n < HD // LANES:
                start = pl.multiple_of(kv_start(to_pair, to_core) + n * LANES, LANES)
            else:
                start = pl.multiple_of(q_start(to_pair, to_core) + n * LANES - HD, LANES)
            outs[k][n * rows : (n + 1) * rows, :] = w_ref[:, pl.ds(start, LANES)]
        outs[k][3 * HD // LANES * rows :, :] = ids


def team_kernel(*refs):
    _, pair, core = place()
    parts, (kv_out, q_out, *q_halves) = refs[:TEAM], refs[TEAM:]
    rows = q_out.shape[0] // TEAM
    member = pair * 2 + core
    for k in range(TEAM):
        here = aligned(member ^ k, rows)
        for n in range(3 * HD // LANES):
            out = kv_out if n < HD // LANES else q_out
            first = n * LANES if n < HD // LANES else n * LANES - HD
            part = parts[k][n * rows : (n + 1) * rows, :]
            out[here, first : first + LANES] = part
            if out is q_out:
                q_halves[first // HD][here, first % HD : first % HD + LANES] = part
    below = [part[3 * HD // LANES * rows :, :].astype(jnp.float32) for part in parts]
    ids = sum(below[1:], below[0]).astype(jnp.bfloat16)
    kv_out[TEAM * rows :, :] = jnp.concatenate([ids] * (HD // LANES), 1)


def join_kernel(*refs):
    out = refs[-1]
    for n, ref in enumerate(refs[:-1]):
        width = ref.shape[1]
        out[:, n * width : (n + 1) * width] = ref[...]


def stack_kernel(*refs):
    _, pair, core = place()
    tokens, out, sems = refs[:TEAM], refs[TEAM], refs[TEAM + 1]
    rows = tokens[0].shape[0]
    member = pair * 2 + core
    run([
        pltpu.make_async_copy(tokens[k], out.at[aligned(member ^ k, rows), :], sems.at[k]) for k in range(TEAM)
    ])


def project_kernel(n_out, depth, is_kv, x_ref, *refs):
    n_outs = 1 if is_kv else 2
    weights, (gain_ref, cos_ref, sin_ref) = refs[: -5 - n_outs], refs[-5 - n_outs : -2 - n_outs]
    outs, (w_all, sems) = refs[-2 - n_outs : -2], refs[-2:]
    req = lax.axis_index("req")
    outer = lax.axis_index("blk") // TEAM
    _, pair, core = place()
    member = pair * 2 + core
    rows = x_ref.shape[0] // TEAM
    direct = depth % LANES == 0
    places = []
    for i, piece in enumerate(weights):
        from_req = req ^ (i // 2)
        tall = piece.shape[0] // (n_out - 1 if i % 2 else 1)
        for n in range(n_out - 1 if i % 2 else 1):
            from_outer = lax.rem(outer + n_out - n - i % 2, n_out)
            places.append((piece.at[pl.ds(n * tall, depth), :], aligned(from_req * n_out + from_outer, depth)))
    if not direct:
        run([
            pltpu.make_async_copy(piece, w_all.at[there, :], sems.at[n]) for n, (piece, there) in enumerate(places)
        ])
    half = HD // 2
    gain = gain_ref[...]
    if is_kv:
        gain = jnp.where(core == 0, gain, 1.0)
    for out, steps in zip(outs, [(0, 1, 2, 3)] if is_kv else [(1, 3), (0, 2)]):
        def team_rows(ref, cols):
            if is_kv:
                return ref[:, cols]
            return jnp.concatenate([ref[aligned(member ^ k, rows), cols] for k in steps], 0)

        every = slice(None)
        cosine, sine = team_rows(cos_ref, every), team_rows(sin_ref, every)
        if is_kv:
            cosine = jnp.where(core == 0, cosine, 1.0)
            sine = jnp.where(core == 0, sine, 0.0)
        if direct:
            product = 0.0
            for piece, there in places:
                product += jnp.dot(team_rows(x_ref, there), piece[...], preferred_element_type=jnp.float32)
        else:
            product = jnp.dot(team_rows(x_ref, every), w_all[...], preferred_element_type=jnp.float32)
        for h in range(out.shape[1] // HD):
            head = product[:, h * HD : (h + 1) * HD]
            mean = jnp.mean(head * head, axis=-1, keepdims=True)
            head = head * lax.rsqrt(mean + NORM_EPS) * gain
            front, second = head[:, :half], head[:, half:]
            out[:, h * HD : h * HD + half] = (front * cosine - second * sine).astype(jnp.bfloat16)
            out[:, h * HD + half : (h + 1) * HD] = (second * cosine + front * sine).astype(jnp.bfloat16)


def attend_kernel(blk_rows, step, store, q_ref, near_ref, ids_ref, length_ref, out):
    _, pair, core = place()
    length = length_ref[0]
    rows = out.shape[0]
    member = (pair * 2 + core) ^ step
    total = store.shape[1]
    quarter = total // 4
    heads = 2 * (out.shape[1] // (2 * HD))
    first = step // 2 * rows
    for j in range(rows // blk_rows):
        block = ids_ref[member * (rows // blk_rows) + j]
        here = slice(first + j * blk_rows, first + (j + 1) * blk_rows)
        there = slice(j * blk_rows, (j + 1) * blk_rows)
        for variant in range(4):
            seen = (variant + 1) * quarter

            @pl.when((block * blk_rows) // quarter == variant)
            def _():
                queries = jnp.concatenate(
                    [ref[here, h * HD : (h + 1) * HD] for ref in (q_ref, near_ref) for h in range(heads // 2)], 0
                )
                shape = (heads * blk_rows, 1)
                query_pos = block * blk_rows + lax.rem(lax.broadcasted_iota(jnp.int32, shape, 0), blk_rows)
                limit = jnp.minimum(query_pos, length - 1)
                key_pos = lax.broadcasted_iota(jnp.int32, (1, seen), 1)
                scores = lax.dot_general(
                    queries,
                    store[0, :seen, :],
                    (((1,), (1,)), ((), ())),
                    preferred_element_type=jnp.float32,
                )
                scores = jnp.where(key_pos <= limit, scores, jnp.finfo(jnp.float32).min)
                weights = jnp.exp(scores - jnp.max(scores, axis=-1, keepdims=True))
                row_sum = jnp.sum(weights, axis=-1, keepdims=True)
                summed = jnp.dot(
                    weights.astype(jnp.bfloat16), store[1, :seen, :], preferred_element_type=jnp.float32
                )
                result = jnp.where(query_pos < length, summed / row_sum, 0.0).astype(jnp.bfloat16)
                for n in range(heads):
                    side = core if n < heads // 2 else 1 - core
                    column = side * (heads // 2) + n % (heads // 2)
                    out[there, aligned(column, HD)] = result[n * blk_rows : (n + 1) * blk_rows]


def pages_kernel(n_out, blk_rows, *refs):
    mine, other = refs[:n_out], refs[n_out : 2 * n_out]
    ids_ref, info_ref, own, away, store = refs[2 * n_out :]
    _, _, core = place()
    per_piece = mine[0].shape[0] // blk_rows
    for k in range(n_out):
        for j in range(per_piece):
            there = aligned(ids_ref[k * per_piece + j], blk_rows)
            here = slice(j * blk_rows, (j + 1) * blk_rows)
            store[core, there, :] = mine[k][here, :]
            store[1 - core, there, :] = other[k][here, :]
    slots = own.shape[0]
    row = lax.broadcasted_iota(jnp.int32, (blk_rows, HD), 0)
    for target, base in ((away, slots), (own, 0)):
        for i in range(slots):
            here = aligned(info_ref[1, base + i], blk_rows)
            live = row < info_ref[2, base + i]
            for half in range(2):
                page = store[half, here, :]
                target[i, :, half * HD : (half + 1) * HD] = jnp.where(live, page, jnp.zeros_like(page))


def finish_kernel(kept, from_far, own_pages, got_pages, info_ref, att_out, page_out, sems):
    _, pair, _ = place()
    width = kept.shape[1]
    copies = [
        pltpu.make_async_copy(kept, att_out.at[:, aligned(pair, width)], sems.at[0]),
        pltpu.make_async_copy(from_far, att_out.at[:, aligned(1 - pair, width)], sems.at[1]),
    ]
    for copy in copies:
        copy.start()
    for i in range(page_out.shape[0]):
        here = info_ref[0, i] == pair
        ours = pltpu.make_async_copy(own_pages.at[i], page_out.at[i], sems.at[2 + i])
        theirs = pltpu.make_async_copy(got_pages.at[i], page_out.at[i], sems.at[2 + i])
        copies.append(ours)

        @pl.when(here)
        def _():
            ours.start()

        @pl.when(jnp.logical_not(here))
        def _():
            theirs.start()

    for copy in copies:
        copy.wait()


def body(tokens, block_ids, lengths, page_table, qkv_weight, q_gain, k_gain):
    n_req, n_blk = lax.axis_size("req"), lax.axis_size("blk")
    n_out = n_blk // TEAM
    bf16 = jnp.bfloat16
    shape = jax.ShapeDtypeStruct
    blk = lax.axis_index("blk")
    member = blk % TEAM

    def in_team(array, k):
        return lax.ppermute(array, "blk", [(i, i ^ k) for i in range(n_blk)])

    def in_req(array, k):
        return lax.ppermute(array, "req", [(i, i ^ k) for i in range(n_req)])

    def across(array, k):
        return lax.ppermute(array, "blk", [(i, (i + TEAM * k) % n_blk) for i in range(n_blk)])

    def sync(*arrays):
        return lax.optimization_barrier(arrays)

    w_rows = qkv_weight.shape[0]
    per_device = block_ids.shape[1]
    own = tokens[0]
    rows = own.shape[0]
    parts = pl.pallas_call(
        pack_kernel,
        out_shape=[shape((3 * HD // LANES * w_rows + ID_ROWS, LANES), bf16)] * TEAM,
        in_specs=[ANY] * 2,
        out_specs=[VMEM] * TEAM,
        scratch_shapes=[
            pltpu.VMEM(qkv_weight.shape, bf16),
            pltpu.SMEM(block_ids.shape, jnp.int32),
            pltpu.SemaphoreType.DMA((2,)),
        ],
        compiler_params=params(4),
        name="pack",
    )(qkv_weight, block_ids)
    head_rows = shape((TEAM * w_rows, HD), bf16)
    kv, q, qa, qb = pl.pallas_call(
        team_kernel,
        out_shape=[shape((TEAM * w_rows + ID_ROWS, HD), bf16), shape((TEAM * w_rows, 2 * HD), bf16), head_rows, head_rows],
        in_specs=[VMEM] * TEAM,
        out_specs=[VMEM] * 4,
        compiler_params=params(2),
        name="team",
    )(parts[0], *[in_team(parts[k], k) for k in range(1, TEAM)])

    def from_others(piece):
        got = [across(piece, k) for k in range(1, n_out)]
        return got[0] if len(got) == 1 else jnp.concatenate(got, 0)

    kv, q, own = sync(kv, q, own)
    kv_o, kv_x, kv_y = from_others(kv), in_req(kv, 1), in_req(kv, 2)
    far, own_near = in_team(own, 2), in_team(own, 1)
    kv_x, kv_y, q, own_near = sync(kv_x, kv_y, q, own_near)
    kv_d, q_x = in_req(kv_x, 2), in_req(q, 1)
    kv_o, kv_d, qa = sync(kv_o, kv_d, qa)
    qa_o, kv_ox, kv_oy = from_others(qa), in_req(kv_o, 1), in_req(kv_o, 2)
    kv_ox, kv_oy, q_x, q, qa_o, qb, far = sync(kv_ox, kv_oy, q_x, q, qa_o, qb, far)
    kv_od, q_y, qb_o, far_near = in_req(kv_oy, 1), in_req(q, 2), from_others(qb), in_team(far, 1)
    kv_od, q_y, qb_o, far_near = sync(kv_od, q_y, qb_o, far_near)
    kv_weight = [kv, kv_o, kv_x, kv_ox, kv_y, kv_oy, kv_d, kv_od]
    stacked = pl.pallas_call(
        stack_kernel,
        out_shape=shape((TEAM * rows, own.shape[1]), bf16),
        in_specs=[ANY] * TEAM,
        out_specs=VMEM,
        scratch_shapes=[pltpu.SemaphoreType.DMA((TEAM,))],
        compiler_params=params(4),
        name="stack",
    )(own, own_near, far, far_near)

    blk_rows = rows // per_device
    tall = kv.shape[0]
    team_ids = kv[tall - ID_ROWS, : TEAM * per_device][None].astype(jnp.int32)
    other_ids = kv_o.reshape(n_out - 1, tall, HD)[:, tall - ID_ROWS, : TEAM * per_device].astype(jnp.int32)
    all_ids = jnp.concatenate([team_ids, other_ids], 0).reshape(-1)

    offsets = jnp.arange(blk_rows, dtype=jnp.int32)
    positions = (team_ids[0][:, None] * blk_rows + offsets[None, :]).reshape(-1, 1)
    inverse = jnp.power(jnp.float32(ROPE_BASE), -2.0 * jnp.arange(HD // 2).astype(jnp.float32) / HD)
    angles = positions.astype(jnp.float32) * inverse[None, :]
    cosine, sine = jnp.cos(angles), jnp.sin(angles)

    def project(weight, is_kv, gain):
        width = weight[0].shape[1]
        depth = own.shape[1]
        n_outs = 1 if is_kv else 2
        return pl.pallas_call(
            functools.partial(project_kernel, n_out, TEAM * w_rows, is_kv),
            out_shape=[shape((TEAM * rows // n_outs, width), bf16)] * n_outs,
            in_specs=[VMEM] * (4 + len(weight)),
            out_specs=[VMEM] * n_outs,
            scratch_shapes=[
                pltpu.VMEM((depth, width) if w_rows * TEAM % LANES else (ID_ROWS, LANES), bf16),
                pltpu.SemaphoreType.DMA((n_req * n_out,)),
            ],
            cost_estimate=pl.CostEstimate(
                flops=2 * TEAM * rows * depth * width, bytes_accessed=6 * MIB, transcendentals=0
            ),
            compiler_params=params(12),
            name="project_kv" if is_kv else "project_q",
        )(stacked, *weight, gain[None, :], cosine, sine)

    (made,) = project(kv_weight, True, k_gain)
    q_o = pl.pallas_call(
        join_kernel,
        out_shape=shape((qa_o.shape[0], 2 * HD), bf16),
        in_specs=[VMEM] * 2,
        out_specs=VMEM,
        compiler_params=params(2 + 2 * n_out // 8),
        name="join",
    )(qa_o, qb_o)
    q_ox, q_oy = in_req(q_o, 1), in_req(q_o, 2)
    q_ox, q_oy, q_y = sync(q_ox, q_oy, q_y)
    q_d, q_od = in_req(q_y, 1), in_req(q_ox, 2)
    q_weight = [q, q_o, q_x, q_ox, q_y, q_oy, q_d, q_od]
    mine = [made] + [across(made, k) for k in range(1, n_out)]
    other = [in_team(part, 1) for part in mine]

    to_near, queries = project(q_weight, False, q_gain)
    from_near = in_team(to_near, 1)

    table = page_table[0].reshape(-1)
    per_head = page_table.shape[2]
    slot_count = page_table.shape[1] * per_head // n_blk
    wanted = jnp.concatenate(
        [b * slot_count + jnp.arange(slot_count, dtype=jnp.int32) for b in (blk, blk ^ 2)]
    )
    flat = jnp.sum(
        jnp.where(wanted[:, None] == table[None, :], jnp.arange(table.shape[0], dtype=jnp.int32)[None, :], 0), 1
    )
    block = flat % per_head
    info = jnp.stack([flat // per_head, block, lengths[0] - block * blk_rows])

    total = TEAM * rows * n_out
    store_mib = -(-2 * total * HD * 2 // MIB)
    page_shape = shape((slot_count, blk_rows, 2 * HD), bf16)
    own_pages, away_pages, store = pl.pallas_call(
        functools.partial(pages_kernel, n_out, blk_rows),
        out_shape=[page_shape, page_shape, shape((2, total, HD), bf16)],
        in_specs=[VMEM] * (2 * n_out) + [SMEM] * 2,
        out_specs=[VMEM] * 3,
        cost_estimate=pl.CostEstimate(flops=0, bytes_accessed=4 * MIB, transcendentals=0),
        compiler_params=params(2 * store_mib + 4),
        name="pages",
    )(*mine, *other, all_ids, info)
    got_pages = in_team(away_pages, 2)

    def attend(step):
        return pl.pallas_call(
            functools.partial(attend_kernel, blk_rows, step),
            out_shape=shape((rows, H // 2 * HD), bf16),
            in_specs=[VMEM] * 3 + [SMEM] * 2,
            out_specs=VMEM,
            cost_estimate=pl.CostEstimate(
                flops=2 * H * HD * rows * total, bytes_accessed=4 * MIB, transcendentals=0
            ),
            compiler_params=params(store_mib + 4 + 4 * total // 1024),
            name="attend",
        )(store, queries, from_near, all_ids, lengths)

    from_far = in_team(attend(2), 2)
    kept = attend(0)

    attended, pages = pl.pallas_call(
        finish_kernel,
        out_shape=[shape((rows, H * HD), bf16), page_shape],
        in_specs=[ANY] * 4 + [SMEM],
        out_specs=[ANY] * 2,
        scratch_shapes=[pltpu.SemaphoreType.DMA((2 + slot_count,))],
        compiler_params=params(1),
        name="finish",
    )(kept, from_far, own_pages, got_pages, info)
    return attended[None], pages[None]


def solution(mesh):
    in_specs = (
        P("req", "blk", None),
        P("req", "blk"),
        P("req"),
        P("req", None, None),
        P(("req", "blk"), None),
        P(),
        P(),
    )
    out_specs = (P("req", "blk", None), P("req", "blk", None, None))
    return jax.shard_map(body, mesh=mesh, in_specs=in_specs, out_specs=out_specs, check_vma=False)
```

```python
import functools

import jax
import jax.numpy as jnp
from jax import lax
from jax.experimental import pallas as pl
from jax.experimental.pallas import tpu as pltpu
from jax.sharding import PartitionSpec as P

H = 8
KVH = 2
HD = 256
TEAM = 4
ID_ROWS = 16
LANES = 128
ROPE_BASE = 1000000.0
NORM_EPS = 1e-06
MIB = 1024 * 1024

ANY = pl.BlockSpec(memory_space=pl.ANY)
VMEM = pl.BlockSpec(memory_space=pltpu.VMEM)
SMEM = pl.BlockSpec(memory_space=pltpu.SMEM)


def params(mib):
    return pltpu.CompilerParams(vmem_limit_bytes=mib * MIB)


def place():
    blk = lax.axis_index("blk")
    return lax.axis_index("req"), (blk // 2) % 2, blk % 2


def run(copies):
    for copy in copies:
        copy.start()
    for copy in copies:
        copy.wait()


def aligned(index, size):
    return pl.ds(pl.multiple_of(index * size, size), size)


def q_start(pair, core):
    return pl.multiple_of((pair * 2 + core) * 2 * HD, 2 * HD)


def kv_start(pair, core):
    return pl.multiple_of(H * HD + core * KVH * HD + pair * HD, HD)


def pack_kernel(w_hbm, ids_hbm, tokens_hbm, *refs):
    outs, (w_ref, ids_ref, tokens_ref, sems) = refs[:TEAM], refs[TEAM:]
    run([
        pltpu.make_async_copy(source, there, sems.at[n])
        for n, (source, there) in enumerate(((w_hbm, w_ref), (ids_hbm, ids_ref), (tokens_hbm, tokens_ref)))
    ])
    _, pair, core = place()
    member = pair * 2 + core
    rows = w_ref.shape[0]
    per_device = ids_ref.shape[1]
    lane = lax.broadcasted_iota(jnp.int32, (ID_ROWS, LANES), 1) - member * per_device
    ids = jnp.zeros((ID_ROWS, LANES), jnp.int32)
    for j in range(per_device):
        ids = jnp.where(lane == j, ids_ref[0, j], ids)
    ids = ids.astype(jnp.float32).astype(jnp.bfloat16)
    blocks = 3 * HD // LANES
    for k in range(TEAM):
        to_pair, to_core = pair ^ (k // 2), core ^ (k % 2)
        for n in range(blocks):
            if n < HD // LANES:
                start = pl.multiple_of(kv_start(to_pair, to_core) + n * LANES, LANES)
            else:
                start = pl.multiple_of(q_start(to_pair, to_core) + n * LANES - HD, LANES)
            outs[k][n * rows : (n + 1) * rows, :] = w_ref[:, pl.ds(start, LANES)]
        outs[k][blocks * rows : blocks * rows + ID_ROWS, :] = ids
    token_rows = tokens_ref.shape[0]
    for n in range(tokens_ref.shape[1] // LANES):
        first = blocks * rows + ID_ROWS + n * token_rows
        outs[1][first : first + token_rows, :] = tokens_ref[:, n * LANES : (n + 1) * LANES]


def team_kernel(*refs):
    _, pair, core = place()
    parts, (kv_out, q_out, whole) = refs[:TEAM], refs[TEAM:]
    rows = q_out.shape[0] // TEAM
    member = pair * 2 + core
    for k in range(TEAM):
        here = aligned(member ^ k, rows)
        for n in range(3 * HD // LANES):
            out = kv_out if n < HD // LANES else q_out
            first = n * LANES if n < HD // LANES else n * LANES - HD
            part = parts[k][n * rows : (n + 1) * rows, :]
            out[here, first : first + LANES] = part
            whole[here, n * LANES : (n + 1) * LANES] = part
    first = 3 * HD // LANES * rows
    below = [part[first : first + ID_ROWS, :].astype(jnp.float32) for part in parts]
    ids = sum(below[1:], below[0]).astype(jnp.bfloat16)
    kv_out[TEAM * rows :, :] = jnp.concatenate([ids] * (HD // LANES), 1)


def stack_kernel(first_row, own, near, far, far_near, out):
    _, pair, core = place()
    rows = own.shape[0]
    member = pair * 2 + core
    for k, ref in ((0, own), (2, far), (3, far_near)):
        out[aligned(member ^ k, rows), :] = ref[...]
    here = aligned(member ^ 1, rows)
    for n in range(out.shape[1] // LANES):
        first = first_row + n * rows
        out[here, n * LANES : (n + 1) * LANES] = near[first : first + rows, :]


def project_kernel(n_out, depth, is_kv, x_ref, *refs):
    n_outs = 1 if is_kv else 2
    weights, (gain_ref, cos_ref, sin_ref) = refs[: -5 - n_outs], refs[-5 - n_outs : -2 - n_outs]
    outs, (w_all, sems) = refs[-2 - n_outs : -2], refs[-2:]
    req = lax.axis_index("req")
    outer = lax.axis_index("blk") // TEAM
    _, pair, core = place()
    member = pair * 2 + core
    rows = x_ref.shape[0] // TEAM
    width = outs[0].shape[1]
    direct = depth % LANES == 0
    places = []
    for i, piece in enumerate(weights):
        from_req = req ^ (i // 2)
        tall = piece.shape[0] // (n_out - 1 if i % 2 else 1)
        for n in range(n_out - 1 if i % 2 else 1):
            from_outer = lax.rem(outer + n_out - n - i % 2, n_out)
            cols = slice(None) if piece.shape[1] == width else slice(*((0, HD) if is_kv else (HD, 3 * HD)))
            places.append((piece.at[pl.ds(n * tall, depth), cols], aligned(from_req * n_out + from_outer, depth)))
    if not direct:
        run([
            pltpu.make_async_copy(piece, w_all.at[there, :], sems.at[n]) for n, (piece, there) in enumerate(places)
        ])
    half = HD // 2
    gain = gain_ref[...]
    if is_kv:
        gain = jnp.where(core == 0, gain, 1.0)
    for out, steps in zip(outs, [(0, 1, 2, 3)] if is_kv else [(1, 3), (0, 2)]):
        def team_rows(ref, cols):
            if is_kv:
                return ref[:, cols]
            return jnp.concatenate([ref[aligned(member ^ k, rows), cols] for k in steps], 0)

        every = slice(None)
        cosine, sine = team_rows(cos_ref, every), team_rows(sin_ref, every)
        if is_kv:
            cosine = jnp.where(core == 0, cosine, 1.0)
            sine = jnp.where(core == 0, sine, 0.0)
        if direct:
            product = 0.0
            for piece, there in places:
                product += jnp.dot(team_rows(x_ref, there), piece[...], preferred_element_type=jnp.float32)
        else:
            product = jnp.dot(team_rows(x_ref, every), w_all[...], preferred_element_type=jnp.float32)
        for h in range(out.shape[1] // HD):
            head = product[:, h * HD : (h + 1) * HD]
            mean = jnp.mean(head * head, axis=-1, keepdims=True)
            head = head * lax.rsqrt(mean + NORM_EPS) * gain
            front, second = head[:, :half], head[:, half:]
            out[:, h * HD : h * HD + half] = (front * cosine - second * sine).astype(jnp.bfloat16)
            out[:, h * HD + half : (h + 1) * HD] = (second * cosine + front * sine).astype(jnp.bfloat16)


def attend_kernel(blk_rows, step, store, q_ref, near_ref, ids_ref, length_ref, out):
    _, pair, core = place()
    length = length_ref[0]
    rows = out.shape[0]
    member = (pair * 2 + core) ^ step
    total = store.shape[1]
    quarter = total // 4
    heads = 2 * (out.shape[1] // (2 * HD))
    first = step // 2 * rows
    for j in range(rows // blk_rows):
        block = ids_ref[member * (rows // blk_rows) + j]
        here = slice(first + j * blk_rows, first + (j + 1) * blk_rows)
        there = slice(j * blk_rows, (j + 1) * blk_rows)
        for variant in range(4):
            seen = (variant + 1) * quarter

            @pl.when((block * blk_rows) // quarter == variant)
            def _():
                queries = jnp.concatenate(
                    [ref[here, h * HD : (h + 1) * HD] for ref in (q_ref, near_ref) for h in range(heads // 2)], 0
                )
                shape = (heads * blk_rows, 1)
                query_pos = block * blk_rows + lax.rem(lax.broadcasted_iota(jnp.int32, shape, 0), blk_rows)
                limit = jnp.minimum(query_pos, length - 1)
                key_pos = lax.broadcasted_iota(jnp.int32, (1, seen), 1)
                scores = lax.dot_general(
                    queries,
                    store[0, :seen, :],
                    (((1,), (1,)), ((), ())),
                    preferred_element_type=jnp.float32,
                )
                scores = jnp.where(key_pos <= limit, scores, jnp.finfo(jnp.float32).min)
                weights = jnp.exp(scores - jnp.max(scores, axis=-1, keepdims=True))
                row_sum = jnp.sum(weights, axis=-1, keepdims=True)
                summed = jnp.dot(
                    weights.astype(jnp.bfloat16), store[1, :seen, :], preferred_element_type=jnp.float32
                )
                result = jnp.where(query_pos < length, summed / row_sum, 0.0).astype(jnp.bfloat16)
                for n in range(heads):
                    side = core if n < heads // 2 else 1 - core
                    column = side * (heads // 2) + n % (heads // 2)
                    out[there, aligned(column, HD)] = result[n * blk_rows : (n + 1) * blk_rows]


def pages_kernel(n_out, blk_rows, *refs):
    mine, other = refs[:n_out], refs[n_out : 2 * n_out]
    ids_ref, info_ref, own, away, store = refs[2 * n_out :]
    _, _, core = place()
    per_piece = mine[0].shape[0] // blk_rows
    for k in range(n_out):
        for j in range(per_piece):
            there = aligned(ids_ref[k * per_piece + j], blk_rows)
            here = slice(j * blk_rows, (j + 1) * blk_rows)
            store[core, there, :] = mine[k][here, :]
            store[1 - core, there, :] = other[k][here, :]
    slots = own.shape[0]
    row = lax.broadcasted_iota(jnp.int32, (blk_rows, HD), 0)
    for target, base in ((away, slots), (own, 0)):
        for i in range(slots):
            here = aligned(info_ref[1, base + i], blk_rows)
            live = row < info_ref[2, base + i]
            for half in range(2):
                page = store[half, here, :]
                target[i, :, half * HD : (half + 1) * HD] = jnp.where(live, page, jnp.zeros_like(page))


def finish_kernel(kept, from_far, own_pages, got_pages, info_ref, att_out, page_out, sems):
    _, pair, _ = place()
    width = kept.shape[1]
    copies = [
        pltpu.make_async_copy(kept, att_out.at[:, aligned(pair, width)], sems.at[0]),
        pltpu.make_async_copy(from_far, att_out.at[:, aligned(1 - pair, width)], sems.at[1]),
    ]
    for copy in copies:
        copy.start()
    for i in range(page_out.shape[0]):
        here = info_ref[0, i] == pair
        ours = pltpu.make_async_copy(own_pages.at[i], page_out.at[i], sems.at[2 + i])
        theirs = pltpu.make_async_copy(got_pages.at[i], page_out.at[i], sems.at[2 + i])
        copies.append(ours)

        @pl.when(here)
        def _():
            ours.start()

        @pl.when(jnp.logical_not(here))
        def _():
            theirs.start()

    for copy in copies:
        copy.wait()


def body(tokens, block_ids, lengths, page_table, qkv_weight, q_gain, k_gain):
    n_req, n_blk = lax.axis_size("req"), lax.axis_size("blk")
    n_out = n_blk // TEAM
    bf16 = jnp.bfloat16
    shape = jax.ShapeDtypeStruct
    blk = lax.axis_index("blk")
    member = blk % TEAM

    def in_team(array, k):
        return lax.ppermute(array, "blk", [(i, i ^ k) for i in range(n_blk)])

    def in_req(array, k):
        return lax.ppermute(array, "req", [(i, i ^ k) for i in range(n_req)])

    def across(array, k):
        return lax.ppermute(array, "blk", [(i, (i + TEAM * k) % n_blk) for i in range(n_blk)])

    def sync(*arrays):
        return lax.optimization_barrier(arrays)

    w_rows = qkv_weight.shape[0]
    per_device = block_ids.shape[1]
    own = tokens[0]
    rows = own.shape[0]
    packed_rows = 3 * HD // LANES * w_rows + ID_ROWS
    parts = pl.pallas_call(
        pack_kernel,
        out_shape=[
            shape((packed_rows + (own.size // LANES if k == 1 else 0), LANES), bf16) for k in range(TEAM)
        ],
        in_specs=[pl.BlockSpec(memory_space=pltpu.HBM)] * 3,
        out_specs=[VMEM] * TEAM,
        scratch_shapes=[
            pltpu.VMEM(qkv_weight.shape, bf16),
            pltpu.SMEM(block_ids.shape, jnp.int32),
            pltpu.VMEM(own.shape, bf16),
            pltpu.SemaphoreType.DMA((3,)),
        ],
        compiler_params=params(4),
        name="pack",
    )(qkv_weight, block_ids, own)
    got = [parts[0]] + [in_team(parts[k], k) for k in range(1, TEAM)]
    kv, q, w = pl.pallas_call(
        team_kernel,
        out_shape=[
            shape((TEAM * w_rows + ID_ROWS, HD), bf16),
            shape((TEAM * w_rows, 2 * HD), bf16),
            shape((TEAM * w_rows, 3 * HD), bf16),
        ],
        in_specs=[VMEM] * TEAM,
        out_specs=[VMEM] * 3,
        compiler_params=params(2),
        name="team",
    )(*got)

    def from_others(piece):
        got = [across(piece, k) for k in range(1, n_out)]
        return got[0] if len(got) == 1 else jnp.concatenate(got, 0)

    kv, q, w, own = sync(kv, q, w, own)
    kv_o, w_x, w_y = from_others(kv), in_req(w, 1), in_req(w, 2)
    q_o, far = from_others(q), in_team(own, 2)
    kv_o, w_x, w_y = sync(kv_o, w_x, w_y)
    kv_ox, kv_oy, w_d = in_req(kv_o, 1), in_req(kv_o, 2), in_req(w_x, 2)
    kv_ox, kv_oy = sync(kv_ox, kv_oy)
    kv_od = in_req(kv_oy, 1)
    kv_od, w_d, q_o, far = sync(kv_od, w_d, q_o, far)
    far_near = in_team(far, 1)
    q_o, far_near = sync(q_o, far_near)
    q_ox, q_oy = in_req(q_o, 1), in_req(q_o, 2)
    kv_weight = [w, kv_o, w_x, kv_ox, w_y, kv_oy, w_d, kv_od]
    stacked = pl.pallas_call(
        functools.partial(stack_kernel, packed_rows),
        out_shape=shape((TEAM * rows, own.shape[1]), bf16),
        in_specs=[VMEM] * TEAM,
        out_specs=VMEM,
        compiler_params=params(2),
        name="stack",
    )(own, got[1], far, far_near)

    blk_rows = rows // per_device
    tall = kv.shape[0]
    team_ids = kv[tall - ID_ROWS, : TEAM * per_device][None].astype(jnp.int32)
    other_ids = kv_o.reshape(n_out - 1, tall, HD)[:, tall - ID_ROWS, : TEAM * per_device].astype(jnp.int32)
    all_ids = jnp.concatenate([team_ids, other_ids], 0).reshape(-1)

    offsets = jnp.arange(blk_rows, dtype=jnp.int32)
    positions = (team_ids[0][:, None] * blk_rows + offsets[None, :]).reshape(-1, 1)
    inverse = jnp.power(jnp.float32(ROPE_BASE), -2.0 * jnp.arange(HD // 2).astype(jnp.float32) / HD)
    angles = positions.astype(jnp.float32) * inverse[None, :]
    cosine, sine = jnp.cos(angles), jnp.sin(angles)

    def project(weight, is_kv, gain):
        width = weight[1].shape[1]
        depth = own.shape[1]
        n_outs = 1 if is_kv else 2
        return pl.pallas_call(
            functools.partial(project_kernel, n_out, TEAM * w_rows, is_kv),
            out_shape=[shape((TEAM * rows // n_outs, width), bf16)] * n_outs,
            in_specs=[VMEM] * (4 + len(weight)),
            out_specs=[VMEM] * n_outs,
            scratch_shapes=[
                pltpu.VMEM((depth, width) if w_rows * TEAM % LANES else (ID_ROWS, LANES), bf16),
                pltpu.SemaphoreType.DMA((n_req * n_out,)),
            ],
            cost_estimate=pl.CostEstimate(
                flops=2 * TEAM * rows * depth * width, bytes_accessed=6 * MIB, transcendentals=0
            ),
            compiler_params=params(4 if w_rows * TEAM % LANES == 0 else 12),
            name="project_kv" if is_kv else "project_q",
        )(stacked, *weight, gain[None, :], cosine, sine)

    (made,) = project(kv_weight, True, k_gain)
    q_ox, q_oy = sync(q_ox, q_oy)
    q_od = in_req(q_oy, 1)
    q_weight = [w, q_o, w_x, q_ox, w_y, q_oy, w_d, q_od]
    mine = [made] + [across(made, k) for k in range(1, n_out)]
    other = [in_team(part, 1) for part in mine]

    to_near, queries = project(q_weight, False, q_gain)
    from_near = in_team(to_near, 1)

    table = page_table[0].reshape(-1)
    per_head = page_table.shape[2]
    slot_count = page_table.shape[1] * per_head // n_blk
    wanted = jnp.concatenate(
        [b * slot_count + jnp.arange(slot_count, dtype=jnp.int32) for b in (blk, blk ^ 2)]
    )
    flat = jnp.sum(
        jnp.where(wanted[:, None] == table[None, :], jnp.arange(table.shape[0], dtype=jnp.int32)[None, :], 0), 1
    )
    block = flat % per_head
    info = jnp.stack([flat // per_head, block, lengths[0] - block * blk_rows])

    total = TEAM * rows * n_out
    store_mib = -(-2 * total * HD * 2 // MIB)
    page_shape = shape((slot_count, blk_rows, 2 * HD), bf16)
    own_pages, away_pages, store = pl.pallas_call(
        functools.partial(pages_kernel, n_out, blk_rows),
        out_shape=[page_shape, page_shape, shape((2, total, HD), bf16)],
        in_specs=[VMEM] * (2 * n_out) + [SMEM] * 2,
        out_specs=[VMEM] * 3,
        cost_estimate=pl.CostEstimate(flops=0, bytes_accessed=4 * MIB, transcendentals=0),
        compiler_params=params(store_mib + 1),
        name="pages",
    )(*mine, *other, all_ids, info)
    got_pages = in_team(away_pages, 2)

    def attend(step):
        return pl.pallas_call(
            functools.partial(attend_kernel, blk_rows, step),
            out_shape=shape((rows, H // 2 * HD), bf16),
            in_specs=[VMEM] * 3 + [SMEM] * 2,
            out_specs=VMEM,
            cost_estimate=pl.CostEstimate(
                flops=2 * H * HD * rows * total, bytes_accessed=4 * MIB, transcendentals=0
            ),
            compiler_params=params(store_mib + 2 + 3 * total // 1024),
            name="attend",
        )(store, queries, from_near, all_ids, lengths)

    from_far = in_team(attend(2), 2)
    kept = attend(0)

    attended, pages = pl.pallas_call(
        finish_kernel,
        out_shape=[shape((rows, H * HD), bf16), page_shape],
        in_specs=[ANY] * 4 + [SMEM],
        out_specs=[ANY] * 2,
        scratch_shapes=[pltpu.SemaphoreType.DMA((2 + slot_count,))],
        compiler_params=params(1),
        name="finish",
    )(kept, from_far, own_pages, got_pages, info)
    return attended[None], pages[None]


def solution(mesh):
    in_specs = (
        P("req", "blk", None),
        P("req", "blk"),
        P("req"),
        P("req", None, None),
        P(("req", "blk"), None),
        P(),
        P(),
    )
    out_specs = (P("req", "blk", None), P("req", "blk", None, None))
    return jax.shard_map(body, mesh=mesh, in_specs=in_specs, out_specs=out_specs, check_vma=False)
```

```python
import functools

import jax
import jax.numpy as jnp
from jax import lax
from jax.experimental import pallas as pl
from jax.experimental.pallas import tpu as pltpu
from jax.sharding import PartitionSpec as P

H = 8
KVH = 2
HD = 256
TEAM = 4
ID_ROWS = 16
LANES = 128
ROPE_BASE = 1000000.0
NORM_EPS = 1e-06
MIB = 1024 * 1024

ANY = pl.BlockSpec(memory_space=pl.ANY)
VMEM = pl.BlockSpec(memory_space=pltpu.VMEM)
SMEM = pl.BlockSpec(memory_space=pltpu.SMEM)


def params(mib):
    return pltpu.CompilerParams(vmem_limit_bytes=mib * MIB)


def place():
    blk = lax.axis_index("blk")
    return lax.axis_index("req"), (blk // 2) % 2, blk % 2


def run(copies):
    for copy in copies:
        copy.start()
    for copy in copies:
        copy.wait()


def aligned(index, size):
    return pl.ds(pl.multiple_of(index * size, size), size)


def q_start(pair, core):
    return pl.multiple_of((pair * 2 + core) * 2 * HD, 2 * HD)


def kv_start(pair, core):
    return pl.multiple_of(H * HD + core * KVH * HD + pair * HD, HD)


def pack_kernel(w_hbm, ids_hbm, tokens_hbm, *refs):
    outs, (w_ref, ids_ref, tokens_ref, sems) = refs[:TEAM], refs[TEAM:]
    run([
        pltpu.make_async_copy(source, there, sems.at[n])
        for n, (source, there) in enumerate(((w_hbm, w_ref), (ids_hbm, ids_ref), (tokens_hbm, tokens_ref)))
    ])
    _, pair, core = place()
    member = pair * 2 + core
    rows = w_ref.shape[0]
    per_device = ids_ref.shape[1]
    lane = lax.broadcasted_iota(jnp.int32, (ID_ROWS, LANES), 1) - member * per_device
    ids = jnp.zeros((ID_ROWS, LANES), jnp.int32)
    for j in range(per_device):
        ids = jnp.where(lane == j, ids_ref[0, j], ids)
    ids = ids.astype(jnp.float32).astype(jnp.bfloat16)
    blocks = 3 * HD // LANES
    for k in range(TEAM):
        to_pair, to_core = pair ^ (k // 2), core ^ (k % 2)
        for n in range(blocks):
            if n < HD // LANES:
                start = pl.multiple_of(kv_start(to_pair, to_core) + n * LANES, LANES)
            else:
                start = pl.multiple_of(q_start(to_pair, to_core) + n * LANES - HD, LANES)
            outs[k][n * rows : (n + 1) * rows, :] = w_ref[:, pl.ds(start, LANES)]
        outs[k][blocks * rows : blocks * rows + ID_ROWS, :] = ids
    token_rows = tokens_ref.shape[0]
    for n in range(tokens_ref.shape[1] // LANES):
        first = blocks * rows + ID_ROWS + n * token_rows
        outs[1][first : first + token_rows, :] = tokens_ref[:, n * LANES : (n + 1) * LANES]


def team_kernel(*refs):
    _, pair, core = place()
    parts, (kv_out, q_out, whole) = refs[:TEAM], refs[TEAM:]
    rows = q_out.shape[0] // TEAM
    member = pair * 2 + core
    for k in range(TEAM):
        here = aligned(member ^ k, rows)
        for n in range(3 * HD // LANES):
            out = kv_out if n < HD // LANES else q_out
            first = n * LANES if n < HD // LANES else n * LANES - HD
            part = parts[k][n * rows : (n + 1) * rows, :]
            out[here, first : first + LANES] = part
            whole[here, n * LANES : (n + 1) * LANES] = part
    first = 3 * HD // LANES * rows
    below = [part[first : first + ID_ROWS, :].astype(jnp.float32) for part in parts]
    ids = sum(below[1:], below[0]).astype(jnp.bfloat16)
    kv_out[TEAM * rows :, :] = jnp.concatenate([ids] * (HD // LANES), 1)


def cut_kernel(whole, kv_out, q_out):
    kv_out[...] = whole[:, :HD]
    q_out[...] = whole[:, HD:]


def project_kernel(n_out, depth, first_row, is_kv, own, near, far, far_near, *refs):
    n_outs = 1 if is_kv else 2
    weights, (gain_ref, cos_ref, sin_ref) = refs[: -5 - n_outs], refs[-5 - n_outs : -2 - n_outs]
    outs, (w_all, sems) = refs[-2 - n_outs : -2], refs[-2:]
    req = lax.axis_index("req")
    outer = lax.axis_index("blk") // TEAM
    _, pair, core = place()
    member = pair * 2 + core
    rows = own.shape[0]
    width = outs[0].shape[1]
    direct = depth % LANES == 0
    places = []
    for i, piece in enumerate(weights):
        from_req = req ^ (i // 2)
        tall = piece.shape[0] // (n_out - 1 if i % 2 else 1)
        for n in range(n_out - 1 if i % 2 else 1):
            from_outer = lax.rem(outer + n_out - n - i % 2, n_out)
            cols = slice(None) if piece.shape[1] == width else slice(*((0, HD) if is_kv else (HD, 3 * HD)))
            places.append((piece.at[pl.ds(n * tall, depth), cols], from_req * n_out + from_outer))
    if not direct:
        run([
            pltpu.make_async_copy(piece, w_all.at[aligned(index, depth), :], sems.at[n])
            for n, (piece, index) in enumerate(places)
        ])
    half = HD // 2
    gain = gain_ref[...]
    if is_kv:
        gain = jnp.where(core == 0, gain, 1.0)
    for out, steps in zip(outs, [(0, 1, 2, 3)] if is_kv else [(1, 3), (0, 2)]):

        def token_rows(k, start, size):
            if k != 1:
                return (own, None, far, far_near)[k][:, pl.ds(start, size)]
            blocks = []
            for n in range(size // LANES):
                first = pl.multiple_of(first_row + (start // LANES + n) * rows, 16)
                blocks.append(near[pl.ds(first, rows), :])
            return jnp.concatenate(blocks, 1)

        def team_rows(start, size):
            return jnp.concatenate([token_rows(k, start, size) for k in steps], 0)

        cosine, sine = (
            jnp.concatenate([ref[aligned(member ^ k, rows), :] for k in steps], 0) for ref in (cos_ref, sin_ref)
        )
        if is_kv:
            cosine = jnp.where(core == 0, cosine, 1.0)
            sine = jnp.where(core == 0, sine, 0.0)
        if direct:
            product = 0.0
            for piece, index in places:
                x = team_rows(pl.multiple_of(index * depth, depth), depth)
                product += jnp.dot(x, piece[...], preferred_element_type=jnp.float32)
        else:
            product = jnp.dot(team_rows(0, w_all.shape[0]), w_all[...], preferred_element_type=jnp.float32)
        for h in range(out.shape[1] // HD):
            head = product[:, h * HD : (h + 1) * HD]
            mean = jnp.mean(head * head, axis=-1, keepdims=True)
            head = head * lax.rsqrt(mean + NORM_EPS) * gain
            front, second = head[:, :half], head[:, half:]
            turned = jnp.concatenate([front * cosine - second * sine, second * cosine + front * sine], 1)
            turned = turned.astype(jnp.bfloat16)
            for n, k in enumerate(steps):
                there = aligned(member ^ k if is_kv else n, rows)
                out[there, h * HD : (h + 1) * HD] = turned[n * rows : (n + 1) * rows]


def attend_kernel(blk_rows, step, store, q_ref, near_ref, ids_ref, length_ref, out):
    _, pair, core = place()
    length = length_ref[0]
    rows = out.shape[0]
    member = (pair * 2 + core) ^ step
    total = store.shape[1]
    quarter = total // 4
    heads = 2 * (out.shape[1] // (2 * HD))
    first = step // 2 * rows
    for j in range(rows // blk_rows):
        block = ids_ref[member * (rows // blk_rows) + j]
        here = slice(first + j * blk_rows, first + (j + 1) * blk_rows)
        there = slice(j * blk_rows, (j + 1) * blk_rows)
        for variant in range(4):
            seen = (variant + 1) * quarter

            @pl.when((block * blk_rows) // quarter == variant)
            def _():
                queries = jnp.concatenate(
                    [ref[here, h * HD : (h + 1) * HD] for ref in (q_ref, near_ref) for h in range(heads // 2)], 0
                )
                shape = (heads * blk_rows, 1)
                query_pos = block * blk_rows + lax.rem(lax.broadcasted_iota(jnp.int32, shape, 0), blk_rows)
                limit = jnp.minimum(query_pos, length - 1)
                key_pos = lax.broadcasted_iota(jnp.int32, (1, seen), 1)
                scores = lax.dot_general(
                    queries,
                    store[0, :seen, :],
                    (((1,), (1,)), ((), ())),
                    preferred_element_type=jnp.float32,
                )
                scores = jnp.where(key_pos <= limit, scores, jnp.finfo(jnp.float32).min)
                weights = jnp.exp(scores - jnp.max(scores, axis=-1, keepdims=True))
                row_sum = jnp.sum(weights, axis=-1, keepdims=True)
                summed = jnp.dot(
                    weights.astype(jnp.bfloat16), store[1, :seen, :], preferred_element_type=jnp.float32
                )
                result = jnp.where(query_pos < length, summed / row_sum, 0.0).astype(jnp.bfloat16)
                for n in range(heads):
                    side = core if n < heads // 2 else 1 - core
                    column = side * (heads // 2) + n % (heads // 2)
                    out[there, aligned(column, HD)] = result[n * blk_rows : (n + 1) * blk_rows]


def pages_kernel(n_out, blk_rows, *refs):
    mine, other = refs[:n_out], refs[n_out : 2 * n_out]
    ids_ref, info_ref, own, away, store = refs[2 * n_out :]
    _, _, core = place()
    per_piece = mine[0].shape[0] // blk_rows
    for k in range(n_out):
        for j in range(per_piece):
            there = aligned(ids_ref[k * per_piece + j], blk_rows)
            here = slice(j * blk_rows, (j + 1) * blk_rows)
            store[core, there, :] = mine[k][here, :]
            store[1 - core, there, :] = other[k][here, :]
    slots = own.shape[0]
    row = lax.broadcasted_iota(jnp.int32, (blk_rows, HD), 0)
    for target, base in ((away, slots), (own, 0)):
        for i in range(slots):
            here = aligned(info_ref[1, base + i], blk_rows)
            live = row < info_ref[2, base + i]
            for half in range(2):
                page = store[half, here, :]
                target[i, :, half * HD : (half + 1) * HD] = jnp.where(live, page, jnp.zeros_like(page))


def finish_kernel(kept, from_far, own_pages, got_pages, info_ref, att_out, page_out, sems):
    _, pair, _ = place()
    width = kept.shape[1]
    copies = [
        pltpu.make_async_copy(kept, att_out.at[:, aligned(pair, width)], sems.at[0]),
        pltpu.make_async_copy(from_far, att_out.at[:, aligned(1 - pair, width)], sems.at[1]),
    ]
    for copy in copies:
        copy.start()
    for i in range(page_out.shape[0]):
        here = info_ref[0, i] == pair
        ours = pltpu.make_async_copy(own_pages.at[i], page_out.at[i], sems.at[2 + i])
        theirs = pltpu.make_async_copy(got_pages.at[i], page_out.at[i], sems.at[2 + i])
        copies.append(ours)

        @pl.when(here)
        def _():
            ours.start()

        @pl.when(jnp.logical_not(here))
        def _():
            theirs.start()

    for copy in copies:
        copy.wait()


def body(tokens, block_ids, lengths, page_table, qkv_weight, q_gain, k_gain):
    n_req, n_blk = lax.axis_size("req"), lax.axis_size("blk")
    n_out = n_blk // TEAM
    bf16 = jnp.bfloat16
    shape = jax.ShapeDtypeStruct
    blk = lax.axis_index("blk")
    member = blk % TEAM

    def in_team(array, k):
        return lax.ppermute(array, "blk", [(i, i ^ k) for i in range(n_blk)])

    def in_req(array, k):
        return lax.ppermute(array, "req", [(i, i ^ k) for i in range(n_req)])

    def across(array, k):
        return lax.ppermute(array, "blk", [(i, (i + TEAM * k) % n_blk) for i in range(n_blk)])

    def sync(*arrays):
        return lax.optimization_barrier(arrays)

    w_rows = qkv_weight.shape[0]
    per_device = block_ids.shape[1]
    own = tokens[0]
    rows = own.shape[0]
    packed_rows = 3 * HD // LANES * w_rows + ID_ROWS
    parts = pl.pallas_call(
        pack_kernel,
        out_shape=[
            shape((packed_rows + (own.size // LANES if k == 1 else 0), LANES), bf16) for k in range(TEAM)
        ],
        in_specs=[pl.BlockSpec(memory_space=pltpu.HBM)] * 3,
        out_specs=[VMEM] * TEAM,
        scratch_shapes=[
            pltpu.VMEM(qkv_weight.shape, bf16),
            pltpu.SMEM(block_ids.shape, jnp.int32),
            pltpu.VMEM(own.shape, bf16),
            pltpu.SemaphoreType.DMA((3,)),
        ],
        compiler_params=params(56),
        name="pack",
    )(qkv_weight, block_ids, own)
    got = [parts[0]] + [in_team(parts[k], k) for k in range(1, TEAM)]
    kv, q, w = pl.pallas_call(
        team_kernel,
        out_shape=[
            shape((TEAM * w_rows + ID_ROWS, HD), bf16),
            shape((TEAM * w_rows, 2 * HD), bf16),
            shape((TEAM * w_rows, 3 * HD), bf16),
        ],
        in_specs=[VMEM] * TEAM,
        out_specs=[VMEM] * 3,
        compiler_params=params(2),
        name="team",
    )(*got)

    def from_others(piece):
        got = [across(piece, k) for k in range(1, n_out)]
        return got[0] if len(got) == 1 else jnp.concatenate(got, 0)

    kv, q, w, own = sync(kv, q, w, own)
    kv_o, w_x, w_y = from_others(kv), in_req(w, 1), in_req(w, 2)
    q_o, far = from_others(q), in_team(own, 2)

    blk_rows = rows // per_device
    tall = kv.shape[0]
    team_ids = kv[tall - ID_ROWS, : TEAM * per_device][None].astype(jnp.int32)
    other_ids = kv_o.reshape(n_out - 1, tall, HD)[:, tall - ID_ROWS, : TEAM * per_device].astype(jnp.int32)
    all_ids = jnp.concatenate([team_ids, other_ids], 0).reshape(-1)

    offsets = jnp.arange(blk_rows, dtype=jnp.int32)
    positions = (team_ids[0][:, None] * blk_rows + offsets[None, :]).reshape(-1, 1)
    inverse = jnp.power(jnp.float32(ROPE_BASE), -2.0 * jnp.arange(HD // 2).astype(jnp.float32) / HD)
    angles = positions.astype(jnp.float32) * inverse[None, :]
    cosine, sine = jnp.cos(angles), jnp.sin(angles)

    table = page_table[0].reshape(-1)
    per_head = page_table.shape[2]
    slot_count = page_table.shape[1] * per_head // n_blk
    wanted = jnp.concatenate(
        [b * slot_count + jnp.arange(slot_count, dtype=jnp.int32) for b in (blk, blk ^ 2)]
    )
    flat = jnp.sum(
        jnp.where(wanted[:, None] == table[None, :], jnp.arange(table.shape[0], dtype=jnp.int32)[None, :], 0), 1
    )
    block = flat % per_head
    info = jnp.stack([flat // per_head, block, lengths[0] - block * blk_rows])

    kv_o, w_x, w_y = sync(kv_o, w_x, w_y)
    kv_x, q_x = pl.pallas_call(
        cut_kernel,
        out_shape=[shape((w_x.shape[0], HD), bf16), shape((w_x.shape[0], 2 * HD), bf16)],
        in_specs=[VMEM],
        out_specs=[VMEM] * 2,
        compiler_params=params(1),
        name="cut",
    )(w_x)
    kv_ox, kv_oy, kv_d = in_req(kv_o, 1), in_req(kv_o, 2), in_req(kv_x, 2)
    kv_ox, kv_oy, kv_d, q_o, far, cosine, sine, all_ids, info = sync(
        kv_ox, kv_oy, kv_d, q_o, far, cosine, sine, all_ids, info
    )
    kv_od, far_near = in_req(kv_oy, 1), in_team(far, 1)
    kv_od, far_near, q_o = sync(kv_od, far_near, q_o)
    q_ox, q_oy = in_req(q_o, 1), in_req(q_o, 2)
    kv_weight = [kv, kv_o, w_x, kv_ox, w_y, kv_oy, kv_d, kv_od]

    def project(weight, is_kv, gain):
        width = weight[1].shape[1]
        depth = own.shape[1]
        n_outs = 1 if is_kv else 2
        return pl.pallas_call(
            functools.partial(project_kernel, n_out, TEAM * w_rows, packed_rows, is_kv),
            out_shape=[shape((TEAM * rows // n_outs, width), bf16)] * n_outs,
            in_specs=[VMEM] * (7 + len(weight)),
            out_specs=[VMEM] * n_outs,
            scratch_shapes=[
                pltpu.VMEM((depth, width) if w_rows * TEAM % LANES else (ID_ROWS, LANES), bf16),
                pltpu.SemaphoreType.DMA((n_req * n_out,)),
            ],
            cost_estimate=pl.CostEstimate(
                flops=2 * TEAM * rows * depth * width, bytes_accessed=6 * MIB, transcendentals=0
            ),
            compiler_params=params(4 if w_rows * TEAM % LANES == 0 else 12),
            name="project_kv" if is_kv else "project_q",
        )(own, got[1], far, far_near, *weight, gain[None, :], cosine, sine)

    (made,) = project(kv_weight, True, k_gain)
    q_ox, q_oy, q_x = sync(q_ox, q_oy, q_x)
    q_od, q_d = in_req(q_oy, 1), in_req(q_x, 2)
    q_weight = [q, q_o, w_x, q_ox, w_y, q_oy, q_d, q_od]
    mine = [made] + [across(made, k) for k in range(1, n_out)]
    other = [in_team(part, 1) for part in mine]

    to_near, queries = project(q_weight, False, q_gain)
    from_near = in_team(to_near, 1)

    total = TEAM * rows * n_out
    store_mib = -(-2 * total * HD * 2 // MIB)
    page_shape = shape((slot_count, blk_rows, 2 * HD), bf16)
    own_pages, away_pages, store = pl.pallas_call(
        functools.partial(pages_kernel, n_out, blk_rows),
        out_shape=[page_shape, page_shape, shape((2, total, HD), bf16)],
        in_specs=[VMEM] * (2 * n_out) + [SMEM] * 2,
        out_specs=[VMEM] * 3,
        cost_estimate=pl.CostEstimate(flops=0, bytes_accessed=4 * MIB, transcendentals=0),
        compiler_params=params(store_mib + 1),
        name="pages",
    )(*mine, *other, all_ids, info)
    got_pages = in_team(away_pages, 2)

    def attend(step):
        return pl.pallas_call(
            functools.partial(attend_kernel, blk_rows, step),
            out_shape=shape((rows, H // 2 * HD), bf16),
            in_specs=[VMEM] * 3 + [SMEM] * 2,
            out_specs=VMEM,
            cost_estimate=pl.CostEstimate(
                flops=2 * H * HD * rows * total, bytes_accessed=4 * MIB, transcendentals=0
            ),
            compiler_params=params(store_mib + 2 + 3 * total // 1024),
            name="attend",
        )(store, queries, from_near, all_ids, lengths)

    from_far = in_team(attend(2), 2)
    kept = attend(0)

    attended, pages = pl.pallas_call(
        finish_kernel,
        out_shape=[shape((rows, H * HD), bf16), page_shape],
        in_specs=[ANY] * 4 + [SMEM],
        out_specs=[ANY] * 2,
        scratch_shapes=[pltpu.SemaphoreType.DMA((2 + slot_count,))],
        compiler_params=params(1),
        name="finish",
    )(kept, from_far, own_pages, got_pages, info)
    return attended[None], pages[None]


def solution(mesh):
    in_specs = (
        P("req", "blk", None),
        P("req", "blk"),
        P("req"),
        P("req", None, None),
        P(("req", "blk"), None),
        P(),
        P(),
    )
    out_specs = (P("req", "blk", None), P("req", "blk", None, None))
    return jax.shard_map(body, mesh=mesh, in_specs=in_specs, out_specs=out_specs, check_vma=False)
```

```python
import functools

import jax
import jax.numpy as jnp
from jax import lax
from jax.experimental import pallas as pl
from jax.experimental.pallas import tpu as pltpu
from jax.sharding import PartitionSpec as P

H = 8
KVH = 2
HD = 256
TEAM = 4
ID_ROWS = 16
LANES = 128
ROPE_BASE = 1000000.0
NORM_EPS = 1e-06
MIB = 1024 * 1024

ANY = pl.BlockSpec(memory_space=pl.ANY)
VMEM = pl.BlockSpec(memory_space=pltpu.VMEM)
SMEM = pl.BlockSpec(memory_space=pltpu.SMEM)


def params(mib):
    return pltpu.CompilerParams(vmem_limit_bytes=mib * MIB)


def place():
    blk = lax.axis_index("blk")
    return lax.axis_index("req"), (blk // 2) % 2, blk % 2


def run(copies):
    for copy in copies:
        copy.start()
    for copy in copies:
        copy.wait()


def aligned(index, size):
    return pl.ds(pl.multiple_of(index * size, size), size)


def q_start(pair, core):
    return pl.multiple_of((pair * 2 + core) * 2 * HD, 2 * HD)


def kv_start(pair, core):
    return pl.multiple_of(H * HD + core * KVH * HD + pair * HD, HD)


def pack_kernel(w_hbm, ids_hbm, tokens_hbm, *refs):
    outs, (w_ref, ids_ref, tokens_ref, sems) = refs[:TEAM], refs[TEAM:]
    run([
        pltpu.make_async_copy(source, there, sems.at[n])
        for n, (source, there) in enumerate(((w_hbm, w_ref), (ids_hbm, ids_ref), (tokens_hbm, tokens_ref)))
    ])
    _, pair, core = place()
    member = pair * 2 + core
    rows = w_ref.shape[0]
    per_device = ids_ref.shape[1]
    lane = lax.broadcasted_iota(jnp.int32, (ID_ROWS, LANES), 1) - member * per_device
    ids = jnp.zeros((ID_ROWS, LANES), jnp.int32)
    for j in range(per_device):
        ids = jnp.where(lane == j, ids_ref[0, j], ids)
    ids = ids.astype(jnp.float32).astype(jnp.bfloat16)
    blocks = 3 * HD // LANES
    for k in range(TEAM):
        to_pair, to_core = pair ^ (k // 2), core ^ (k % 2)
        for n in range(blocks):
            if n < HD // LANES:
                start = pl.multiple_of(kv_start(to_pair, to_core) + n * LANES, LANES)
            else:
                start = pl.multiple_of(q_start(to_pair, to_core) + n * LANES - HD, LANES)
            outs[k][n * rows : (n + 1) * rows, :] = w_ref[:, pl.ds(start, LANES)]
        outs[k][blocks * rows : blocks * rows + ID_ROWS, :] = ids
    token_rows = tokens_ref.shape[0]
    for n in range(tokens_ref.shape[1] // LANES):
        first = blocks * rows + ID_ROWS + n * token_rows
        outs[1][first : first + token_rows, :] = tokens_ref[:, n * LANES : (n + 1) * LANES]


def team_kernel(*refs):
    _, pair, core = place()
    parts, (kv_out, q_out, whole) = refs[:TEAM], refs[TEAM:]
    rows = q_out.shape[0] // TEAM
    member = pair * 2 + core
    for k in range(TEAM):
        here = aligned(member ^ k, rows)
        for n in range(3 * HD // LANES):
            out = kv_out if n < HD // LANES else q_out
            first = n * LANES if n < HD // LANES else n * LANES - HD
            part = parts[k][n * rows : (n + 1) * rows, :]
            out[here, first : first + LANES] = part
            whole[here, n * LANES : (n + 1) * LANES] = part
    first = 3 * HD // LANES * rows
    below = [part[first : first + ID_ROWS, :].astype(jnp.float32) for part in parts]
    ids = sum(below[1:], below[0]).astype(jnp.bfloat16)
    kv_out[TEAM * rows :, :] = jnp.concatenate([ids] * (HD // LANES), 1)


def regroup_kernel(kv_o, w_x, kv_out, q_out):
    rows = kv_o.shape[0]
    kv_out[:rows, :] = kv_o[...]
    kv_out[rows:, :] = w_x[:, :HD]
    q_out[...] = w_x[:, HD:]


def project_kernel(n_out, depth, tall, starts, first_row, is_kv, own, near, far, far_near, *refs):
    n_outs = 1 if is_kv else 2
    weights, (gain_ref, cos_ref, sin_ref) = refs[: -5 - n_outs], refs[-5 - n_outs : -2 - n_outs]
    outs, (w_all, sems) = refs[-2 - n_outs : -2], refs[-2:]
    req = lax.axis_index("req")
    outer = lax.axis_index("blk") // TEAM
    _, pair, core = place()
    member = pair * 2 + core
    rows = own.shape[0]
    width = outs[0].shape[1]
    direct = depth % LANES == 0
    places = []
    for i, piece in enumerate(weights):
        from_req = req ^ (i // 2)
        for n in range(n_out - 1 if i % 2 else 1):
            from_outer = lax.rem(outer + n_out - n - i % 2, n_out)
            row, column = starts[i]
            part = piece.at[pl.ds(row + n * tall, depth), column : column + width]
            places.append((part, from_req * n_out + from_outer))
    if not direct:
        run([
            pltpu.make_async_copy(piece, w_all.at[aligned(index, depth), :], sems.at[n])
            for n, (piece, index) in enumerate(places)
        ])
    half = HD // 2
    gain = gain_ref[...]
    if is_kv:
        gain = jnp.where(core == 0, gain, 1.0)
    for out, steps in zip(outs, [(0, 1, 2, 3)] if is_kv else [(1, 3), (0, 2)]):

        def token_rows(k, start, size):
            if k != 1:
                return (own, None, far, far_near)[k][:, pl.ds(start, size)]
            blocks = []
            for n in range(size // LANES):
                first = pl.multiple_of(first_row + (start // LANES + n) * rows, 16)
                blocks.append(near[pl.ds(first, rows), :])
            return jnp.concatenate(blocks, 1)

        def team_rows(start, size):
            return jnp.concatenate([token_rows(k, start, size) for k in steps], 0)

        cosine, sine = (
            jnp.concatenate([ref[aligned(member ^ k, rows), :] for k in steps], 0) for ref in (cos_ref, sin_ref)
        )
        if is_kv:
            cosine = jnp.where(core == 0, cosine, 1.0)
            sine = jnp.where(core == 0, sine, 0.0)
        if direct:
            product = 0.0
            for piece, index in places:
                x = team_rows(pl.multiple_of(index * depth, depth), depth)
                product += jnp.dot(x, piece[...], preferred_element_type=jnp.float32)
        else:
            product = jnp.dot(team_rows(0, w_all.shape[0]), w_all[...], preferred_element_type=jnp.float32)
        for h in range(out.shape[1] // HD):
            head = product[:, h * HD : (h + 1) * HD]
            mean = jnp.mean(head * head, axis=-1, keepdims=True)
            head = head * lax.rsqrt(mean + NORM_EPS) * gain
            front, second = head[:, :half], head[:, half:]
            turned = jnp.concatenate([front * cosine - second * sine, second * cosine + front * sine], 1)
            turned = turned.astype(jnp.bfloat16)
            for n, k in enumerate(steps):
                there = aligned(member ^ k if is_kv else n, rows)
                out[there, h * HD : (h + 1) * HD] = turned[n * rows : (n + 1) * rows]


def attend_kernel(blk_rows, step, store, q_ref, near_ref, ids_ref, length_ref, out):
    _, pair, core = place()
    length = length_ref[0]
    rows = out.shape[0]
    member = (pair * 2 + core) ^ step
    total = store.shape[1]
    quarter = total // 4
    heads = 2 * (out.shape[1] // (2 * HD))
    first = step // 2 * rows
    for j in range(rows // blk_rows):
        block = ids_ref[member * (rows // blk_rows) + j]
        here = slice(first + j * blk_rows, first + (j + 1) * blk_rows)
        there = slice(j * blk_rows, (j + 1) * blk_rows)
        for variant in range(4):
            seen = (variant + 1) * quarter

            @pl.when((block * blk_rows) // quarter == variant)
            def _():
                queries = jnp.concatenate(
                    [ref[here, h * HD : (h + 1) * HD] for ref in (q_ref, near_ref) for h in range(heads // 2)], 0
                )
                shape = (heads * blk_rows, 1)
                query_pos = block * blk_rows + lax.rem(lax.broadcasted_iota(jnp.int32, shape, 0), blk_rows)
                limit = jnp.minimum(query_pos, length - 1)
                key_pos = lax.broadcasted_iota(jnp.int32, (1, seen), 1)
                scores = lax.dot_general(
                    queries,
                    store[0, :seen, :],
                    (((1,), (1,)), ((), ())),
                    preferred_element_type=jnp.float32,
                )
                scores = jnp.where(key_pos <= limit, scores, jnp.finfo(jnp.float32).min)
                weights = jnp.exp(scores - jnp.max(scores, axis=-1, keepdims=True))
                row_sum = jnp.sum(weights, axis=-1, keepdims=True)
                summed = jnp.dot(
                    weights.astype(jnp.bfloat16), store[1, :seen, :], preferred_element_type=jnp.float32
                )
                result = jnp.where(query_pos < length, summed / row_sum, 0.0).astype(jnp.bfloat16)
                for n in range(heads):
                    side = core if n < heads // 2 else 1 - core
                    column = side * (heads // 2) + n % (heads // 2)
                    out[there, aligned(column, HD)] = result[n * blk_rows : (n + 1) * blk_rows]


def pages_kernel(n_out, blk_rows, *refs):
    mine, other = refs[:n_out], refs[n_out : 2 * n_out]
    ids_ref, info_ref, own, away, store = refs[2 * n_out :]
    _, _, core = place()
    per_piece = mine[0].shape[0] // blk_rows
    for k in range(n_out):
        for j in range(per_piece):
            there = aligned(ids_ref[k * per_piece + j], blk_rows)
            here = slice(j * blk_rows, (j + 1) * blk_rows)
            store[core, there, :] = mine[k][here, :]
            store[1 - core, there, :] = other[k][here, :]
    slots = own.shape[0]
    row = lax.broadcasted_iota(jnp.int32, (blk_rows, HD), 0)
    for target, base in ((away, slots), (own, 0)):
        for i in range(slots):
            here = aligned(info_ref[1, base + i], blk_rows)
            live = row < info_ref[2, base + i]
            for half in range(2):
                page = store[half, here, :]
                target[i, :, half * HD : (half + 1) * HD] = jnp.where(live, page, jnp.zeros_like(page))


def finish_kernel(kept, from_far, own_pages, got_pages, info_ref, att_out, page_out, sems):
    _, pair, _ = place()
    width = kept.shape[1]
    copies = [
        pltpu.make_async_copy(kept, att_out.at[:, aligned(pair, width)], sems.at[0]),
        pltpu.make_async_copy(from_far, att_out.at[:, aligned(1 - pair, width)], sems.at[1]),
    ]
    for copy in copies:
        copy.start()
    for i in range(page_out.shape[0]):
        here = info_ref[0, i] == pair
        ours = pltpu.make_async_copy(own_pages.at[i], page_out.at[i], sems.at[2 + i])
        theirs = pltpu.make_async_copy(got_pages.at[i], page_out.at[i], sems.at[2 + i])
        copies.append(ours)

        @pl.when(here)
        def _():
            ours.start()

        @pl.when(jnp.logical_not(here))
        def _():
            theirs.start()

    for copy in copies:
        copy.wait()


def body(tokens, block_ids, lengths, page_table, qkv_weight, q_gain, k_gain):
    n_req, n_blk = lax.axis_size("req"), lax.axis_size("blk")
    n_out = n_blk // TEAM
    bf16 = jnp.bfloat16
    shape = jax.ShapeDtypeStruct
    blk = lax.axis_index("blk")
    member = blk % TEAM

    def in_team(array, k):
        return lax.ppermute(array, "blk", [(i, i ^ k) for i in range(n_blk)])

    def in_req(array, k):
        return lax.ppermute(array, "req", [(i, i ^ k) for i in range(n_req)])

    def across(array, k):
        return lax.ppermute(array, "blk", [(i, (i + TEAM * k) % n_blk) for i in range(n_blk)])

    def sync(*arrays):
        return lax.optimization_barrier(arrays)

    w_rows = qkv_weight.shape[0]
    per_device = block_ids.shape[1]
    own = tokens[0]
    rows = own.shape[0]
    packed_rows = 3 * HD // LANES * w_rows + ID_ROWS
    parts = pl.pallas_call(
        pack_kernel,
        out_shape=[
            shape((packed_rows + (own.size // LANES if k == 1 else 0), LANES), bf16) for k in range(TEAM)
        ],
        in_specs=[pl.BlockSpec(memory_space=pltpu.HBM)] * 3,
        out_specs=[VMEM] * TEAM,
        scratch_shapes=[
            pltpu.VMEM(qkv_weight.shape, bf16),
            pltpu.SMEM(block_ids.shape, jnp.int32),
            pltpu.VMEM(own.shape, bf16),
            pltpu.SemaphoreType.DMA((3,)),
        ],
        compiler_params=params(56),
        name="pack",
    )(qkv_weight, block_ids, own)
    got = [parts[0]] + [in_team(parts[k], k) for k in range(1, TEAM)]
    kv, q, w = pl.pallas_call(
        team_kernel,
        out_shape=[
            shape((TEAM * w_rows + ID_ROWS, HD), bf16),
            shape((TEAM * w_rows, 2 * HD), bf16),
            shape((TEAM * w_rows, 3 * HD), bf16),
        ],
        in_specs=[VMEM] * TEAM,
        out_specs=[VMEM] * 3,
        compiler_params=params(2),
        name="team",
    )(*got)

    def from_others(piece):
        got = [across(piece, k) for k in range(1, n_out)]
        return got[0] if len(got) == 1 else jnp.concatenate(got, 0)

    kv, q, w, own = sync(kv, q, w, own)
    kv_o, w_x, w_y = from_others(kv), in_req(w, 1), in_req(w, 2)
    q_o, far = from_others(q), in_team(own, 2)

    blk_rows = rows // per_device
    tall = kv.shape[0]
    team_ids = kv[tall - ID_ROWS, : TEAM * per_device][None].astype(jnp.int32)
    other_ids = kv_o.reshape(n_out - 1, tall, HD)[:, tall - ID_ROWS, : TEAM * per_device].astype(jnp.int32)
    all_ids = jnp.concatenate([team_ids, other_ids], 0).reshape(-1)

    offsets = jnp.arange(blk_rows, dtype=jnp.int32)
    positions = (team_ids[0][:, None] * blk_rows + offsets[None, :]).reshape(-1, 1)
    inverse = jnp.power(jnp.float32(ROPE_BASE), -2.0 * jnp.arange(HD // 2).astype(jnp.float32) / HD)
    angles = positions.astype(jnp.float32) * inverse[None, :]
    cosine, sine = jnp.cos(angles), jnp.sin(angles)

    table = page_table[0].reshape(-1)
    per_head = page_table.shape[2]
    slot_count = page_table.shape[1] * per_head // n_blk
    wanted = jnp.concatenate(
        [b * slot_count + jnp.arange(slot_count, dtype=jnp.int32) for b in (blk, blk ^ 2)]
    )
    flat = jnp.sum(
        jnp.where(wanted[:, None] == table[None, :], jnp.arange(table.shape[0], dtype=jnp.int32)[None, :], 0), 1
    )
    block = flat % per_head
    info = jnp.stack([flat // per_head, block, lengths[0] - block * blk_rows])

    kv_o, w_x, w_y = sync(kv_o, w_x, w_y)
    others = kv_o.shape[0]
    kv_o_x, q_x = pl.pallas_call(
        regroup_kernel,
        out_shape=[shape((others + w_x.shape[0], HD), bf16), shape((w_x.shape[0], 2 * HD), bf16)],
        in_specs=[VMEM] * 2,
        out_specs=[VMEM] * 2,
        compiler_params=params(1),
        name="regroup",
    )(kv_o, w_x)
    kv_ox, kv_oy_d, kv_od = in_req(kv_o, 1), in_req(kv_o_x, 2), in_req(kv_o, 3)
    kv_ox, kv_oy_d, kv_od, q_o, far, cosine, sine, all_ids, info = sync(
        kv_ox, kv_oy_d, kv_od, q_o, far, cosine, sine, all_ids, info
    )
    far_near = in_team(far, 1)
    far_near, q_o = sync(far_near, q_o)
    q_ox, q_oy = in_req(q_o, 1), in_req(q_o, 2)
    kv_weight = [(kv, 0, 0), (kv_o, 0, 0), (w_x, 0, 0), (kv_ox, 0, 0)]
    kv_weight += [(w_y, 0, 0), (kv_oy_d, 0, 0), (kv_oy_d, others, 0), (kv_od, 0, 0)]

    def project(weight, is_kv, gain):
        starts = [part[1:] for part in weight]
        weight = [part[0] for part in weight]
        width = weight[1].shape[1]
        step = weight[1].shape[0] // (n_out - 1)
        depth = own.shape[1]
        n_outs = 1 if is_kv else 2
        return pl.pallas_call(
            functools.partial(project_kernel, n_out, TEAM * w_rows, step, starts, packed_rows, is_kv),
            out_shape=[shape((TEAM * rows // n_outs, width), bf16)] * n_outs,
            in_specs=[VMEM] * (7 + len(weight)),
            out_specs=[VMEM] * n_outs,
            scratch_shapes=[
                pltpu.VMEM((depth, width) if w_rows * TEAM % LANES else (ID_ROWS, LANES), bf16),
                pltpu.SemaphoreType.DMA((n_req * n_out,)),
            ],
            cost_estimate=pl.CostEstimate(
                flops=2 * TEAM * rows * depth * width, bytes_accessed=6 * MIB, transcendentals=0
            ),
            compiler_params=params(4 if w_rows * TEAM % LANES == 0 else 12),
            name="project_kv" if is_kv else "project_q",
        )(own, got[1], far, far_near, *weight, gain[None, :], cosine, sine)

    (made,) = project(kv_weight, True, k_gain)
    q_ox, q_oy, q_x = sync(q_ox, q_oy, q_x)
    q_od, q_d = in_req(q_oy, 1), in_req(q_x, 2)
    q_weight = [(q, 0, 0), (q_o, 0, 0), (w_x, 0, HD), (q_ox, 0, 0)]
    q_weight += [(w_y, 0, HD), (q_oy, 0, 0), (q_d, 0, 0), (q_od, 0, 0)]
    mine = [made] + [across(made, k) for k in range(1, n_out)]
    other = [in_team(part, 1) for part in mine]

    to_near, queries = project(q_weight, False, q_gain)
    from_near = in_team(to_near, 1)

    total = TEAM * rows * n_out
    store_mib = -(-2 * total * HD * 2 // MIB)
    page_shape = shape((slot_count, blk_rows, 2 * HD), bf16)
    own_pages, away_pages, store = pl.pallas_call(
        functools.partial(pages_kernel, n_out, blk_rows),
        out_shape=[page_shape, page_shape, shape((2, total, HD), bf16)],
        in_specs=[VMEM] * (2 * n_out) + [SMEM] * 2,
        out_specs=[VMEM] * 3,
        cost_estimate=pl.CostEstimate(flops=0, bytes_accessed=4 * MIB, transcendentals=0),
        compiler_params=params(store_mib + 1),
        name="pages",
    )(*mine, *other, all_ids, info)
    got_pages = in_team(away_pages, 2)

    def attend(step):
        return pl.pallas_call(
            functools.partial(attend_kernel, blk_rows, step),
            out_shape=shape((rows, H // 2 * HD), bf16),
            in_specs=[VMEM] * 3 + [SMEM] * 2,
            out_specs=VMEM,
            cost_estimate=pl.CostEstimate(
                flops=2 * H * HD * rows * total, bytes_accessed=4 * MIB, transcendentals=0
            ),
            compiler_params=params(store_mib + 2 + 3 * total // 1024),
            name="attend",
        )(store, queries, from_near, all_ids, lengths)

    from_far = in_team(attend(2), 2)
    kept = attend(0)

    attended, pages = pl.pallas_call(
        finish_kernel,
        out_shape=[shape((rows, H * HD), bf16), page_shape],
        in_specs=[ANY] * 4 + [SMEM],
        out_specs=[ANY] * 2,
        scratch_shapes=[pltpu.SemaphoreType.DMA((2 + slot_count,))],
        compiler_params=params(1),
        name="finish",
    )(kept, from_far, own_pages, got_pages, info)
    return attended[None], pages[None]


def solution(mesh):
    in_specs = (
        P("req", "blk", None),
        P("req", "blk"),
        P("req"),
        P("req", None, None),
        P(("req", "blk"), None),
        P(),
        P(),
    )
    out_specs = (P("req", "blk", None), P("req", "blk", None, None))
    return jax.shard_map(body, mesh=mesh, in_specs=in_specs, out_specs=out_specs, check_vma=False)
```

```python
import functools

import jax
import jax.numpy as jnp
from jax import lax
from jax.experimental import pallas as pl
from jax.experimental.pallas import tpu as pltpu
from jax.sharding import PartitionSpec as P

H = 8
KVH = 2
HD = 256
TEAM = 4
ID_ROWS = 16
LANES = 128
ROPE_BASE = 1000000.0
NORM_EPS = 1e-06
MIB = 1024 * 1024

ANY = pl.BlockSpec(memory_space=pl.ANY)
VMEM = pl.BlockSpec(memory_space=pltpu.VMEM)
SMEM = pl.BlockSpec(memory_space=pltpu.SMEM)


def params(mib):
    return pltpu.CompilerParams(vmem_limit_bytes=mib * MIB)


def place():
    blk = lax.axis_index("blk")
    return lax.axis_index("req"), (blk // 2) % 2, blk % 2


def run(copies):
    for copy in copies:
        copy.start()
    for copy in copies:
        copy.wait()


def aligned(index, size):
    return pl.ds(pl.multiple_of(index * size, size), size)


def q_start(pair, core):
    return pl.multiple_of((pair * 2 + core) * 2 * HD, 2 * HD)


def kv_start(pair, core):
    return pl.multiple_of(H * HD + core * KVH * HD + pair * HD, HD)


def pack_kernel(w_hbm, ids_hbm, tokens_hbm, *refs):
    outs, (w_ref, ids_ref, tokens_ref, sems) = refs[:TEAM], refs[TEAM:]
    run([
        pltpu.make_async_copy(source, there, sems.at[n])
        for n, (source, there) in enumerate(((w_hbm, w_ref), (ids_hbm, ids_ref), (tokens_hbm, tokens_ref)))
    ])
    _, pair, core = place()
    member = pair * 2 + core
    rows = w_ref.shape[0]
    per_device = ids_ref.shape[1]
    lane = lax.broadcasted_iota(jnp.int32, (ID_ROWS, LANES), 1) - member * per_device
    ids = jnp.zeros((ID_ROWS, LANES), jnp.int32)
    for j in range(per_device):
        ids = jnp.where(lane == j, ids_ref[0, j], ids)
    ids = ids.astype(jnp.float32).astype(jnp.bfloat16)
    blocks = 3 * HD // LANES
    for k in range(TEAM):
        to_pair, to_core = pair ^ (k // 2), core ^ (k % 2)
        for n in range(blocks):
            if n < HD // LANES:
                start = pl.multiple_of(kv_start(to_pair, to_core) + n * LANES, LANES)
            else:
                start = pl.multiple_of(q_start(to_pair, to_core) + n * LANES - HD, LANES)
            outs[k][n * rows : (n + 1) * rows, :] = w_ref[:, pl.ds(start, LANES)]
        outs[k][blocks * rows : blocks * rows + ID_ROWS, :] = ids
    token_rows = tokens_ref.shape[0]
    for n in range(tokens_ref.shape[1] // LANES):
        first = blocks * rows + ID_ROWS + n * token_rows
        outs[1][first : first + token_rows, :] = tokens_ref[:, n * LANES : (n + 1) * LANES]


def team_kernel(*refs):
    _, pair, core = place()
    parts, (kv_out, q_out, whole) = refs[:TEAM], refs[TEAM:]
    rows = q_out.shape[0] // TEAM
    member = pair * 2 + core
    for k in range(TEAM):
        here = aligned(member ^ k, rows)
        for n in range(3 * HD // LANES):
            out = kv_out if n < HD // LANES else q_out
            first = n * LANES if n < HD // LANES else n * LANES - HD
            part = parts[k][n * rows : (n + 1) * rows, :]
            out[here, first : first + LANES] = part
            whole[here, n * LANES : (n + 1) * LANES] = part
    first = 3 * HD // LANES * rows
    below = [part[first : first + ID_ROWS, :].astype(jnp.float32) for part in parts]
    ids = sum(below[1:], below[0]).astype(jnp.bfloat16)
    kv_out[TEAM * rows :, :] = jnp.concatenate([ids] * (HD // LANES), 1)


def regroup_kernel(kv_o, w_x, kv_out, q_out):
    rows = kv_o.shape[0]
    kv_out[:rows, :] = kv_o[...]
    kv_out[rows:, :] = w_x[:, :HD]
    q_out[...] = w_x[:, HD:]


def join_kernel(first, second, out):
    rows = first.shape[0]
    out[:rows, :] = first[...]
    out[rows:, :] = second[...]


def project_kernel(n_out, depth, tall, starts, first_row, sets, is_kv, *refs):
    n_outs = len(sets)
    n_tokens = sum(len(steps) for steps in sets)
    tokens = dict(zip(sorted(sum(sets, ())), refs[:n_tokens]))
    refs = refs[n_tokens:]
    weights, (gain_ref, cos_ref, sin_ref) = refs[: -5 - n_outs], refs[-5 - n_outs : -2 - n_outs]
    outs, (w_all, sems) = refs[-2 - n_outs : -2], refs[-2:]
    req = lax.axis_index("req")
    outer = lax.axis_index("blk") // TEAM
    _, pair, core = place()
    member = pair * 2 + core
    rows = tokens[0].shape[0] if 0 in tokens else tokens[2].shape[0]
    width = outs[0].shape[1]
    direct = depth % LANES == 0
    places = []
    for i, piece in enumerate(weights):
        from_req = req ^ (i // 2)
        for n in range(n_out - 1 if i % 2 else 1):
            from_outer = lax.rem(outer + n_out - n - i % 2, n_out)
            row, column = starts[i]
            part = piece.at[pl.ds(row + n * tall, depth), column : column + width]
            places.append((part, from_req * n_out + from_outer))
    if not direct:
        run([
            pltpu.make_async_copy(piece, w_all.at[aligned(index, depth), :], sems.at[n])
            for n, (piece, index) in enumerate(places)
        ])
    half = HD // 2
    gain = gain_ref[...]
    if is_kv:
        gain = jnp.where(core == 0, gain, 1.0)
    for out, steps in zip(outs, sets):

        def token_rows(k, start, size):
            if k != 1:
                return tokens[k][:, pl.ds(start, size)]
            blocks = []
            for n in range(size // LANES):
                first = pl.multiple_of(first_row + (start // LANES + n) * rows, 16)
                blocks.append(tokens[k][pl.ds(first, rows), :])
            return jnp.concatenate(blocks, 1)

        def team_rows(start, size):
            return jnp.concatenate([token_rows(k, start, size) for k in steps], 0)

        cosine, sine = (
            jnp.concatenate([ref[aligned(member ^ k, rows), :] for k in steps], 0) for ref in (cos_ref, sin_ref)
        )
        if is_kv:
            cosine = jnp.where(core == 0, cosine, 1.0)
            sine = jnp.where(core == 0, sine, 0.0)
        if direct:
            product = 0.0
            for piece, index in places:
                x = team_rows(pl.multiple_of(index * depth, depth), depth)
                product += jnp.dot(x, piece[...], preferred_element_type=jnp.float32)
        else:
            product = jnp.dot(team_rows(0, w_all.shape[0]), w_all[...], preferred_element_type=jnp.float32)
        for h in range(out.shape[1] // HD):
            head = product[:, h * HD : (h + 1) * HD]
            mean = jnp.mean(head * head, axis=-1, keepdims=True)
            head = head * lax.rsqrt(mean + NORM_EPS) * gain
            front, second = head[:, :half], head[:, half:]
            turned = jnp.concatenate([front * cosine - second * sine, second * cosine + front * sine], 1)
            turned = turned.astype(jnp.bfloat16)
            for n, k in enumerate(steps):
                there = aligned((member ^ k) % 2 if is_kv else n, rows)
                out[there, h * HD : (h + 1) * HD] = turned[n * rows : (n + 1) * rows]


def attend_kernel(blk_rows, step, store, q_ref, near_ref, ids_ref, length_ref, out):
    _, pair, core = place()
    length = length_ref[0]
    rows = out.shape[0]
    member = (pair * 2 + core) ^ step
    total = store.shape[1]
    quarter = total // 4
    heads = 2 * (out.shape[1] // (2 * HD))
    first = step // 2 * rows
    for j in range(rows // blk_rows):
        block = ids_ref[member * (rows // blk_rows) + j]
        here = slice(first + j * blk_rows, first + (j + 1) * blk_rows)
        there = slice(j * blk_rows, (j + 1) * blk_rows)
        for variant in range(4):
            seen = (variant + 1) * quarter

            @pl.when((block * blk_rows) // quarter == variant)
            def _():
                queries = jnp.concatenate(
                    [ref[here, h * HD : (h + 1) * HD] for ref in (q_ref, near_ref) for h in range(heads // 2)], 0
                )
                shape = (heads * blk_rows, 1)
                query_pos = block * blk_rows + lax.rem(lax.broadcasted_iota(jnp.int32, shape, 0), blk_rows)
                limit = jnp.minimum(query_pos, length - 1)
                key_pos = lax.broadcasted_iota(jnp.int32, (1, seen), 1)
                scores = lax.dot_general(
                    queries,
                    store[0, :seen, :],
                    (((1,), (1,)), ((), ())),
                    preferred_element_type=jnp.float32,
                )
                scores = jnp.where(key_pos <= limit, scores, jnp.finfo(jnp.float32).min)
                weights = jnp.exp(scores - jnp.max(scores, axis=-1, keepdims=True))
                row_sum = jnp.sum(weights, axis=-1, keepdims=True)
                summed = jnp.dot(
                    weights.astype(jnp.bfloat16), store[1, :seen, :], preferred_element_type=jnp.float32
                )
                result = jnp.where(query_pos < length, summed / row_sum, 0.0).astype(jnp.bfloat16)
                for n in range(heads):
                    side = core if n < heads // 2 else 1 - core
                    column = side * (heads // 2) + n % (heads // 2)
                    out[there, aligned(column, HD)] = result[n * blk_rows : (n + 1) * blk_rows]


def pages_kernel(n_out, blk_rows, *refs):
    mine, other = refs[: 2 * n_out], refs[2 * n_out : 4 * n_out - 1]
    ids_ref, info_ref, own, away, store = refs[4 * n_out - 1 :]
    _, pair, core = place()
    per_half = mine[0].shape[0] // blk_rows
    for n in range(2 * n_out):
        side = pair if n % 2 == 0 else 1 - pair
        for j in range(per_half):
            there = aligned(ids_ref[(n // 2 * 2 + side) * per_half + j], blk_rows)
            here = slice(j * blk_rows, (j + 1) * blk_rows)
            store[core, there, :] = mine[n][here, :]
            if n < 2:
                here = slice((n * per_half + j) * blk_rows, (n * per_half + j + 1) * blk_rows)
            store[1 - core, there, :] = other[max(n - 1, 0)][here, :]
    slots = own.shape[0]
    row = lax.broadcasted_iota(jnp.int32, (blk_rows, HD), 0)
    for target, base in ((away, slots), (own, 0)):
        for i in range(slots):
            here = aligned(info_ref[1, base + i], blk_rows)
            live = row < info_ref[2, base + i]
            for half in range(2):
                page = store[half, here, :]
                target[i, :, half * HD : (half + 1) * HD] = jnp.where(live, page, jnp.zeros_like(page))


def finish_kernel(kept, from_far, own_pages, got_pages, info_ref, att_out, page_out, sems):
    _, pair, _ = place()
    width = kept.shape[1]
    copies = [
        pltpu.make_async_copy(kept, att_out.at[:, aligned(pair, width)], sems.at[0]),
        pltpu.make_async_copy(from_far, att_out.at[:, aligned(1 - pair, width)], sems.at[1]),
    ]
    for copy in copies:
        copy.start()
    for i in range(page_out.shape[0]):
        here = info_ref[0, i] == pair
        ours = pltpu.make_async_copy(own_pages.at[i], page_out.at[i], sems.at[2 + i])
        theirs = pltpu.make_async_copy(got_pages.at[i], page_out.at[i], sems.at[2 + i])
        copies.append(ours)

        @pl.when(here)
        def _():
            ours.start()

        @pl.when(jnp.logical_not(here))
        def _():
            theirs.start()

    for copy in copies:
        copy.wait()


def body(tokens, block_ids, lengths, page_table, qkv_weight, q_gain, k_gain):
    n_req, n_blk = lax.axis_size("req"), lax.axis_size("blk")
    n_out = n_blk // TEAM
    bf16 = jnp.bfloat16
    shape = jax.ShapeDtypeStruct
    blk = lax.axis_index("blk")
    member = blk % TEAM

    def in_team(array, k):
        return lax.ppermute(array, "blk", [(i, i ^ k) for i in range(n_blk)])

    def in_req(array, k):
        return lax.ppermute(array, "req", [(i, i ^ k) for i in range(n_req)])

    def across(array, k):
        return lax.ppermute(array, "blk", [(i, (i + TEAM * k) % n_blk) for i in range(n_blk)])

    def sync(*arrays):
        return lax.optimization_barrier(arrays)

    w_rows = qkv_weight.shape[0]
    per_device = block_ids.shape[1]
    own = tokens[0]
    rows = own.shape[0]
    packed_rows = 3 * HD // LANES * w_rows + ID_ROWS
    parts = pl.pallas_call(
        pack_kernel,
        out_shape=[
            shape((packed_rows + (own.size // LANES if k == 1 else 0), LANES), bf16) for k in range(TEAM)
        ],
        in_specs=[pl.BlockSpec(memory_space=pltpu.HBM)] * 3,
        out_specs=[VMEM] * TEAM,
        scratch_shapes=[
            pltpu.VMEM(qkv_weight.shape, bf16),
            pltpu.SMEM(block_ids.shape, jnp.int32),
            pltpu.VMEM(own.shape, bf16),
            pltpu.SemaphoreType.DMA((3,)),
        ],
        compiler_params=params(56),
        name="pack",
    )(qkv_weight, block_ids, own)
    got = [parts[0]] + [in_team(parts[k], k) for k in range(1, TEAM)]
    kv, q, w = pl.pallas_call(
        team_kernel,
        out_shape=[
            shape((TEAM * w_rows + ID_ROWS, HD), bf16),
            shape((TEAM * w_rows, 2 * HD), bf16),
            shape((TEAM * w_rows, 3 * HD), bf16),
        ],
        in_specs=[VMEM] * TEAM,
        out_specs=[VMEM] * 3,
        compiler_params=params(2),
        name="team",
    )(*got)

    def from_others(piece):
        got = [across(piece, k) for k in range(1, n_out)]
        return got[0] if len(got) == 1 else jnp.concatenate(got, 0)

    kv, q, w, own = sync(kv, q, w, own)
    kv_o, w_x, w_y = from_others(kv), in_req(w, 1), in_req(w, 2)
    q_o, far = from_others(q), in_team(own, 2)

    blk_rows = rows // per_device
    tall = kv.shape[0]
    team_ids = kv[tall - ID_ROWS, : TEAM * per_device][None].astype(jnp.int32)
    other_ids = kv_o.reshape(n_out - 1, tall, HD)[:, tall - ID_ROWS, : TEAM * per_device].astype(jnp.int32)
    all_ids = jnp.concatenate([team_ids, other_ids], 0).reshape(-1)

    offsets = jnp.arange(blk_rows, dtype=jnp.int32)
    positions = (team_ids[0][:, None] * blk_rows + offsets[None, :]).reshape(-1, 1)
    inverse = jnp.power(jnp.float32(ROPE_BASE), -2.0 * jnp.arange(HD // 2).astype(jnp.float32) / HD)
    angles = positions.astype(jnp.float32) * inverse[None, :]
    cosine, sine = jnp.cos(angles), jnp.sin(angles)

    table = page_table[0].reshape(-1)
    per_head = page_table.shape[2]
    slot_count = page_table.shape[1] * per_head // n_blk
    wanted = jnp.concatenate(
        [b * slot_count + jnp.arange(slot_count, dtype=jnp.int32) for b in (blk, blk ^ 2)]
    )
    flat = jnp.sum(
        jnp.where(wanted[:, None] == table[None, :], jnp.arange(table.shape[0], dtype=jnp.int32)[None, :], 0), 1
    )
    block = flat % per_head
    info = jnp.stack([flat // per_head, block, lengths[0] - block * blk_rows])

    kv_o, w_x, w_y = sync(kv_o, w_x, w_y)
    others = kv_o.shape[0]
    kv_o_x, q_x = pl.pallas_call(
        regroup_kernel,
        out_shape=[shape((others + w_x.shape[0], HD), bf16), shape((w_x.shape[0], 2 * HD), bf16)],
        in_specs=[VMEM] * 2,
        out_specs=[VMEM] * 2,
        compiler_params=params(1),
        name="regroup",
    )(kv_o, w_x)
    kv_ox, kv_oy_d, kv_od = in_req(kv_o, 1), in_req(kv_o_x, 2), in_req(kv_o, 3)
    kv_ox, kv_oy_d, kv_od, q_o, far, cosine, sine, all_ids, info = sync(
        kv_ox, kv_oy_d, kv_od, q_o, far, cosine, sine, all_ids, info
    )
    far_near, q_ox, q_oy = in_team(far, 1), in_req(q_o, 1), in_req(q_o, 2)
    team_tokens = [own, got[1], far, far_near]
    kv_weight = [(kv, 0, 0), (kv_o, 0, 0), (w_x, 0, 0), (kv_ox, 0, 0)]
    kv_weight += [(w_y, 0, 0), (kv_oy_d, 0, 0), (kv_oy_d, others, 0), (kv_od, 0, 0)]

    def project(weight, sets, is_kv, gain):
        starts = [part[1:] for part in weight]
        weight = [part[0] for part in weight]
        width = weight[1].shape[1]
        step = weight[1].shape[0] // (n_out - 1)
        depth = own.shape[1]
        n_outs = len(sets)
        used = [team_tokens[k] for k in sorted(sum(sets, ()))]
        return pl.pallas_call(
            functools.partial(project_kernel, n_out, TEAM * w_rows, step, starts, packed_rows, sets, is_kv),
            out_shape=[shape((2 * rows, width), bf16)] * n_outs,
            in_specs=[VMEM] * (3 + len(used) + len(weight)),
            out_specs=[VMEM] * n_outs,
            scratch_shapes=[
                pltpu.VMEM((depth, width) if w_rows * TEAM % LANES else (ID_ROWS, LANES), bf16),
                pltpu.SemaphoreType.DMA((n_req * n_out,)),
            ],
            cost_estimate=pl.CostEstimate(
                flops=2 * len(used) * rows * depth * width, bytes_accessed=6 * MIB, transcendentals=0
            ),
            compiler_params=params(4 if w_rows * TEAM % LANES == 0 else 12),
            name="project_kv" if is_kv else "project_q",
        )(*used, *weight, gain[None, :], cosine, sine)

    halves = [project(kv_weight, [steps], True, k_gain)[0] for steps in ((0, 1), (2, 3))]
    mine = halves + [across(half, k) for k in range(1, n_out) for half in halves]
    q_ox, q_oy, q_x, mine[2], halves[1] = sync(q_ox, q_oy, q_x, mine[2], halves[1])
    q_od, q_d = in_req(q_oy, 1), in_req(q_x, 2)
    q_weight = [(q, 0, 0), (q_o, 0, 0), (w_x, 0, HD), (q_ox, 0, 0)]
    q_weight += [(w_y, 0, HD), (q_oy, 0, 0), (q_d, 0, 0), (q_od, 0, 0)]
    made = pl.pallas_call(
        join_kernel,
        out_shape=shape((TEAM * rows, HD), bf16),
        in_specs=[VMEM] * 2,
        out_specs=VMEM,
        compiler_params=params(1),
        name="join",
    )(*halves)
    other = [in_team(made, 1)] + [in_team(half, 1) for half in mine[2:]]

    to_near, queries = project(q_weight, [(1, 3), (0, 2)], False, q_gain)
    from_near = in_team(to_near, 1)

    total = TEAM * rows * n_out
    store_mib = -(-2 * total * HD * 2 // MIB)
    page_shape = shape((slot_count, blk_rows, 2 * HD), bf16)
    own_pages, away_pages, store = pl.pallas_call(
        functools.partial(pages_kernel, n_out, blk_rows),
        out_shape=[page_shape, page_shape, shape((2, total, HD), bf16)],
        in_specs=[VMEM] * (4 * n_out - 1) + [SMEM] * 2,
        out_specs=[VMEM] * 3,
        cost_estimate=pl.CostEstimate(flops=0, bytes_accessed=4 * MIB, transcendentals=0),
        compiler_params=params(store_mib + 1),
        name="pages",
    )(*mine, *other, all_ids, info)
    got_pages = in_team(away_pages, 2)

    def attend(step):
        return pl.pallas_call(
            functools.partial(attend_kernel, blk_rows, step),
            out_shape=shape((rows, H // 2 * HD), bf16),
            in_specs=[VMEM] * 3 + [SMEM] * 2,
            out_specs=VMEM,
            cost_estimate=pl.CostEstimate(
                flops=2 * H * HD * rows * total, bytes_accessed=4 * MIB, transcendentals=0
            ),
            compiler_params=params(store_mib + 2 + 3 * total // 1024),
            name="attend",
        )(store, queries, from_near, all_ids, lengths)

    from_far = in_team(attend(2), 2)
    kept = attend(0)

    attended, pages = pl.pallas_call(
        finish_kernel,
        out_shape=[shape((rows, H * HD), bf16), page_shape],
        in_specs=[ANY] * 4 + [SMEM],
        out_specs=[ANY] * 2,
        scratch_shapes=[pltpu.SemaphoreType.DMA((2 + slot_count,))],
        compiler_params=params(1),
        name="finish",
    )(kept, from_far, own_pages, got_pages, info)
    return attended[None], pages[None]


def solution(mesh):
    in_specs = (
        P("req", "blk", None),
        P("req", "blk"),
        P("req"),
        P("req", None, None),
        P(("req", "blk"), None),
        P(),
        P(),
    )
    out_specs = (P("req", "blk", None), P("req", "blk", None, None))
    return jax.shard_map(body, mesh=mesh, in_specs=in_specs, out_specs=out_specs, check_vma=False)
```

```python
import functools

import jax
import jax.numpy as jnp
import numpy as np
from jax import lax
from jax.experimental import pallas as pl
from jax.experimental.pallas import tpu as pltpu
from jax.sharding import PartitionSpec as P

H = 8
KVH = 2
HD = 256
TEAM = 4
ID_ROWS = 16
LANES = 128
ROPE_BASE = 1000000.0
NORM_EPS = 1e-06
MIB = 1024 * 1024

ANY = pl.BlockSpec(memory_space=pl.ANY)
VMEM = pl.BlockSpec(memory_space=pltpu.VMEM)
SMEM = pl.BlockSpec(memory_space=pltpu.SMEM)


def params(mib):
    return pltpu.CompilerParams(vmem_limit_bytes=mib * MIB)


def place():
    blk = lax.axis_index("blk")
    return lax.axis_index("req"), (blk // 2) % 2, blk % 2


def run(copies):
    for copy in copies:
        copy.start()
    for copy in copies:
        copy.wait()


def aligned(index, size):
    return pl.ds(pl.multiple_of(index * size, size), size)


def q_start(pair, core):
    return pl.multiple_of((pair * 2 + core) * 2 * HD, 2 * HD)


def kv_start(pair, core):
    return pl.multiple_of(H * HD + core * KVH * HD + pair * HD, HD)


def pack_kernel(w_hbm, ids_hbm, tokens_hbm, *refs):
    outs, (w_ref, ids_ref, tokens_ref, sems) = refs[:TEAM], refs[TEAM:]
    run([
        pltpu.make_async_copy(source, there, sems.at[n])
        for n, (source, there) in enumerate(((w_hbm, w_ref), (ids_hbm, ids_ref), (tokens_hbm, tokens_ref)))
    ])
    _, pair, core = place()
    member = pair * 2 + core
    rows = w_ref.shape[0]
    per_device = ids_ref.shape[1]
    lane = lax.broadcasted_iota(jnp.int32, (ID_ROWS, LANES), 1) - member * per_device
    ids = jnp.zeros((ID_ROWS, LANES), jnp.int32)
    for j in range(per_device):
        ids = jnp.where(lane == j, ids_ref[0, j], ids)
    ids = ids.astype(jnp.float32).astype(jnp.bfloat16)
    blocks = 3 * HD // LANES
    for k in range(TEAM):
        to_pair, to_core = pair ^ (k // 2), core ^ (k % 2)
        for n in range(blocks):
            if n < HD // LANES:
                start = pl.multiple_of(kv_start(to_pair, to_core) + n * LANES, LANES)
            else:
                start = pl.multiple_of(q_start(to_pair, to_core) + n * LANES - HD, LANES)
            outs[k][n * rows : (n + 1) * rows, :] = w_ref[:, pl.ds(start, LANES)]
        outs[k][blocks * rows : blocks * rows + ID_ROWS, :] = ids
    token_rows = tokens_ref.shape[0]
    for n in range(tokens_ref.shape[1] // LANES):
        first = blocks * rows + ID_ROWS + n * token_rows
        outs[1][first : first + token_rows, :] = tokens_ref[:, n * LANES : (n + 1) * LANES]


def read_id(piece, row, n):
    ids = piece[row : row + ID_ROWS, :LANES].astype(jnp.float32)[:1]
    lane = lax.broadcasted_iota(jnp.int32, ids.shape, 1)
    return jnp.sum(jnp.where(lane == n, ids, 0.0)).astype(jnp.int32)


def angle_kernel(piece, first_cos, first_sin, off_cos, off_sin, cos_out, sin_out):
    blk_rows = off_cos.shape[0]
    for n in range(cos_out.shape[0] // blk_rows):
        block = pl.ds(read_id(piece, piece.shape[0] - ID_ROWS, n), 1)
        here = slice(n * blk_rows, (n + 1) * blk_rows)
        cosine, sine = first_cos[block, :], first_sin[block, :]
        cos_out[here, :] = cosine * off_cos[...] - sine * off_sin[...]
        sin_out[here, :] = sine * off_cos[...] + cosine * off_sin[...]


def invert_table(table, flat_of):
    per_head = table.shape[2]
    for head in range(table.shape[1]):

        @pl.loop(0, per_head)
        def _(block):
            flat_of[table[0, head, block]] = head * per_head + block


def team_kernel(*refs):
    _, pair, core = place()
    parts, (kv_out, q_out, whole) = refs[:TEAM], refs[TEAM:]
    rows = q_out.shape[0] // TEAM
    member = pair * 2 + core
    for k in range(TEAM):
        here = aligned(member ^ k, rows)
        for n in range(3 * HD // LANES):
            out = kv_out if n < HD // LANES else q_out
            first = n * LANES if n < HD // LANES else n * LANES - HD
            part = parts[k][n * rows : (n + 1) * rows, :]
            out[here, first : first + LANES] = part
            whole[here, n * LANES : (n + 1) * LANES] = part
    first = 3 * HD // LANES * rows
    below = [part[first : first + ID_ROWS, :].astype(jnp.float32) for part in parts]
    ids = sum(below[1:], below[0]).astype(jnp.bfloat16)
    kv_out[TEAM * rows :, :] = jnp.concatenate([ids] * (HD // LANES), 1)


def regroup_kernel(kv_o, w_x, kv_out, q_out):
    rows = kv_o.shape[0]
    kv_out[:rows, :] = kv_o[...]
    kv_out[rows:, :] = w_x[:, :HD]
    q_out[...] = w_x[:, HD:]


def project_kernel(n_out, depth, tall, starts, first_row, is_kv, own, near, far, far_near, *refs):
    n_outs = 1 if is_kv else 2
    weights, (gain_ref, cos_ref, sin_ref) = refs[: -5 - n_outs], refs[-5 - n_outs : -2 - n_outs]
    outs, (w_all, sems) = refs[-2 - n_outs : -2], refs[-2:]
    req = lax.axis_index("req")
    outer = lax.axis_index("blk") // TEAM
    _, pair, core = place()
    member = pair * 2 + core
    rows = own.shape[0]
    width = outs[0].shape[1]
    direct = depth % LANES == 0
    places = []
    for i, piece in enumerate(weights):
        from_req = req ^ (i // 2)
        for n in range(n_out - 1 if i % 2 else 1):
            from_outer = lax.rem(outer + n_out - n - i % 2, n_out)
            row, column = starts[i]
            part = piece.at[pl.ds(row + n * tall, depth), column : column + width]
            places.append((part, from_req * n_out + from_outer))
    if not direct:
        run([
            pltpu.make_async_copy(piece, w_all.at[aligned(index, depth), :], sems.at[n])
            for n, (piece, index) in enumerate(places)
        ])
    half = HD // 2
    gain = gain_ref[...]
    if is_kv:
        gain = jnp.where(core == 0, gain, 1.0)
    for out, steps in zip(outs, [(0, 1, 2, 3)] if is_kv else [(1, 3), (0, 2)]):

        def token_rows(k, start, size):
            if k != 1:
                return (own, None, far, far_near)[k][:, pl.ds(start, size)]
            blocks = []
            for n in range(size // LANES):
                first = pl.multiple_of(first_row + (start // LANES + n) * rows, 16)
                blocks.append(near[pl.ds(first, rows), :])
            return jnp.concatenate(blocks, 1)

        def team_rows(start, size):
            return jnp.concatenate([token_rows(k, start, size) for k in steps], 0)

        cosine, sine = (
            jnp.concatenate([ref[aligned(member ^ k, rows), :] for k in steps], 0) for ref in (cos_ref, sin_ref)
        )
        if is_kv:
            cosine = jnp.where(core == 0, cosine, 1.0)
            sine = jnp.where(core == 0, sine, 0.0)
        if direct:
            product = 0.0
            for piece, index in places:
                x = team_rows(pl.multiple_of(index * depth, depth), depth)
                product += jnp.dot(x, piece[...], preferred_element_type=jnp.float32)
        else:
            product = jnp.dot(team_rows(0, w_all.shape[0]), w_all[...], preferred_element_type=jnp.float32)
        for h in range(out.shape[1] // HD):
            head = product[:, h * HD : (h + 1) * HD]
            mean = jnp.mean(head * head, axis=-1, keepdims=True)
            head = head * lax.rsqrt(mean + NORM_EPS) * gain
            front, second = head[:, :half], head[:, half:]
            turned = jnp.concatenate([front * cosine - second * sine, second * cosine + front * sine], 1)
            turned = turned.astype(jnp.bfloat16)
            for n, k in enumerate(steps):
                there = aligned(member ^ k if is_kv else n, rows)
                out[there, h * HD : (h + 1) * HD] = turned[n * rows : (n + 1) * rows]


def attend_kernel(blk_rows, step, store, q_ref, near_ref, piece, length_ref, out):
    _, pair, core = place()
    length = length_ref[0]
    rows = out.shape[0]
    member = (pair * 2 + core) ^ step
    total = store.shape[1]
    quarter = total // 4
    heads = 2 * (out.shape[1] // (2 * HD))
    first = step // 2 * rows
    for j in range(rows // blk_rows):
        block = read_id(piece, piece.shape[0] - ID_ROWS, member * (rows // blk_rows) + j)
        here = slice(first + j * blk_rows, first + (j + 1) * blk_rows)
        there = slice(j * blk_rows, (j + 1) * blk_rows)
        for variant in range(4):
            seen = (variant + 1) * quarter

            @pl.when((block * blk_rows) // quarter == variant)
            def _():
                queries = jnp.concatenate(
                    [ref[here, h * HD : (h + 1) * HD] for ref in (q_ref, near_ref) for h in range(heads // 2)], 0
                )
                shape = (heads * blk_rows, 1)
                query_pos = block * blk_rows + lax.rem(lax.broadcasted_iota(jnp.int32, shape, 0), blk_rows)
                limit = jnp.minimum(query_pos, length - 1)
                key_pos = lax.broadcasted_iota(jnp.int32, (1, seen), 1)
                scores = lax.dot_general(
                    queries,
                    store[0, :seen, :],
                    (((1,), (1,)), ((), ())),
                    preferred_element_type=jnp.float32,
                )
                scores = jnp.where(key_pos <= limit, scores, jnp.finfo(jnp.float32).min)
                weights = jnp.exp(scores - jnp.max(scores, axis=-1, keepdims=True))
                row_sum = jnp.sum(weights, axis=-1, keepdims=True)
                summed = jnp.dot(
                    weights.astype(jnp.bfloat16), store[1, :seen, :], preferred_element_type=jnp.float32
                )
                result = jnp.where(query_pos < length, summed / row_sum, 0.0).astype(jnp.bfloat16)
                for n in range(heads):
                    side = core if n < heads // 2 else 1 - core
                    column = side * (heads // 2) + n % (heads // 2)
                    out[there, aligned(column, HD)] = result[n * blk_rows : (n + 1) * blk_rows]


def pages_kernel(n_out, blk_rows, *refs):
    mine, other = refs[:n_out], refs[n_out : 2 * n_out]
    piece, piece_o, table, length_ref, own, away, store, flat_of = refs[2 * n_out :]
    _, _, core = place()
    tall = piece.shape[0]
    per_piece = mine[0].shape[0] // blk_rows
    for k in range(n_out):
        for j in range(per_piece):
            block = read_id(*((piece_o, k * tall - ID_ROWS) if k else (piece, tall - ID_ROWS)), j)
            there = aligned(block, blk_rows)
            here = slice(j * blk_rows, (j + 1) * blk_rows)
            store[core, there, :] = mine[k][here, :]
            store[1 - core, there, :] = other[k][here, :]
    slots = own.shape[0]
    row = lax.broadcasted_iota(jnp.int32, (blk_rows, HD), 0)
    invert_table(table, flat_of)
    blk = lax.axis_index("blk")
    for target, device in ((away, blk ^ 2), (own, blk)):
        for i in range(slots):
            block = lax.rem(flat_of[device * slots + i], table.shape[2])
            here = aligned(block, blk_rows)
            live = row < length_ref[0] - block * blk_rows
            for half in range(2):
                page = store[half, here, :]
                target[i, :, half * HD : (half + 1) * HD] = jnp.where(live, page, jnp.zeros_like(page))


def finish_kernel(kept, from_far, own_pages, got_pages, table, att_out, page_out, flat_of, sems):
    _, pair, _ = place()
    invert_table(table, flat_of)
    slots = page_out.shape[0]
    width = kept.shape[1]
    copies = [
        pltpu.make_async_copy(kept, att_out.at[:, aligned(pair, width)], sems.at[0]),
        pltpu.make_async_copy(from_far, att_out.at[:, aligned(1 - pair, width)], sems.at[1]),
    ]
    for copy in copies:
        copy.start()
    for i in range(page_out.shape[0]):
        here = lax.div(flat_of[lax.axis_index("blk") * slots + i], table.shape[2]) == pair
        ours = pltpu.make_async_copy(own_pages.at[i], page_out.at[i], sems.at[2 + i])
        theirs = pltpu.make_async_copy(got_pages.at[i], page_out.at[i], sems.at[2 + i])
        copies.append(ours)

        @pl.when(here)
        def _():
            ours.start()

        @pl.when(jnp.logical_not(here))
        def _():
            theirs.start()

    for copy in copies:
        copy.wait()


def body(tokens, block_ids, lengths, page_table, qkv_weight, q_gain, k_gain):
    n_req, n_blk = lax.axis_size("req"), lax.axis_size("blk")
    n_out = n_blk // TEAM
    bf16 = jnp.bfloat16
    shape = jax.ShapeDtypeStruct
    blk = lax.axis_index("blk")
    member = blk % TEAM

    def in_team(array, k):
        return lax.ppermute(array, "blk", [(i, i ^ k) for i in range(n_blk)])

    def in_req(array, k):
        return lax.ppermute(array, "req", [(i, i ^ k) for i in range(n_req)])

    def across(array, k):
        return lax.ppermute(array, "blk", [(i, (i + TEAM * k) % n_blk) for i in range(n_blk)])

    def sync(*arrays):
        return lax.optimization_barrier(arrays)

    w_rows = qkv_weight.shape[0]
    per_device = block_ids.shape[1]
    own = tokens[0]
    rows = own.shape[0]
    packed_rows = 3 * HD // LANES * w_rows + ID_ROWS
    parts = pl.pallas_call(
        pack_kernel,
        out_shape=[
            shape((packed_rows + (own.size // LANES if k == 1 else 0), LANES), bf16) for k in range(TEAM)
        ],
        in_specs=[pl.BlockSpec(memory_space=pltpu.HBM)] * 3,
        out_specs=[VMEM] * TEAM,
        scratch_shapes=[
            pltpu.VMEM(qkv_weight.shape, bf16),
            pltpu.SMEM(block_ids.shape, jnp.int32),
            pltpu.VMEM(own.shape, bf16),
            pltpu.SemaphoreType.DMA((3,)),
        ],
        compiler_params=params(56),
        name="pack",
    )(qkv_weight, block_ids, own)
    got = [parts[0]] + [in_team(parts[k], k) for k in range(1, TEAM)]
    kv, q, w = pl.pallas_call(
        team_kernel,
        out_shape=[
            shape((TEAM * w_rows + ID_ROWS, HD), bf16),
            shape((TEAM * w_rows, 2 * HD), bf16),
            shape((TEAM * w_rows, 3 * HD), bf16),
        ],
        in_specs=[VMEM] * TEAM,
        out_specs=[VMEM] * 3,
        compiler_params=params(2),
        name="team",
    )(*got)

    def from_others(piece):
        got = [across(piece, k) for k in range(1, n_out)]
        return got[0] if len(got) == 1 else jnp.concatenate(got, 0)

    kv, q, w, own = sync(kv, q, w, own)
    kv_o, w_x, w_y = from_others(kv), in_req(w, 1), in_req(w, 2)
    q_o, far = from_others(q), in_team(own, 2)

    blk_rows = rows // per_device
    half = HD // 2
    inverse = np.float64(ROPE_BASE) ** (-2.0 * np.arange(half) / HD)
    tables = []
    for positions in (np.arange(per_device * n_blk) * blk_rows, np.arange(blk_rows)):
        angles = positions[:, None] * inverse[None, :]
        tables += [np.cos(angles).astype(np.float32), np.sin(angles).astype(np.float32)]
    cosine, sine = pl.pallas_call(
        angle_kernel,
        out_shape=[shape((TEAM * rows, half), jnp.float32)] * 2,
        in_specs=[VMEM] * 5,
        out_specs=[VMEM] * 2,
        cost_estimate=pl.CostEstimate(flops=0, bytes_accessed=38 * MIB, transcendentals=0),
        compiler_params=params(2),
        name="angles",
    )(kv, *tables)
    slot_count = page_table.shape[1] * page_table.shape[2] // n_blk

    kv_o, w_x, w_y = sync(kv_o, w_x, w_y)
    others = kv_o.shape[0]
    kv_o_x, q_x = pl.pallas_call(
        regroup_kernel,
        out_shape=[shape((others + w_x.shape[0], HD), bf16), shape((w_x.shape[0], 2 * HD), bf16)],
        in_specs=[VMEM] * 2,
        out_specs=[VMEM] * 2,
        compiler_params=params(1),
        name="regroup",
    )(kv_o, w_x)
    kv_ox, kv_oy_d, kv_od = in_req(kv_o, 1), in_req(kv_o_x, 2), in_req(kv_o, 3)
    kv_ox, kv_oy_d, kv_od, q_o, far, cosine, sine = sync(kv_ox, kv_oy_d, kv_od, q_o, far, cosine, sine)
    far_near = in_team(far, 1)
    far_near, q_o = sync(far_near, q_o)
    q_ox, q_oy = in_req(q_o, 1), in_req(q_o, 2)
    kv_weight = [(kv, 0, 0), (kv_o, 0, 0), (w_x, 0, 0), (kv_ox, 0, 0)]
    kv_weight += [(w_y, 0, 0), (kv_oy_d, 0, 0), (kv_oy_d, others, 0), (kv_od, 0, 0)]

    def project(weight, is_kv, gain):
        starts = [part[1:] for part in weight]
        weight = [part[0] for part in weight]
        width = weight[1].shape[1]
        step = weight[1].shape[0] // (n_out - 1)
        depth = own.shape[1]
        n_outs = 1 if is_kv else 2
        return pl.pallas_call(
            functools.partial(project_kernel, n_out, TEAM * w_rows, step, starts, packed_rows, is_kv),
            out_shape=[shape((TEAM * rows // n_outs, width), bf16)] * n_outs,
            in_specs=[VMEM] * (7 + len(weight)),
            out_specs=[VMEM] * n_outs,
            scratch_shapes=[
                pltpu.VMEM((depth, width) if w_rows * TEAM % LANES else (ID_ROWS, LANES), bf16),
                pltpu.SemaphoreType.DMA((n_req * n_out,)),
            ],
            cost_estimate=pl.CostEstimate(
                flops=2 * TEAM * rows * depth * width, bytes_accessed=6 * MIB, transcendentals=0
            ),
            compiler_params=params(4 if w_rows * TEAM % LANES == 0 else 12),
            name="project_kv" if is_kv else "project_q",
        )(own, got[1], far, far_near, *weight, gain[None, :], cosine, sine)

    (made,) = project(kv_weight, True, k_gain)
    q_ox, q_oy, q_x = sync(q_ox, q_oy, q_x)
    q_od, q_d = in_req(q_oy, 1), in_req(q_x, 2)
    q_weight = [(q, 0, 0), (q_o, 0, 0), (w_x, 0, HD), (q_ox, 0, 0)]
    q_weight += [(w_y, 0, HD), (q_oy, 0, 0), (q_d, 0, 0), (q_od, 0, 0)]
    mine = [made] + [across(made, k) for k in range(1, n_out)]
    other = [in_team(part, 1) for part in mine]

    to_near, queries = project(q_weight, False, q_gain)
    from_near = in_team(to_near, 1)

    total = TEAM * rows * n_out
    store_mib = -(-2 * total * HD * 2 // MIB)
    page_shape = shape((slot_count, blk_rows, 2 * HD), bf16)
    own_pages, away_pages, store = pl.pallas_call(
        functools.partial(pages_kernel, n_out, blk_rows),
        out_shape=[page_shape, page_shape, shape((2, total, HD), bf16)],
        in_specs=[VMEM] * (2 * n_out + 2) + [SMEM] * 2,
        out_specs=[VMEM] * 3,
        scratch_shapes=[pltpu.SMEM((page_table.size,), jnp.int32)],
        cost_estimate=pl.CostEstimate(flops=0, bytes_accessed=4 * MIB, transcendentals=0),
        compiler_params=params(store_mib + 1),
        name="pages",
    )(*mine, *other, kv, kv_o, page_table, lengths)
    got_pages = in_team(away_pages, 2)

    def attend(step):
        return pl.pallas_call(
            functools.partial(attend_kernel, blk_rows, step),
            out_shape=shape((rows, H // 2 * HD), bf16),
            in_specs=[VMEM] * 4 + [SMEM],
            out_specs=VMEM,
            cost_estimate=pl.CostEstimate(
                flops=2 * H * HD * rows * total, bytes_accessed=4 * MIB, transcendentals=0
            ),
            compiler_params=params(store_mib + 2 + 3 * total // 1024),
            name="attend",
        )(store, queries, from_near, kv, lengths)

    from_far = in_team(attend(2), 2)
    kept = attend(0)

    attended, pages = pl.pallas_call(
        finish_kernel,
        out_shape=[shape((rows, H * HD), bf16), page_shape],
        in_specs=[ANY] * 4 + [SMEM],
        out_specs=[ANY] * 2,
        scratch_shapes=[pltpu.SMEM((page_table.size,), jnp.int32), pltpu.SemaphoreType.DMA((2 + slot_count,))],
        compiler_params=params(1),
        name="finish",
    )(kept, from_far, own_pages, got_pages, page_table)
    return attended[None], pages[None]


def solution(mesh):
    in_specs = (
        P("req", "blk", None),
        P("req", "blk"),
        P("req"),
        P("req", None, None),
        P(("req", "blk"), None),
        P(),
        P(),
    )
    out_specs = (P("req", "blk", None), P("req", "blk", None, None))
    return jax.shard_map(body, mesh=mesh, in_specs=in_specs, out_specs=out_specs, check_vma=False)
```

```python
import functools

import jax
import jax.numpy as jnp
import numpy as np
from jax import lax
from jax.experimental import pallas as pl
from jax.experimental.pallas import tpu as pltpu
from jax.sharding import PartitionSpec as P

H = 8
KVH = 2
HD = 256
TEAM = 4
ID_ROWS = 16
LANES = 128
ROPE_BASE = 1000000.0
NORM_EPS = 1e-06
MIB = 1024 * 1024

ANY = pl.BlockSpec(memory_space=pl.ANY)
VMEM = pl.BlockSpec(memory_space=pltpu.VMEM)
SMEM = pl.BlockSpec(memory_space=pltpu.SMEM)


def params(mib):
    return pltpu.CompilerParams(vmem_limit_bytes=mib * MIB)


def place():
    blk = lax.axis_index("blk")
    return lax.axis_index("req"), (blk // 2) % 2, blk % 2


def run(copies):
    for copy in copies:
        copy.start()
    for copy in copies:
        copy.wait()


def aligned(index, size):
    return pl.ds(pl.multiple_of(index * size, size), size)


def q_start(pair, core):
    return pl.multiple_of((pair * 2 + core) * 2 * HD, 2 * HD)


def kv_start(pair, core):
    return pl.multiple_of(H * HD + core * KVH * HD + pair * HD, HD)


def pack_kernel(w_hbm, ids_hbm, tokens_hbm, *refs):
    outs, (w_ref, ids_ref, tokens_ref, sems) = refs[:TEAM], refs[TEAM:]
    run([
        pltpu.make_async_copy(source, there, sems.at[n])
        for n, (source, there) in enumerate(((w_hbm, w_ref), (ids_hbm, ids_ref), (tokens_hbm, tokens_ref)))
    ])
    _, pair, core = place()
    member = pair * 2 + core
    rows = w_ref.shape[0]
    per_device = ids_ref.shape[1]
    lane = lax.broadcasted_iota(jnp.int32, (ID_ROWS, LANES), 1) - member * per_device
    ids = jnp.zeros((ID_ROWS, LANES), jnp.int32)
    for j in range(per_device):
        ids = jnp.where(lane == j, ids_ref[0, j], ids)
    ids = ids.astype(jnp.float32).astype(jnp.bfloat16)
    blocks = 3 * HD // LANES
    for k in range(TEAM):
        to_pair, to_core = pair ^ (k // 2), core ^ (k % 2)
        for n in range(blocks):
            if n < HD // LANES:
                start = pl.multiple_of(kv_start(to_pair, to_core) + n * LANES, LANES)
            else:
                start = pl.multiple_of(q_start(to_pair, to_core) + n * LANES - HD, LANES)
            outs[k][n * rows : (n + 1) * rows, :] = w_ref[:, pl.ds(start, LANES)]
        outs[k][blocks * rows : blocks * rows + ID_ROWS, :] = ids
    token_rows = tokens_ref.shape[0]
    for n in range(tokens_ref.shape[1] // LANES):
        first = blocks * rows + ID_ROWS + n * token_rows
        outs[1][first : first + token_rows, :] = tokens_ref[:, n * LANES : (n + 1) * LANES]


def read_id(piece, row, n):
    ids = piece[row : row + ID_ROWS, :LANES].astype(jnp.float32)[:1]
    lane = lax.broadcasted_iota(jnp.int32, ids.shape, 1)
    return jnp.sum(jnp.where(lane == n, ids, 0.0)).astype(jnp.int32)


def angle_kernel(piece, first_cos, first_sin, off_cos, off_sin, cos_out, sin_out):
    blk_rows = off_cos.shape[0]
    for n in range(cos_out.shape[0] // blk_rows):
        block = pl.ds(read_id(piece, piece.shape[0] - ID_ROWS, n), 1)
        here = slice(n * blk_rows, (n + 1) * blk_rows)
        cosine, sine = first_cos[block, :], first_sin[block, :]
        cos_out[here, :] = cosine * off_cos[...] - sine * off_sin[...]
        sin_out[here, :] = sine * off_cos[...] + cosine * off_sin[...]


def invert_table(table, flat_of):
    per_head = table.shape[2]
    for head in range(table.shape[1]):

        @pl.loop(0, per_head)
        def _(block):
            flat_of[table[0, head, block]] = head * per_head + block


def team_kernel(*refs):
    _, pair, core = place()
    parts, (kv_out, q_out, whole) = refs[:TEAM], refs[TEAM:]
    rows = q_out.shape[0] // TEAM
    member = pair * 2 + core
    for k in range(TEAM):
        here = aligned(member ^ k, rows)
        for n in range(3 * HD // LANES):
            out = kv_out if n < HD // LANES else q_out
            first = n * LANES if n < HD // LANES else n * LANES - HD
            part = parts[k][n * rows : (n + 1) * rows, :]
            out[here, first : first + LANES] = part
            whole[here, n * LANES : (n + 1) * LANES] = part
    first = 3 * HD // LANES * rows
    below = [part[first : first + ID_ROWS, :].astype(jnp.float32) for part in parts]
    ids = sum(below[1:], below[0]).astype(jnp.bfloat16)
    kv_out[TEAM * rows :, :] = jnp.concatenate([ids] * (HD // LANES), 1)


def regroup_kernel(kv_o, w_x, kv_out, q_out):
    rows = kv_o.shape[0]
    kv_out[:rows, :] = kv_o[...]
    kv_out[rows:, :] = w_x[:, :HD]
    q_out[...] = w_x[:, HD:]


def project_kernel(n_out, depth, tall, starts, first_row, is_kv, own, near, far, far_near, *refs):
    n_outs = 1 if is_kv else 2
    weights, (gain_ref, cos_ref, sin_ref) = refs[: -5 - n_outs], refs[-5 - n_outs : -2 - n_outs]
    outs, (w_all, sems) = refs[-2 - n_outs : -2], refs[-2:]
    req = lax.axis_index("req")
    outer = lax.axis_index("blk") // TEAM
    _, pair, core = place()
    member = pair * 2 + core
    rows = own.shape[0]
    width = outs[0].shape[1]
    direct = depth % LANES == 0
    places = []
    for i, piece in enumerate(weights):
        from_req = req ^ (i // 2)
        for n in range(n_out - 1 if i % 2 else 1):
            from_outer = lax.rem(outer + n_out - n - i % 2, n_out)
            row, column = starts[i]
            part = piece.at[pl.ds(row + n * tall, depth), column : column + width]
            places.append((part, from_req * n_out + from_outer))
    if not direct:
        run([
            pltpu.make_async_copy(piece, w_all.at[aligned(index, depth), :], sems.at[n])
            for n, (piece, index) in enumerate(places)
        ])
    half = HD // 2
    gain = gain_ref[...]
    if is_kv:
        gain = jnp.where(core == 0, gain, 1.0)
    for out, steps in zip(outs, [(0, 1, 2, 3)] if is_kv else [(1, 3), (0, 2)]):

        def token_rows(k, start, size):
            if k != 1:
                return (own, None, far, far_near)[k][:, pl.ds(start, size)]
            blocks = []
            for n in range(size // LANES):
                first = pl.multiple_of(first_row + (start // LANES + n) * rows, 16)
                blocks.append(near[pl.ds(first, rows), :])
            return jnp.concatenate(blocks, 1)

        def team_rows(start, size):
            return jnp.concatenate([token_rows(k, start, size) for k in steps], 0)

        cosine, sine = (
            jnp.concatenate([ref[aligned(member ^ k, rows), :] for k in steps], 0) for ref in (cos_ref, sin_ref)
        )
        if is_kv:
            cosine = jnp.where(core == 0, cosine, 1.0)
            sine = jnp.where(core == 0, sine, 0.0)
        if direct:
            product = 0.0
            for piece, index in places:
                x = team_rows(pl.multiple_of(index * depth, depth), depth)
                product += jnp.dot(x, piece[...], preferred_element_type=jnp.float32)
        else:
            product = jnp.dot(team_rows(0, w_all.shape[0]), w_all[...], preferred_element_type=jnp.float32)
        for h in range(out.shape[1] // HD):
            head = product[:, h * HD : (h + 1) * HD]
            mean = jnp.mean(head * head, axis=-1, keepdims=True)
            head = head * lax.rsqrt(mean + NORM_EPS) * gain
            front, second = head[:, :half], head[:, half:]
            turned = jnp.concatenate([front * cosine - second * sine, second * cosine + front * sine], 1)
            turned = turned.astype(jnp.bfloat16)
            for n, k in enumerate(steps):
                there = aligned(member ^ k if is_kv else n, rows)
                out[there, h * HD : (h + 1) * HD] = turned[n * rows : (n + 1) * rows]


def attend_kernel(blk_rows, step, store, q_ref, near_ref, piece, length_ref, out):
    _, pair, core = place()
    length = length_ref[0]
    rows = out.shape[0]
    member = (pair * 2 + core) ^ step
    total = store.shape[1]
    quarter = total // 4
    heads = 2 * (out.shape[1] // (2 * HD))
    first = step // 2 * rows
    for j in range(rows // blk_rows):
        block = read_id(piece, piece.shape[0] - ID_ROWS, member * (rows // blk_rows) + j)
        here = slice(first + j * blk_rows, first + (j + 1) * blk_rows)
        there = slice(j * blk_rows, (j + 1) * blk_rows)
        for variant in range(4):
            seen = (variant + 1) * quarter

            @pl.when((block * blk_rows) // quarter == variant)
            def _():
                queries = jnp.concatenate(
                    [ref[here, h * HD : (h + 1) * HD] for ref in (q_ref, near_ref) for h in range(heads // 2)], 0
                )
                shape = (heads * blk_rows, 1)
                query_pos = block * blk_rows + lax.rem(lax.broadcasted_iota(jnp.int32, shape, 0), blk_rows)
                limit = jnp.minimum(query_pos, length - 1)
                key_pos = lax.broadcasted_iota(jnp.int32, (1, seen), 1)
                scores = lax.dot_general(
                    queries,
                    store[0, :seen, :],
                    (((1,), (1,)), ((), ())),
                    preferred_element_type=jnp.float32,
                )
                scores = jnp.where(key_pos <= limit, scores, jnp.finfo(jnp.float32).min)
                weights = jnp.exp(scores - jnp.max(scores, axis=-1, keepdims=True))
                row_sum = jnp.sum(weights, axis=-1, keepdims=True)
                summed = jnp.dot(
                    weights.astype(jnp.bfloat16), store[1, :seen, :], preferred_element_type=jnp.float32
                )
                result = jnp.where(query_pos < length, summed / row_sum, 0.0).astype(jnp.bfloat16)
                for n in range(heads):
                    side = core if n < heads // 2 else 1 - core
                    column = side * (heads // 2) + n % (heads // 2)
                    out[there, aligned(column, HD)] = result[n * blk_rows : (n + 1) * blk_rows]


def pages_kernel(n_out, blk_rows, *refs):
    mine, other = refs[:n_out], refs[n_out : 2 * n_out]
    piece, piece_o, table, length_ref, own, away, store, flat_of = refs[2 * n_out :]
    _, _, core = place()
    tall = piece.shape[0]
    per_piece = mine[0].shape[0] // blk_rows
    for k in range(n_out):
        for j in range(per_piece):
            block = read_id(*((piece_o, k * tall - ID_ROWS) if k else (piece, tall - ID_ROWS)), j)
            there = aligned(block, blk_rows)
            here = slice(j * blk_rows, (j + 1) * blk_rows)
            store[core, there, :] = mine[k][here, :]
            store[1 - core, there, :] = other[k][here, :]
    slots = own.shape[0]
    row = lax.broadcasted_iota(jnp.int32, (blk_rows, HD), 0)
    invert_table(table, flat_of)
    blk = lax.axis_index("blk")
    for target, device in ((away, blk ^ 2), (own, blk)):
        for i in range(slots):
            block = lax.rem(flat_of[device * slots + i], table.shape[2])
            here = aligned(block, blk_rows)
            live = row < length_ref[0] - block * blk_rows
            for half in range(2):
                page = store[half, here, :]
                target[i, :, half * HD : (half + 1) * HD] = jnp.where(live, page, jnp.zeros_like(page))


def finish_kernel(kept, from_far, own_pages, got_pages, table, att_out, page_out, flat_of, sems):
    _, pair, _ = place()
    invert_table(table, flat_of)
    slots = page_out.shape[0]
    width = kept.shape[1]
    copies = [
        pltpu.make_async_copy(kept, att_out.at[:, aligned(pair, width)], sems.at[0]),
        pltpu.make_async_copy(from_far, att_out.at[:, aligned(1 - pair, width)], sems.at[1]),
    ]
    for copy in copies:
        copy.start()
    for i in range(page_out.shape[0]):
        here = lax.div(flat_of[lax.axis_index("blk") * slots + i], table.shape[2]) == pair
        ours = pltpu.make_async_copy(own_pages.at[i], page_out.at[i], sems.at[2 + i])
        theirs = pltpu.make_async_copy(got_pages.at[i], page_out.at[i], sems.at[2 + i])
        copies.append(ours)

        @pl.when(here)
        def _():
            ours.start()

        @pl.when(jnp.logical_not(here))
        def _():
            theirs.start()

    for copy in copies:
        copy.wait()


def body(tokens, block_ids, lengths, page_table, qkv_weight, q_gain, k_gain):
    n_req, n_blk = lax.axis_size("req"), lax.axis_size("blk")
    n_out = n_blk // TEAM
    bf16 = jnp.bfloat16
    shape = jax.ShapeDtypeStruct
    blk = lax.axis_index("blk")
    member = blk % TEAM

    def in_team(array, k):
        return lax.ppermute(array, "blk", [(i, i ^ k) for i in range(n_blk)])

    def in_req(array, k):
        return lax.ppermute(array, "req", [(i, i ^ k) for i in range(n_req)])

    def across(array, k):
        return lax.ppermute(array, "blk", [(i, (i + TEAM * k) % n_blk) for i in range(n_blk)])

    def sync(*arrays):
        return lax.optimization_barrier(arrays)

    w_rows = qkv_weight.shape[0]
    per_device = block_ids.shape[1]
    own = tokens[0]
    rows = own.shape[0]
    packed_rows = 3 * HD // LANES * w_rows + ID_ROWS
    parts = pl.pallas_call(
        pack_kernel,
        out_shape=[
            shape((packed_rows + (own.size // LANES if k == 1 else 0), LANES), bf16) for k in range(TEAM)
        ],
        in_specs=[pl.BlockSpec(memory_space=pltpu.HBM)] * 3,
        out_specs=[VMEM] * TEAM,
        scratch_shapes=[
            pltpu.VMEM(qkv_weight.shape, bf16),
            pltpu.SMEM(block_ids.shape, jnp.int32),
            pltpu.VMEM(own.shape, bf16),
            pltpu.SemaphoreType.DMA((3,)),
        ],
        compiler_params=params(56),
        name="pack",
    )(qkv_weight, block_ids, own)
    got = [parts[0]] + [in_team(parts[k], k) for k in range(1, TEAM)]
    kv, q, w = pl.pallas_call(
        team_kernel,
        out_shape=[
            shape((TEAM * w_rows + ID_ROWS, HD), bf16),
            shape((TEAM * w_rows, 2 * HD), bf16),
            shape((TEAM * w_rows, 3 * HD), bf16),
        ],
        in_specs=[VMEM] * TEAM,
        out_specs=[VMEM] * 3,
        compiler_params=params(2),
        name="team",
    )(*got)

    def from_others(piece):
        got = [across(piece, k) for k in range(1, n_out)]
        return got[0] if len(got) == 1 else jnp.concatenate(got, 0)

    kv, q, w, own = sync(kv, q, w, own)
    kv_o, w_x, w_y = from_others(kv), in_req(w, 1), in_req(w, 2)
    q_o, far = from_others(q), in_team(own, 2)

    blk_rows = rows // per_device
    half = HD // 2
    inverse = np.float64(ROPE_BASE) ** (-2.0 * np.arange(half) / HD)
    tables = []
    for positions in (np.arange(per_device * n_blk) * blk_rows, np.arange(blk_rows)):
        angles = positions[:, None] * inverse[None, :]
        tables += [np.cos(angles).astype(np.float32), np.sin(angles).astype(np.float32)]
    cosine, sine = pl.pallas_call(
        angle_kernel,
        out_shape=[shape((TEAM * rows, half), jnp.float32)] * 2,
        in_specs=[VMEM] * 5,
        out_specs=[VMEM] * 2,
        cost_estimate=pl.CostEstimate(flops=10**10, bytes_accessed=40 * 10**6, transcendentals=0),
        compiler_params=params(2),
        name="angles",
    )(kv, *tables)
    slot_count = page_table.shape[1] * page_table.shape[2] // n_blk

    kv_o, w_x, w_y = sync(kv_o, w_x, w_y)
    others = kv_o.shape[0]
    kv_o_x, q_x = pl.pallas_call(
        regroup_kernel,
        out_shape=[shape((others + w_x.shape[0], HD), bf16), shape((w_x.shape[0], 2 * HD), bf16)],
        in_specs=[VMEM] * 2,
        out_specs=[VMEM] * 2,
        compiler_params=params(1),
        name="regroup",
    )(kv_o, w_x)
    kv_ox, kv_oy_d, kv_od = in_req(kv_o, 1), in_req(kv_o_x, 2), in_req(kv_o, 3)
    kv_ox, kv_oy_d, kv_od, q_o, far, cosine, sine = sync(kv_ox, kv_oy_d, kv_od, q_o, far, cosine, sine)
    far_near = in_team(far, 1)
    far_near, q_o = sync(far_near, q_o)
    q_ox, q_oy = in_req(q_o, 1), in_req(q_o, 2)
    kv_weight = [(kv, 0, 0), (kv_o, 0, 0), (w_x, 0, 0), (kv_ox, 0, 0)]
    kv_weight += [(w_y, 0, 0), (kv_oy_d, 0, 0), (kv_oy_d, others, 0), (kv_od, 0, 0)]

    def project(weight, is_kv, gain):
        starts = [part[1:] for part in weight]
        weight = [part[0] for part in weight]
        width = weight[1].shape[1]
        step = weight[1].shape[0] // (n_out - 1)
        depth = own.shape[1]
        n_outs = 1 if is_kv else 2
        return pl.pallas_call(
            functools.partial(project_kernel, n_out, TEAM * w_rows, step, starts, packed_rows, is_kv),
            out_shape=[shape((TEAM * rows // n_outs, width), bf16)] * n_outs,
            in_specs=[VMEM] * (7 + len(weight)),
            out_specs=[VMEM] * n_outs,
            scratch_shapes=[
                pltpu.VMEM((depth, width) if w_rows * TEAM % LANES else (ID_ROWS, LANES), bf16),
                pltpu.SemaphoreType.DMA((n_req * n_out,)),
            ],
            cost_estimate=pl.CostEstimate(
                flops=2 * TEAM * rows * depth * width, bytes_accessed=6 * MIB, transcendentals=0
            ),
            compiler_params=params(4 if w_rows * TEAM % LANES == 0 else 12),
            name="project_kv" if is_kv else "project_q",
        )(own, got[1], far, far_near, *weight, gain[None, :], cosine, sine)

    (made,) = project(kv_weight, True, k_gain)
    q_ox, q_oy, q_x = sync(q_ox, q_oy, q_x)
    q_od, q_d = in_req(q_oy, 1), in_req(q_x, 2)
    q_weight = [(q, 0, 0), (q_o, 0, 0), (w_x, 0, HD), (q_ox, 0, 0)]
    q_weight += [(w_y, 0, HD), (q_oy, 0, 0), (q_d, 0, 0), (q_od, 0, 0)]
    mine = [made] + [across(made, k) for k in range(1, n_out)]
    other = [in_team(part, 1) for part in mine]

    to_near, queries = project(q_weight, False, q_gain)
    from_near = in_team(to_near, 1)

    total = TEAM * rows * n_out
    store_mib = -(-2 * total * HD * 2 // MIB)
    page_shape = shape((slot_count, blk_rows, 2 * HD), bf16)
    own_pages, away_pages, store = pl.pallas_call(
        functools.partial(pages_kernel, n_out, blk_rows),
        out_shape=[page_shape, page_shape, shape((2, total, HD), bf16)],
        in_specs=[VMEM] * (2 * n_out + 2) + [SMEM] * 2,
        out_specs=[VMEM] * 3,
        scratch_shapes=[pltpu.SMEM((page_table.size,), jnp.int32)],
        cost_estimate=pl.CostEstimate(flops=0, bytes_accessed=4 * MIB, transcendentals=0),
        compiler_params=params(store_mib + 1),
        name="pages",
    )(*mine, *other, kv, kv_o, page_table, lengths)
    got_pages = in_team(away_pages, 2)

    def attend(step):
        return pl.pallas_call(
            functools.partial(attend_kernel, blk_rows, step),
            out_shape=shape((rows, H // 2 * HD), bf16),
            in_specs=[VMEM] * 4 + [SMEM],
            out_specs=VMEM,
            cost_estimate=pl.CostEstimate(
                flops=2 * H * HD * rows * total, bytes_accessed=4 * MIB, transcendentals=0
            ),
            compiler_params=params(store_mib + 2 + 3 * total // 1024),
            name="attend",
        )(store, queries, from_near, kv, lengths)

    from_far = in_team(attend(2), 2)
    kept = attend(0)

    attended, pages = pl.pallas_call(
        finish_kernel,
        out_shape=[shape((rows, H * HD), bf16), page_shape],
        in_specs=[ANY] * 4 + [SMEM],
        out_specs=[ANY] * 2,
        scratch_shapes=[pltpu.SMEM((page_table.size,), jnp.int32), pltpu.SemaphoreType.DMA((2 + slot_count,))],
        compiler_params=params(1),
        name="finish",
    )(kept, from_far, own_pages, got_pages, page_table)
    return attended[None], pages[None]


def solution(mesh):
    in_specs = (
        P("req", "blk", None),
        P("req", "blk"),
        P("req"),
        P("req", None, None),
        P(("req", "blk"), None),
        P(),
        P(),
    )
    out_specs = (P("req", "blk", None), P("req", "blk", None, None))
    return jax.shard_map(body, mesh=mesh, in_specs=in_specs, out_specs=out_specs, check_vma=False)
```

```python
import functools

import jax
import jax.numpy as jnp
import numpy as np
from jax import lax
from jax.experimental import pallas as pl
from jax.experimental.pallas import tpu as pltpu
from jax.sharding import PartitionSpec as P

H = 8
KVH = 2
HD = 256
TEAM = 4
ID_ROWS = 16
LANES = 128
ROPE_BASE = 1000000.0
NORM_EPS = 1e-06
MIB = 1024 * 1024

ANY = pl.BlockSpec(memory_space=pl.ANY)
VMEM = pl.BlockSpec(memory_space=pltpu.VMEM)
SMEM = pl.BlockSpec(memory_space=pltpu.SMEM)


def params(mib):
    return pltpu.CompilerParams(vmem_limit_bytes=mib * MIB)


def place():
    blk = lax.axis_index("blk")
    return lax.axis_index("req"), (blk // 2) % 2, blk % 2


def run(copies):
    for copy in copies:
        copy.start()
    for copy in copies:
        copy.wait()


def aligned(index, size):
    return pl.ds(pl.multiple_of(index * size, size), size)


def q_start(pair, core):
    return pl.multiple_of((pair * 2 + core) * 2 * HD, 2 * HD)


def kv_start(pair, core):
    return pl.multiple_of(H * HD + core * KVH * HD + pair * HD, HD)


def pack_kernel(w_hbm, ids_hbm, tokens_hbm, *refs):
    outs, (w_ref, ids_ref, tokens_ref, sems) = refs[:TEAM], refs[TEAM:]
    run([
        pltpu.make_async_copy(source, there, sems.at[n])
        for n, (source, there) in enumerate(((w_hbm, w_ref), (ids_hbm, ids_ref), (tokens_hbm, tokens_ref)))
    ])
    _, pair, core = place()
    member = pair * 2 + core
    rows = w_ref.shape[0]
    per_device = ids_ref.shape[1]
    lane = lax.broadcasted_iota(jnp.int32, (ID_ROWS, LANES), 1) - member * per_device
    ids = jnp.zeros((ID_ROWS, LANES), jnp.int32)
    for j in range(per_device):
        ids = jnp.where(lane == j, ids_ref[0, j], ids)
    ids = ids.astype(jnp.float32).astype(jnp.bfloat16)
    blocks = 3 * HD // LANES
    for k in range(TEAM):
        to_pair, to_core = pair ^ (k // 2), core ^ (k % 2)
        for n in range(blocks):
            if n < HD // LANES:
                start = pl.multiple_of(kv_start(to_pair, to_core) + n * LANES, LANES)
            else:
                start = pl.multiple_of(q_start(to_pair, to_core) + n * LANES - HD, LANES)
            outs[k][n * rows : (n + 1) * rows, :] = w_ref[:, pl.ds(start, LANES)]
        outs[k][blocks * rows : blocks * rows + ID_ROWS, :] = ids
    token_rows = tokens_ref.shape[0]
    for n in range(tokens_ref.shape[1] // LANES):
        first = blocks * rows + ID_ROWS + n * token_rows
        outs[1][first : first + token_rows, :] = tokens_ref[:, n * LANES : (n + 1) * LANES]


def read_id(piece, row, n):
    ids = piece[row : row + ID_ROWS, :LANES].astype(jnp.float32)[:1]
    lane = lax.broadcasted_iota(jnp.int32, ids.shape, 1)
    return jnp.sum(jnp.where(lane == n, ids, 0.0)).astype(jnp.int32)


def angle_kernel(piece, first_cos, first_sin, off_cos, off_sin, cos_out, sin_out):
    blk_rows = off_cos.shape[0]
    for n in range(cos_out.shape[0] // blk_rows):
        block = pl.ds(read_id(piece, piece.shape[0] - ID_ROWS, n), 1)
        here = slice(n * blk_rows, (n + 1) * blk_rows)
        cosine, sine = first_cos[block, :], first_sin[block, :]
        cos_out[here, :] = cosine * off_cos[...] - sine * off_sin[...]
        sin_out[here, :] = sine * off_cos[...] + cosine * off_sin[...]


def invert_table(table, flat_of):
    per_head = table.shape[2]
    for head in range(table.shape[1]):

        @pl.loop(0, per_head)
        def _(block):
            flat_of[table[0, head, block]] = head * per_head + block


def team_kernel(*refs):
    _, pair, core = place()
    parts, (kv_out, q_out, whole) = refs[:TEAM], refs[TEAM:]
    rows = q_out.shape[0] // TEAM
    member = pair * 2 + core
    for k in range(TEAM):
        here = aligned(member ^ k, rows)
        for n in range(3 * HD // LANES):
            out = kv_out if n < HD // LANES else q_out
            first = n * LANES if n < HD // LANES else n * LANES - HD
            part = parts[k][n * rows : (n + 1) * rows, :]
            out[here, first : first + LANES] = part
            whole[here, n * LANES : (n + 1) * LANES] = part
    first = 3 * HD // LANES * rows
    below = [part[first : first + ID_ROWS, :].astype(jnp.float32) for part in parts]
    ids = sum(below[1:], below[0]).astype(jnp.bfloat16)
    kv_out[TEAM * rows :, :] = jnp.concatenate([ids] * (HD // LANES), 1)


def regroup_kernel(kv_o, w_x, kv_out, q_out):
    rows = kv_o.shape[0]
    kv_out[:rows, :] = kv_o[...]
    kv_out[rows:, :] = w_x[:, :HD]
    q_out[...] = w_x[:, HD:]


def project_kernel(n_out, depth, tall, starts, first_row, is_kv, own, near, far, far_near, *refs):
    n_outs = 1 if is_kv else 2
    weights, (gain_ref, cos_ref, sin_ref) = refs[: -5 - n_outs], refs[-5 - n_outs : -2 - n_outs]
    outs, (w_all, sems) = refs[-2 - n_outs : -2], refs[-2:]
    req = lax.axis_index("req")
    outer = lax.axis_index("blk") // TEAM
    _, pair, core = place()
    member = pair * 2 + core
    rows = own.shape[0]
    width = outs[0].shape[1]
    direct = depth % LANES == 0
    places = []
    for i, piece in enumerate(weights):
        from_req = req ^ (i // 2)
        for n in range(n_out - 1 if i % 2 else 1):
            from_outer = lax.rem(outer + n_out - n - i % 2, n_out)
            row, column = starts[i]
            part = piece.at[pl.ds(row + n * tall, depth), column : column + width]
            places.append((part, from_req * n_out + from_outer))
    if not direct:
        run([
            pltpu.make_async_copy(piece, w_all.at[aligned(index, depth), :], sems.at[n])
            for n, (piece, index) in enumerate(places)
        ])
    half = HD // 2
    gain = gain_ref[...]
    if is_kv:
        gain = jnp.where(core == 0, gain, 1.0)
    for out, steps in zip(outs, [(0, 1, 2, 3)] if is_kv else [(1, 3), (0, 2)]):

        def token_rows(k, start, size):
            if k != 1:
                return (own, None, far, far_near)[k][:, pl.ds(start, size)]
            blocks = []
            for n in range(size // LANES):
                first = pl.multiple_of(first_row + (start // LANES + n) * rows, 16)
                blocks.append(near[pl.ds(first, rows), :])
            return jnp.concatenate(blocks, 1)

        def team_rows(start, size):
            return jnp.concatenate([token_rows(k, start, size) for k in steps], 0)

        cosine, sine = (
            jnp.concatenate([ref[aligned(member ^ k, rows), :] for k in steps], 0) for ref in (cos_ref, sin_ref)
        )
        if is_kv:
            cosine = jnp.where(core == 0, cosine, 1.0)
            sine = jnp.where(core == 0, sine, 0.0)
        if direct:
            product = 0.0
            for piece, index in places:
                x = team_rows(pl.multiple_of(index * depth, depth), depth)
                product += jnp.dot(x, piece[...], preferred_element_type=jnp.float32)
        else:
            product = jnp.dot(team_rows(0, w_all.shape[0]), w_all[...], preferred_element_type=jnp.float32)
        for h in range(out.shape[1] // HD):
            head = product[:, h * HD : (h + 1) * HD]
            mean = jnp.mean(head * head, axis=-1, keepdims=True)
            head = head * lax.rsqrt(mean + NORM_EPS) * gain
            front, second = head[:, :half], head[:, half:]
            turned = jnp.concatenate([front * cosine - second * sine, second * cosine + front * sine], 1)
            turned = turned.astype(jnp.bfloat16)
            for n, k in enumerate(steps):
                there = aligned(member ^ k if is_kv else n, rows)
                out[there, h * HD : (h + 1) * HD] = turned[n * rows : (n + 1) * rows]


def attend_kernel(blk_rows, step, store, q_ref, near_ref, piece, length_ref, out):
    _, pair, core = place()
    length = length_ref[0]
    rows = out.shape[0]
    member = (pair * 2 + core) ^ step
    total = store.shape[1]
    quarter = total // 4
    heads = 2 * (out.shape[1] // (2 * HD))
    first = step // 2 * rows
    for j in range(rows // blk_rows):
        block = read_id(piece, piece.shape[0] - ID_ROWS, member * (rows // blk_rows) + j)
        here = slice(first + j * blk_rows, first + (j + 1) * blk_rows)
        there = slice(j * blk_rows, (j + 1) * blk_rows)
        for variant in range(4):
            seen = (variant + 1) * quarter

            @pl.when((block * blk_rows) // quarter == variant)
            def _():
                queries = jnp.concatenate(
                    [ref[here, h * HD : (h + 1) * HD] for ref in (q_ref, near_ref) for h in range(heads // 2)], 0
                )
                shape = (heads * blk_rows, 1)
                query_pos = block * blk_rows + lax.rem(lax.broadcasted_iota(jnp.int32, shape, 0), blk_rows)
                limit = jnp.minimum(query_pos, length - 1)
                key_pos = lax.broadcasted_iota(jnp.int32, (1, seen), 1)
                scores = lax.dot_general(
                    queries,
                    store[0, :seen, :],
                    (((1,), (1,)), ((), ())),
                    preferred_element_type=jnp.float32,
                )
                scores = jnp.where(key_pos <= limit, scores, jnp.finfo(jnp.float32).min)
                weights = jnp.exp(scores - jnp.max(scores, axis=-1, keepdims=True))
                row_sum = jnp.sum(weights, axis=-1, keepdims=True)
                summed = jnp.dot(
                    weights.astype(jnp.bfloat16), store[1, :seen, :], preferred_element_type=jnp.float32
                )
                result = jnp.where(query_pos < length, summed / row_sum, 0.0).astype(jnp.bfloat16)
                for n in range(heads):
                    side = core if n < heads // 2 else 1 - core
                    column = side * (heads // 2) + n % (heads // 2)
                    out[there, aligned(column, HD)] = result[n * blk_rows : (n + 1) * blk_rows]


def live_page(store, table, flat_of, slot, length, blk_rows):
    block = lax.rem(flat_of[slot], table.shape[2])
    page = store[aligned(block, blk_rows), :]
    row = lax.broadcasted_iota(jnp.int32, page.shape, 0)
    return jnp.where(row < length - block * blk_rows, page, jnp.zeros_like(page))


def block_of(pieces, tall, k, j):
    piece, piece_o = pieces
    return read_id(piece_o, k * tall - ID_ROWS, j) if k else read_id(piece, tall - ID_ROWS, j)


def away_kernel(n_out, blk_rows, *refs):
    mine, (piece, piece_o, table, length_ref, away, store, flat_of) = refs[:n_out], refs[n_out:]
    per_piece = mine[0].shape[0] // blk_rows
    for k in range(n_out):
        for j in range(per_piece):
            there = aligned(block_of((piece, piece_o), piece.shape[0], k, j), blk_rows)
            store[there, :] = mine[k][j * blk_rows : (j + 1) * blk_rows, :]
    invert_table(table, flat_of)
    blk = lax.axis_index("blk")
    far = (blk ^ 2) - blk % 2
    slots = away.shape[0] // 2
    for i in range(2 * slots):
        away[i] = live_page(store, table, flat_of, far * slots + i, length_ref[0], blk_rows)


def sort_kernel(n_out, blk_rows, *refs):
    mine, other = refs[:n_out], refs[n_out : 2 * n_out]
    piece, piece_o, store = refs[2 * n_out :]
    _, _, core = place()
    per_piece = mine[0].shape[0] // blk_rows
    for k in range(n_out):
        for j in range(per_piece):
            there = aligned(block_of((piece, piece_o), piece.shape[0], k, j), blk_rows)
            here = slice(j * blk_rows, (j + 1) * blk_rows)
            store[core, there, :] = mine[k][here, :]
            store[1 - core, there, :] = other[k][here, :]


def own_kernel(blk_rows, store, table, length_ref, own, flat_of):
    invert_table(table, flat_of)
    slots = own.shape[0]
    for i in range(slots):
        for half in range(2):
            slot = lax.axis_index("blk") * slots + i
            page = live_page(store.at[half], table, flat_of, slot, length_ref[0], blk_rows)
            own[i, :, half * HD : (half + 1) * HD] = page


def finish_kernel(kept, from_far, own_pages, got, got_near, table, att_out, page_out, flat_of, sems):
    _, pair, core = place()
    invert_table(table, flat_of)
    slots = page_out.shape[0]
    width = kept.shape[1]
    copies = [
        pltpu.make_async_copy(kept, att_out.at[:, aligned(pair, width)], sems.at[0]),
        pltpu.make_async_copy(from_far, att_out.at[:, aligned(1 - pair, width)], sems.at[1]),
    ]
    for copy in copies:
        copy.start()
    for i in range(slots):
        here = lax.div(flat_of[lax.axis_index("blk") * slots + i], table.shape[2]) == pair
        for half in range(2):
            cols = aligned(core if half == 0 else 1 - core, HD)
            there = page_out.at[i, :, cols]
            sem = sems.at[2 + 2 * i + half]
            ours = pltpu.make_async_copy(own_pages.at[i, :, cols], there, sem)
            theirs = pltpu.make_async_copy((got, got_near)[half].at[core * slots + i], there, sem)
            copies.append(ours)

            @pl.when(here)
            def _():
                ours.start()

            @pl.when(jnp.logical_not(here))
            def _():
                theirs.start()

    for copy in copies:
        copy.wait()


def body(tokens, block_ids, lengths, page_table, qkv_weight, q_gain, k_gain):
    n_req, n_blk = lax.axis_size("req"), lax.axis_size("blk")
    n_out = n_blk // TEAM
    bf16 = jnp.bfloat16
    shape = jax.ShapeDtypeStruct
    blk = lax.axis_index("blk")
    member = blk % TEAM

    def in_team(array, k):
        return lax.ppermute(array, "blk", [(i, i ^ k) for i in range(n_blk)])

    def in_req(array, k):
        return lax.ppermute(array, "req", [(i, i ^ k) for i in range(n_req)])

    def across(array, k):
        return lax.ppermute(array, "blk", [(i, (i + TEAM * k) % n_blk) for i in range(n_blk)])

    def sync(*arrays):
        return lax.optimization_barrier(arrays)

    w_rows = qkv_weight.shape[0]
    per_device = block_ids.shape[1]
    own = tokens[0]
    rows = own.shape[0]
    packed_rows = 3 * HD // LANES * w_rows + ID_ROWS
    parts = pl.pallas_call(
        pack_kernel,
        out_shape=[
            shape((packed_rows + (own.size // LANES if k == 1 else 0), LANES), bf16) for k in range(TEAM)
        ],
        in_specs=[pl.BlockSpec(memory_space=pltpu.HBM)] * 3,
        out_specs=[VMEM] * TEAM,
        scratch_shapes=[
            pltpu.VMEM(qkv_weight.shape, bf16),
            pltpu.SMEM(block_ids.shape, jnp.int32),
            pltpu.VMEM(own.shape, bf16),
            pltpu.SemaphoreType.DMA((3,)),
        ],
        compiler_params=params(56),
        name="pack",
    )(qkv_weight, block_ids, own)
    got = [parts[0]] + [in_team(parts[k], k) for k in range(1, TEAM)]
    kv, q, w = pl.pallas_call(
        team_kernel,
        out_shape=[
            shape((TEAM * w_rows + ID_ROWS, HD), bf16),
            shape((TEAM * w_rows, 2 * HD), bf16),
            shape((TEAM * w_rows, 3 * HD), bf16),
        ],
        in_specs=[VMEM] * TEAM,
        out_specs=[VMEM] * 3,
        compiler_params=params(2),
        name="team",
    )(*got)

    def from_others(piece):
        got = [across(piece, k) for k in range(1, n_out)]
        return got[0] if len(got) == 1 else jnp.concatenate(got, 0)

    kv, q, w, own = sync(kv, q, w, own)
    kv_o, w_x, w_y = from_others(kv), in_req(w, 1), in_req(w, 2)
    q_o, far = from_others(q), in_team(own, 2)

    blk_rows = rows // per_device
    half = HD // 2
    inverse = np.float64(ROPE_BASE) ** (-2.0 * np.arange(half) / HD)
    tables = []
    for positions in (np.arange(per_device * n_blk) * blk_rows, np.arange(blk_rows)):
        angles = positions[:, None] * inverse[None, :]
        tables += [np.cos(angles).astype(np.float32), np.sin(angles).astype(np.float32)]
    cosine, sine = pl.pallas_call(
        angle_kernel,
        out_shape=[shape((TEAM * rows, half), jnp.float32)] * 2,
        in_specs=[VMEM] * 5,
        out_specs=[VMEM] * 2,
        cost_estimate=pl.CostEstimate(flops=10**10, bytes_accessed=40 * 10**6, transcendentals=0),
        compiler_params=params(2),
        name="angles",
    )(kv, *tables)
    slot_count = page_table.shape[1] * page_table.shape[2] // n_blk

    kv_o, w_x, w_y = sync(kv_o, w_x, w_y)
    others = kv_o.shape[0]
    kv_o_x, q_x = pl.pallas_call(
        regroup_kernel,
        out_shape=[shape((others + w_x.shape[0], HD), bf16), shape((w_x.shape[0], 2 * HD), bf16)],
        in_specs=[VMEM] * 2,
        out_specs=[VMEM] * 2,
        compiler_params=params(1),
        name="regroup",
    )(kv_o, w_x)
    kv_ox, kv_oy_d, kv_od = in_req(kv_o, 1), in_req(kv_o_x, 2), in_req(kv_o, 3)
    kv_ox, kv_oy_d, kv_od, q_o, far, cosine, sine = sync(kv_ox, kv_oy_d, kv_od, q_o, far, cosine, sine)
    far_near = in_team(far, 1)
    far_near, q_o = sync(far_near, q_o)
    q_ox, q_oy = in_req(q_o, 1), in_req(q_o, 2)
    kv_weight = [(kv, 0, 0), (kv_o, 0, 0), (w_x, 0, 0), (kv_ox, 0, 0)]
    kv_weight += [(w_y, 0, 0), (kv_oy_d, 0, 0), (kv_oy_d, others, 0), (kv_od, 0, 0)]

    def project(weight, is_kv, gain):
        starts = [part[1:] for part in weight]
        weight = [part[0] for part in weight]
        width = weight[1].shape[1]
        step = weight[1].shape[0] // (n_out - 1)
        depth = own.shape[1]
        n_outs = 1 if is_kv else 2
        return pl.pallas_call(
            functools.partial(project_kernel, n_out, TEAM * w_rows, step, starts, packed_rows, is_kv),
            out_shape=[shape((TEAM * rows // n_outs, width), bf16)] * n_outs,
            in_specs=[VMEM] * (7 + len(weight)),
            out_specs=[VMEM] * n_outs,
            scratch_shapes=[
                pltpu.VMEM((depth, width) if w_rows * TEAM % LANES else (ID_ROWS, LANES), bf16),
                pltpu.SemaphoreType.DMA((n_req * n_out,)),
            ],
            cost_estimate=pl.CostEstimate(
                flops=(0 if is_kv else 0), bytes_accessed=MIB, transcendentals=0
            ),
            compiler_params=params(4 if w_rows * TEAM % LANES == 0 else 12),
            name="project_kv" if is_kv else "project_q",
        )(own, got[1], far, far_near, *weight, gain[None, :], cosine, sine)

    (made,) = project(kv_weight, True, k_gain)
    q_ox, q_oy, q_x = sync(q_ox, q_oy, q_x)
    q_od, q_d = in_req(q_oy, 1), in_req(q_x, 2)
    q_weight = [(q, 0, 0), (q_o, 0, 0), (w_x, 0, HD), (q_ox, 0, 0)]
    q_weight += [(w_y, 0, HD), (q_oy, 0, 0), (q_d, 0, 0), (q_od, 0, 0)]
    mine = [made] + [across(made, k) for k in range(1, n_out)]
    other = [in_team(part, 1) for part in mine]

    to_near, queries = project(q_weight, False, q_gain)
    from_near = in_team(to_near, 1)

    total = TEAM * rows * n_out
    store_mib = -(-2 * total * HD * 2 // MIB)
    page_shape = shape((slot_count, blk_rows, 2 * HD), bf16)
    flat_of = pltpu.SMEM((page_table.size,), jnp.int32)
    away_half = pl.pallas_call(
        functools.partial(away_kernel, n_out, blk_rows),
        out_shape=shape((2 * slot_count, blk_rows, HD), bf16),
        in_specs=[VMEM] * (n_out + 2) + [SMEM] * 2,
        out_specs=VMEM,
        scratch_shapes=[pltpu.VMEM((total, HD), bf16), flat_of],
        cost_estimate=pl.CostEstimate(flops=0, bytes_accessed=MIB, transcendentals=0),
        compiler_params=params(store_mib + 1),
        name="away",
    )(*mine, kv, kv_o, page_table, lengths)
    got_half = in_team(away_half, 2)
    store = pl.pallas_call(
        functools.partial(sort_kernel, n_out, blk_rows),
        out_shape=shape((2, total, HD), bf16),
        in_specs=[VMEM] * (2 * n_out + 2),
        out_specs=VMEM,
        cost_estimate=pl.CostEstimate(flops=10**10, bytes_accessed=MIB, transcendentals=0),
        compiler_params=params(store_mib + 1),
        name="sort",
    )(*mine, *other, kv, kv_o)

    def attend(step):
        return pl.pallas_call(
            functools.partial(attend_kernel, blk_rows, step),
            out_shape=shape((rows, H // 2 * HD), bf16),
            in_specs=[VMEM] * 4 + [SMEM],
            out_specs=VMEM,
            cost_estimate=pl.CostEstimate(
                flops=0, bytes_accessed=MIB, transcendentals=0
            ),
            compiler_params=params(store_mib + 2 + 3 * total // 1024),
            name="attend",
        )(store, queries, from_near, kv, lengths)

    from_far = in_team(attend(2), 2)
    kept = attend(0)
    got_half, kept = sync(got_half, kept)
    got_near = in_team(got_half, 1)
    own_pages = pl.pallas_call(
        functools.partial(own_kernel, blk_rows),
        out_shape=page_shape,
        in_specs=[VMEM] + [SMEM] * 2,
        out_specs=VMEM,
        scratch_shapes=[flat_of],
        compiler_params=params(store_mib + 1),
        name="own",
    )(store, page_table, lengths)

    attended, pages = pl.pallas_call(
        finish_kernel,
        out_shape=[shape((rows, H * HD), bf16), page_shape],
        in_specs=[ANY] * 5 + [SMEM],
        out_specs=[ANY] * 2,
        scratch_shapes=[flat_of, pltpu.SemaphoreType.DMA((2 + 2 * slot_count,))],
        compiler_params=params(1),
        name="finish",
    )(kept, from_far, own_pages, got_half, got_near, page_table)
    return attended[None], pages[None]


def solution(mesh):
    in_specs = (
        P("req", "blk", None),
        P("req", "blk"),
        P("req"),
        P("req", None, None),
        P(("req", "blk"), None),
        P(),
        P(),
    )
    out_specs = (P("req", "blk", None), P("req", "blk", None, None))
    return jax.shard_map(body, mesh=mesh, in_specs=in_specs, out_specs=out_specs, check_vma=False)
```

```python
import functools

import jax
import jax.numpy as jnp
import numpy as np
from jax import lax
from jax.experimental import pallas as pl
from jax.experimental.pallas import tpu as pltpu
from jax.sharding import PartitionSpec as P

H = 8
KVH = 2
HD = 256
TEAM = 4
ID_ROWS = 16
LANES = 128
ROPE_BASE = 1000000.0
NORM_EPS = 1e-06
MIB = 1024 * 1024

ANY = pl.BlockSpec(memory_space=pl.ANY)
VMEM = pl.BlockSpec(memory_space=pltpu.VMEM)
SMEM = pl.BlockSpec(memory_space=pltpu.SMEM)


def params(mib):
    return pltpu.CompilerParams(vmem_limit_bytes=mib * MIB)


def place():
    blk = lax.axis_index("blk")
    return lax.axis_index("req"), (blk // 2) % 2, blk % 2


def run(copies):
    for copy in copies:
        copy.start()
    for copy in copies:
        copy.wait()


def aligned(index, size):
    return pl.ds(pl.multiple_of(index * size, size), size)


def q_start(pair, core):
    return pl.multiple_of((pair * 2 + core) * 2 * HD, 2 * HD)


def kv_start(pair, core):
    return pl.multiple_of(H * HD + core * KVH * HD + pair * HD, HD)


def pack_kernel(w_hbm, ids_hbm, tokens_hbm, *refs):
    outs, (w_ref, ids_ref, tokens_ref, sems) = refs[:TEAM], refs[TEAM:]
    run([
        pltpu.make_async_copy(source, there, sems.at[n])
        for n, (source, there) in enumerate(((w_hbm, w_ref), (ids_hbm, ids_ref), (tokens_hbm, tokens_ref)))
    ])
    _, pair, core = place()
    member = pair * 2 + core
    rows = w_ref.shape[0]
    per_device = ids_ref.shape[1]
    lane = lax.broadcasted_iota(jnp.int32, (ID_ROWS, LANES), 1) - member * per_device
    ids = jnp.zeros((ID_ROWS, LANES), jnp.int32)
    for j in range(per_device):
        ids = jnp.where(lane == j, ids_ref[0, j], ids)
    ids = ids.astype(jnp.float32).astype(jnp.bfloat16)
    blocks = 3 * HD // LANES
    for k in range(TEAM):
        to_pair, to_core = pair ^ (k // 2), core ^ (k % 2)
        for n in range(blocks):
            if n < HD // LANES:
                start = pl.multiple_of(kv_start(to_pair, to_core) + n * LANES, LANES)
            else:
                start = pl.multiple_of(q_start(to_pair, to_core) + n * LANES - HD, LANES)
            outs[k][n * rows : (n + 1) * rows, :] = w_ref[:, pl.ds(start, LANES)]
        outs[k][blocks * rows : blocks * rows + ID_ROWS, :] = ids
    token_rows = tokens_ref.shape[0]
    for n in range(tokens_ref.shape[1] // LANES):
        first = blocks * rows + ID_ROWS + n * token_rows
        outs[1][first : first + token_rows, :] = tokens_ref[:, n * LANES : (n + 1) * LANES]


def read_id(piece, row, n):
    ids = piece[row : row + ID_ROWS, :LANES].astype(jnp.float32)[:1]
    if isinstance(n, int):
        return ids[0, n].astype(jnp.int32)
    lane = lax.broadcasted_iota(jnp.int32, ids.shape, 1)
    return jnp.sum(jnp.where(lane == n, ids, 0.0)).astype(jnp.int32)


def angle_kernel(piece, first_cos, first_sin, off_cos, off_sin, cos_out, sin_out):
    blk_rows = off_cos.shape[0]
    for n in range(cos_out.shape[0] // blk_rows):
        block = pl.ds(read_id(piece, piece.shape[0] - ID_ROWS, n), 1)
        here = slice(n * blk_rows, (n + 1) * blk_rows)
        cosine, sine = first_cos[block, :], first_sin[block, :]
        cos_out[here, :] = cosine * off_cos[...] - sine * off_sin[...]
        sin_out[here, :] = sine * off_cos[...] + cosine * off_sin[...]


def invert_table(table, flat_of):
    per_head = table.shape[2]
    for head in range(table.shape[1]):

        @pl.loop(0, per_head)
        def _(block):
            flat_of[table[0, head, block]] = head * per_head + block


def team_kernel(*refs):
    _, pair, core = place()
    parts, (kv_out, q_out, whole) = refs[:TEAM], refs[TEAM:]
    rows = q_out.shape[0] // TEAM
    member = pair * 2 + core
    for k in range(TEAM):
        here = aligned(member ^ k, rows)
        for n in range(3 * HD // LANES):
            out = kv_out if n < HD // LANES else q_out
            first = n * LANES if n < HD // LANES else n * LANES - HD
            part = parts[k][n * rows : (n + 1) * rows, :]
            out[here, first : first + LANES] = part
            whole[here, n * LANES : (n + 1) * LANES] = part
    first = 3 * HD // LANES * rows
    below = [part[first : first + ID_ROWS, :].astype(jnp.float32) for part in parts]
    ids = sum(below[1:], below[0]).astype(jnp.bfloat16)
    kv_out[TEAM * rows :, :] = jnp.concatenate([ids] * (HD // LANES), 1)


def regroup_kernel(kv_o, w_x, kv_out, q_out):
    rows = kv_o.shape[0]
    kv_out[:rows, :] = kv_o[...]
    kv_out[rows:, :] = w_x[:, :HD]
    q_out[...] = w_x[:, HD:]


def project_kernel(n_out, depth, tall, starts, first_row, is_kv, own, near, far, far_near, *refs):
    n_outs = 1 if is_kv else 2
    weights, (gain_ref, cos_ref, sin_ref) = refs[: -5 - n_outs], refs[-5 - n_outs : -2 - n_outs]
    outs, (w_all, sems) = refs[-2 - n_outs : -2], refs[-2:]
    req = lax.axis_index("req")
    outer = lax.axis_index("blk") // TEAM
    _, pair, core = place()
    member = pair * 2 + core
    rows = own.shape[0]
    width = outs[0].shape[1]
    direct = depth % LANES == 0
    places = []
    for i, piece in enumerate(weights):
        from_req = req ^ (i // 2)
        for n in range(n_out - 1 if i % 2 else 1):
            from_outer = lax.rem(outer + n_out - n - i % 2, n_out)
            row, column = starts[i]
            part = piece.at[pl.ds(row + n * tall, depth), column : column + width]
            places.append((part, from_req * n_out + from_outer))
    if not direct:
        run([
            pltpu.make_async_copy(piece, w_all.at[aligned(index, depth), :], sems.at[n])
            for n, (piece, index) in enumerate(places)
        ])
    half = HD // 2
    gain = gain_ref[...]
    if is_kv:
        gain = jnp.where(core == 0, gain, 1.0)
    for out, steps in zip(outs, [(0, 1, 2, 3)] if is_kv else [(1, 3), (0, 2)]):

        def token_rows(k, start, size):
            if k != 1:
                return (own, None, far, far_near)[k][:, pl.ds(start, size)]
            blocks = []
            for n in range(size // LANES):
                first = pl.multiple_of(first_row + (start // LANES + n) * rows, 16)
                blocks.append(near[pl.ds(first, rows), :])
            return jnp.concatenate(blocks, 1)

        def team_rows(start, size):
            return jnp.concatenate([token_rows(k, start, size) for k in steps], 0)

        cosine, sine = (
            jnp.concatenate([ref[aligned(member ^ k, rows), :] for k in steps], 0) for ref in (cos_ref, sin_ref)
        )
        if is_kv:
            cosine = jnp.where(core == 0, cosine, 1.0)
            sine = jnp.where(core == 0, sine, 0.0)
        if direct:
            product = 0.0
            for piece, index in places:
                x = team_rows(pl.multiple_of(index * depth, depth), depth)
                product += jnp.dot(x, piece[...], preferred_element_type=jnp.float32)
        else:
            product = jnp.dot(team_rows(0, w_all.shape[0]), w_all[...], preferred_element_type=jnp.float32)
        for h in range(out.shape[1] // HD):
            head = product[:, h * HD : (h + 1) * HD]
            mean = jnp.mean(head * head, axis=-1, keepdims=True)
            head = head * lax.rsqrt(mean + NORM_EPS) * gain
            front, second = head[:, :half], head[:, half:]
            turned = jnp.concatenate([front * cosine - second * sine, second * cosine + front * sine], 1)
            turned = turned.astype(jnp.bfloat16)
            for n, k in enumerate(steps):
                there = aligned(member ^ k if is_kv else n, rows)
                out[there, h * HD : (h + 1) * HD] = turned[n * rows : (n + 1) * rows]


def attend_kernel(blk_rows, step, store, q_ref, near_ref, piece, length_ref, out):
    _, pair, core = place()
    length = length_ref[0]
    rows = out.shape[0]
    member = (pair * 2 + core) ^ step
    total = store.shape[1]
    quarter = total // 4
    heads = 2 * (out.shape[1] // (2 * HD))
    first = step // 2 * rows
    for j in range(rows // blk_rows):
        block = read_id(piece, piece.shape[0] - ID_ROWS, member * (rows // blk_rows) + j)
        here = slice(first + j * blk_rows, first + (j + 1) * blk_rows)
        there = slice(j * blk_rows, (j + 1) * blk_rows)
        for variant in range(4):
            seen = (variant + 1) * quarter

            @pl.when((block * blk_rows) // quarter == variant)
            def _():
                queries = jnp.concatenate(
                    [ref[here, h * HD : (h + 1) * HD] for ref in (q_ref, near_ref) for h in range(heads // 2)], 0
                )
                shape = (heads * blk_rows, 1)
                query_pos = block * blk_rows + lax.rem(lax.broadcasted_iota(jnp.int32, shape, 0), blk_rows)
                limit = jnp.minimum(query_pos, length - 1)
                key_pos = lax.broadcasted_iota(jnp.int32, (1, seen), 1)
                scores = lax.dot_general(
                    queries,
                    store[0, :seen, :],
                    (((1,), (1,)), ((), ())),
                    preferred_element_type=jnp.float32,
                )
                scores = jnp.where(key_pos <= limit, scores, jnp.finfo(jnp.float32).min)
                weights = jnp.exp(scores - jnp.max(scores, axis=-1, keepdims=True))
                row_sum = jnp.sum(weights, axis=-1, keepdims=True)
                summed = jnp.dot(
                    weights.astype(jnp.bfloat16), store[1, :seen, :], preferred_element_type=jnp.float32
                )
                result = jnp.where(query_pos < length, summed / row_sum, 0.0).astype(jnp.bfloat16)
                for n in range(heads):
                    side = core if n < heads // 2 else 1 - core
                    column = side * (heads // 2) + n % (heads // 2)
                    out[there, aligned(column, HD)] = result[n * blk_rows : (n + 1) * blk_rows]


def live_page(store, table, flat_of, slot, length, blk_rows):
    block = lax.rem(flat_of[slot], table.shape[2])
    page = store[aligned(block, blk_rows), :]
    row = lax.broadcasted_iota(jnp.int32, page.shape, 0)
    return jnp.where(row < length - block * blk_rows, page, jnp.zeros_like(page))


def block_of(pieces, tall, k, j):
    piece, piece_o = pieces
    return read_id(piece_o, k * tall - ID_ROWS, j) if k else read_id(piece, tall - ID_ROWS, j)


def away_kernel(n_out, blk_rows, *refs):
    mine, (piece, piece_o, table, length_ref, away, store, flat_of) = refs[:n_out], refs[n_out:]
    per_piece = mine[0].shape[0] // blk_rows
    for k in range(n_out):
        for j in range(per_piece):
            there = aligned(block_of((piece, piece_o), piece.shape[0], k, j), blk_rows)
            store[there, :] = mine[k][j * blk_rows : (j + 1) * blk_rows, :]
    invert_table(table, flat_of)
    blk = lax.axis_index("blk")
    far = (blk ^ 2) - blk % 2
    slots = away.shape[0] // 2
    for i in range(2 * slots):
        away[i] = live_page(store, table, flat_of, far * slots + i, length_ref[0], blk_rows)


def sort_kernel(n_out, blk_rows, *refs):
    mine, other = refs[:n_out], refs[n_out : 2 * n_out]
    piece, piece_o, store = refs[2 * n_out :]
    _, _, core = place()
    per_piece = mine[0].shape[0] // blk_rows
    for k in range(n_out):
        for j in range(per_piece):
            there = aligned(block_of((piece, piece_o), piece.shape[0], k, j), blk_rows)
            here = slice(j * blk_rows, (j + 1) * blk_rows)
            store[core, there, :] = mine[k][here, :]
            store[1 - core, there, :] = other[k][here, :]


def own_kernel(blk_rows, store, table, length_ref, own, flat_of):
    invert_table(table, flat_of)
    slots = own.shape[0]
    for i in range(slots):
        for half in range(2):
            slot = lax.axis_index("blk") * slots + i
            page = live_page(store.at[half], table, flat_of, slot, length_ref[0], blk_rows)
            own[i, :, half * HD : (half + 1) * HD] = page


def finish_kernel(kept, from_far, own_pages, got, got_near, table, att_out, page_out, flat_of, sems):
    _, pair, core = place()
    invert_table(table, flat_of)
    slots = page_out.shape[0]
    width = kept.shape[1]
    copies = [
        pltpu.make_async_copy(kept, att_out.at[:, aligned(pair, width)], sems.at[0]),
        pltpu.make_async_copy(from_far, att_out.at[:, aligned(1 - pair, width)], sems.at[1]),
    ]
    for copy in copies:
        copy.start()
    for i in range(slots):
        here = lax.div(flat_of[lax.axis_index("blk") * slots + i], table.shape[2]) == pair
        for half in range(2):
            cols = aligned(core if half == 0 else 1 - core, HD)
            there = page_out.at[i, :, cols]
            sem = sems.at[2 + 2 * i + half]
            ours = pltpu.make_async_copy(own_pages.at[i, :, cols], there, sem)
            theirs = pltpu.make_async_copy((got, got_near)[half].at[core * slots + i], there, sem)
            copies.append(ours)

            @pl.when(here)
            def _():
                ours.start()

            @pl.when(jnp.logical_not(here))
            def _():
                theirs.start()

    for copy in copies:
        copy.wait()


def body(tokens, block_ids, lengths, page_table, qkv_weight, q_gain, k_gain):
    n_req, n_blk = lax.axis_size("req"), lax.axis_size("blk")
    n_out = n_blk // TEAM
    bf16 = jnp.bfloat16
    shape = jax.ShapeDtypeStruct
    blk = lax.axis_index("blk")
    member = blk % TEAM

    def in_team(array, k):
        return lax.ppermute(array, "blk", [(i, i ^ k) for i in range(n_blk)])

    def in_req(array, k):
        return lax.ppermute(array, "req", [(i, i ^ k) for i in range(n_req)])

    def across(array, k):
        return lax.ppermute(array, "blk", [(i, (i + TEAM * k) % n_blk) for i in range(n_blk)])

    def sync(*arrays):
        return lax.optimization_barrier(arrays)

    w_rows = qkv_weight.shape[0]
    per_device = block_ids.shape[1]
    own = tokens[0]
    rows = own.shape[0]
    packed_rows = 3 * HD // LANES * w_rows + ID_ROWS
    parts = pl.pallas_call(
        pack_kernel,
        out_shape=[
            shape((packed_rows + (own.size // LANES if k == 1 else 0), LANES), bf16) for k in range(TEAM)
        ],
        in_specs=[pl.BlockSpec(memory_space=pltpu.HBM)] * 3,
        out_specs=[VMEM] * TEAM,
        scratch_shapes=[
            pltpu.VMEM(qkv_weight.shape, bf16),
            pltpu.SMEM(block_ids.shape, jnp.int32),
            pltpu.VMEM(own.shape, bf16),
            pltpu.SemaphoreType.DMA((3,)),
        ],
        compiler_params=params(56),
        name="pack",
    )(qkv_weight, block_ids, own)
    got = [parts[0]] + [in_team(parts[k], k) for k in range(1, TEAM)]
    kv, q, w = pl.pallas_call(
        team_kernel,
        out_shape=[
            shape((TEAM * w_rows + ID_ROWS, HD), bf16),
            shape((TEAM * w_rows, 2 * HD), bf16),
            shape((TEAM * w_rows, 3 * HD), bf16),
        ],
        in_specs=[VMEM] * TEAM,
        out_specs=[VMEM] * 3,
        compiler_params=params(2),
        name="team",
    )(*got)

    def from_others(piece):
        got = [across(piece, k) for k in range(1, n_out)]
        return got[0] if len(got) == 1 else jnp.concatenate(got, 0)

    kv, q, w, own = sync(kv, q, w, own)
    kv_o, w_x, w_y = from_others(kv), in_req(w, 1), in_req(w, 2)
    q_o, far = from_others(q), in_team(own, 2)

    blk_rows = rows // per_device
    half = HD // 2
    inverse = np.float64(ROPE_BASE) ** (-2.0 * np.arange(half) / HD)
    tables = []
    for positions in (np.arange(per_device * n_blk) * blk_rows, np.arange(blk_rows)):
        angles = positions[:, None] * inverse[None, :]
        tables += [np.cos(angles).astype(np.float32), np.sin(angles).astype(np.float32)]
    cosine, sine = pl.pallas_call(
        angle_kernel,
        out_shape=[shape((TEAM * rows, half), jnp.float32)] * 2,
        in_specs=[VMEM] * 5,
        out_specs=[VMEM] * 2,
        cost_estimate=pl.CostEstimate(flops=10**10, bytes_accessed=40 * 10**6, transcendentals=0),
        compiler_params=params(2),
        name="angles",
    )(kv, *tables)
    slot_count = page_table.shape[1] * page_table.shape[2] // n_blk

    kv_o, w_x, w_y = sync(kv_o, w_x, w_y)
    others = kv_o.shape[0]
    kv_o_x, q_x = pl.pallas_call(
        regroup_kernel,
        out_shape=[shape((others + w_x.shape[0], HD), bf16), shape((w_x.shape[0], 2 * HD), bf16)],
        in_specs=[VMEM] * 2,
        out_specs=[VMEM] * 2,
        compiler_params=params(1),
        name="regroup",
    )(kv_o, w_x)
    kv_ox, kv_oy_d, kv_od = in_req(kv_o, 1), in_req(kv_o_x, 2), in_req(kv_o, 3)
    kv_ox, kv_oy_d, kv_od, q_o, far, cosine, sine = sync(kv_ox, kv_oy_d, kv_od, q_o, far, cosine, sine)
    far_near = in_team(far, 1)
    q_ox, q_oy = in_req(q_o, 1), in_req(q_o, 2)
    kv_weight = [(kv, 0, 0), (kv_o, 0, 0), (w_x, 0, 0), (kv_ox, 0, 0)]
    kv_weight += [(w_y, 0, 0), (kv_oy_d, 0, 0), (kv_oy_d, others, 0), (kv_od, 0, 0)]

    def project(weight, is_kv, gain):
        starts = [part[1:] for part in weight]
        weight = [part[0] for part in weight]
        width = weight[1].shape[1]
        step = weight[1].shape[0] // (n_out - 1)
        depth = own.shape[1]
        n_outs = 1 if is_kv else 2
        return pl.pallas_call(
            functools.partial(project_kernel, n_out, TEAM * w_rows, step, starts, packed_rows, is_kv),
            out_shape=[shape((TEAM * rows // n_outs, width), bf16)] * n_outs,
            in_specs=[VMEM] * (7 + len(weight)),
            out_specs=[VMEM] * n_outs,
            scratch_shapes=[
                pltpu.VMEM((depth, width) if w_rows * TEAM % LANES else (ID_ROWS, LANES), bf16),
                pltpu.SemaphoreType.DMA((n_req * n_out,)),
            ],
            cost_estimate=pl.CostEstimate(
                flops=(0 if is_kv else 0), bytes_accessed=MIB, transcendentals=0
            ),
            compiler_params=params(4 if w_rows * TEAM % LANES == 0 else 12),
            name="project_kv" if is_kv else "project_q",
        )(own, got[1], far, far_near, *weight, gain[None, :], cosine, sine)

    (made,) = project(kv_weight, True, k_gain)
    q_ox, q_oy, q_x = sync(q_ox, q_oy, q_x)
    q_od, q_d = in_req(q_oy, 1), in_req(q_x, 2)
    q_weight = [(q, 0, 0), (q_o, 0, 0), (w_x, 0, HD), (q_ox, 0, 0)]
    q_weight += [(w_y, 0, HD), (q_oy, 0, 0), (q_d, 0, 0), (q_od, 0, 0)]
    mine = [made] + [across(made, k) for k in range(1, n_out)]
    other = [in_team(part, 1) for part in mine]

    total = TEAM * rows * n_out
    store_mib = -(-2 * total * HD * 2 // MIB)
    page_shape = shape((slot_count, blk_rows, 2 * HD), bf16)
    flat_of = pltpu.SMEM((page_table.size,), jnp.int32)
    away_half = pl.pallas_call(
        functools.partial(away_kernel, n_out, blk_rows),
        out_shape=shape((2 * slot_count, blk_rows, HD), bf16),
        in_specs=[VMEM] * (n_out + 2) + [SMEM] * 2,
        out_specs=VMEM,
        scratch_shapes=[pltpu.VMEM((total, HD), bf16), flat_of],
        cost_estimate=pl.CostEstimate(flops=0, bytes_accessed=MIB, transcendentals=0),
        compiler_params=params(store_mib + 1),
        name="away",
    )(*mine, kv, kv_o, page_table, lengths)
    got_half = in_team(away_half, 2)
    away_half, q_od, q_d = sync(away_half, q_od, q_d)
    q_weight[-2:] = [(q_d, 0, 0), (q_od, 0, 0)]

    to_near, queries = project(q_weight, False, q_gain)
    from_near = in_team(to_near, 1)

    store = pl.pallas_call(
        functools.partial(sort_kernel, n_out, blk_rows),
        out_shape=shape((2, total, HD), bf16),
        in_specs=[VMEM] * (2 * n_out + 2),
        out_specs=VMEM,
        cost_estimate=pl.CostEstimate(flops=10**10, bytes_accessed=MIB, transcendentals=0),
        compiler_params=params(store_mib + 1),
        name="sort",
    )(*mine, *other, kv, kv_o)

    def attend(step):
        return pl.pallas_call(
            functools.partial(attend_kernel, blk_rows, step),
            out_shape=shape((rows, H // 2 * HD), bf16),
            in_specs=[VMEM] * 4 + [SMEM],
            out_specs=VMEM,
            cost_estimate=pl.CostEstimate(
                flops=0, bytes_accessed=MIB, transcendentals=0
            ),
            compiler_params=params(store_mib + 2 + 3 * total // 1024),
            name="attend",
        )(store, queries, from_near, kv, lengths)

    from_far = in_team(attend(2), 2)
    kept = attend(0)
    got_half, kept = sync(got_half, kept)
    got_near = in_team(got_half, 1)
    own_pages = pl.pallas_call(
        functools.partial(own_kernel, blk_rows),
        out_shape=page_shape,
        in_specs=[VMEM] + [SMEM] * 2,
        out_specs=VMEM,
        scratch_shapes=[flat_of],
        compiler_params=params(store_mib + 1),
        name="own",
    )(store, page_table, lengths)

    attended, pages = pl.pallas_call(
        finish_kernel,
        out_shape=[shape((rows, H * HD), bf16), page_shape],
        in_specs=[ANY] * 5 + [SMEM],
        out_specs=[ANY] * 2,
        scratch_shapes=[flat_of, pltpu.SemaphoreType.DMA((2 + 2 * slot_count,))],
        compiler_params=params(1),
        name="finish",
    )(kept, from_far, own_pages, got_half, got_near, page_table)
    return attended[None], pages[None]


def solution(mesh):
    in_specs = (
        P("req", "blk", None),
        P("req", "blk"),
        P("req"),
        P("req", None, None),
        P(("req", "blk"), None),
        P(),
        P(),
    )
    out_specs = (P("req", "blk", None), P("req", "blk", None, None))
    return jax.shard_map(body, mesh=mesh, in_specs=in_specs, out_specs=out_specs, check_vma=False)
```

```python
import functools

import jax
import jax.numpy as jnp
import numpy as np
from jax import lax
from jax.experimental import pallas as pl
from jax.experimental.pallas import tpu as pltpu
from jax.sharding import PartitionSpec as P

H = 8
KVH = 2
HD = 256
TEAM = 4
ID_ROWS = 16
LANES = 128
ROPE_BASE = 1000000.0
NORM_EPS = 1e-06
MIB = 1024 * 1024

ANY = pl.BlockSpec(memory_space=pl.ANY)
VMEM = pl.BlockSpec(memory_space=pltpu.VMEM)
SMEM = pl.BlockSpec(memory_space=pltpu.SMEM)


def params(mib):
    return pltpu.CompilerParams(vmem_limit_bytes=mib * MIB)


def place():
    blk = lax.axis_index("blk")
    return lax.axis_index("req"), (blk // 2) % 2, blk % 2


def run(copies):
    for copy in copies:
        copy.start()
    for copy in copies:
        copy.wait()


def aligned(index, size):
    return pl.ds(pl.multiple_of(index * size, size), size)


def q_start(pair, core):
    return pl.multiple_of((pair * 2 + core) * 2 * HD, 2 * HD)


def kv_start(pair, core):
    return pl.multiple_of(H * HD + core * KVH * HD + pair * HD, HD)


def pack_kernel(w_hbm, ids_hbm, tokens_hbm, *refs):
    outs, (w_ref, ids_ref, tokens_ref, sems) = refs[:TEAM], refs[TEAM:]
    run([
        pltpu.make_async_copy(source, there, sems.at[n])
        for n, (source, there) in enumerate(((w_hbm, w_ref), (ids_hbm, ids_ref), (tokens_hbm, tokens_ref)))
    ])
    _, pair, core = place()
    member = pair * 2 + core
    rows = w_ref.shape[0]
    per_device = ids_ref.shape[1]
    lane = lax.broadcasted_iota(jnp.int32, (ID_ROWS, LANES), 1) - member * per_device
    ids = jnp.zeros((ID_ROWS, LANES), jnp.int32)
    for j in range(per_device):
        ids = jnp.where(lane == j, ids_ref[0, j], ids)
    ids = ids.astype(jnp.float32).astype(jnp.bfloat16)
    blocks = 3 * HD // LANES
    for k in range(TEAM):
        to_pair, to_core = pair ^ (k // 2), core ^ (k % 2)
        for n in range(blocks):
            if n < HD // LANES:
                start = pl.multiple_of(kv_start(to_pair, to_core) + n * LANES, LANES)
            else:
                start = pl.multiple_of(q_start(to_pair, to_core) + n * LANES - HD, LANES)
            outs[k][n * rows : (n + 1) * rows, :] = w_ref[:, pl.ds(start, LANES)]
        outs[k][blocks * rows : blocks * rows + ID_ROWS, :] = ids
    token_rows = tokens_ref.shape[0]
    for n in range(tokens_ref.shape[1] // LANES):
        first = blocks * rows + ID_ROWS + n * token_rows
        outs[1][first : first + token_rows, :] = tokens_ref[:, n * LANES : (n + 1) * LANES]


def read_id(piece, row, n):
    ids = piece[row : row + ID_ROWS, :LANES].astype(jnp.float32)[:1]
    if isinstance(n, int):
        return ids[0, n].astype(jnp.int32)
    lane = lax.broadcasted_iota(jnp.int32, ids.shape, 1)
    return jnp.sum(jnp.where(lane == n, ids, 0.0)).astype(jnp.int32)


def angle_kernel(piece, first_cos, first_sin, off_cos, off_sin, cos_out, sin_out):
    blk_rows = off_cos.shape[0]
    for n in range(cos_out.shape[0] // blk_rows):
        block = pl.ds(read_id(piece, piece.shape[0] - ID_ROWS, n), 1)
        here = slice(n * blk_rows, (n + 1) * blk_rows)
        cosine, sine = first_cos[block, :], first_sin[block, :]
        cos_out[here, :] = cosine * off_cos[...] - sine * off_sin[...]
        sin_out[here, :] = sine * off_cos[...] + cosine * off_sin[...]


def invert_table(table, flat_of):
    per_head = table.shape[2]
    for head in range(table.shape[1]):

        @pl.loop(0, per_head)
        def _(block):
            flat_of[table[0, head, block]] = head * per_head + block


def keep_kernel(part, out):
    out[...] = part[...]


def team_kernel(*refs):
    _, pair, core = place()
    parts, (kv_out, q_out, whole) = refs[:TEAM], refs[TEAM:]
    rows = q_out.shape[0] // TEAM
    member = pair * 2 + core
    for k in range(TEAM):
        here = aligned(member ^ k, rows)
        for n in range(3 * HD // LANES):
            out = kv_out if n < HD // LANES else q_out
            first = n * LANES if n < HD // LANES else n * LANES - HD
            part = parts[k][n * rows : (n + 1) * rows, :]
            out[here, first : first + LANES] = part
            whole[here, n * LANES : (n + 1) * LANES] = part
    first = 3 * HD // LANES * rows
    below = [part[first : first + ID_ROWS, :].astype(jnp.float32) for part in parts]
    ids = sum(below[1:], below[0]).astype(jnp.bfloat16)
    kv_out[TEAM * rows :, :] = jnp.concatenate([ids] * (HD // LANES), 1)


def regroup_kernel(kv_o, w_x, kv_out, q_out):
    rows = kv_o.shape[0]
    kv_out[:rows, :] = kv_o[...]
    kv_out[rows:, :] = w_x[:, :HD]
    q_out[...] = w_x[:, HD:]


def project_kernel(n_out, depth, tall, starts, first_row, is_kv, own, near, far, far_near, *refs):
    n_outs = 1 if is_kv else 2
    weights, (gain_ref, cos_ref, sin_ref) = refs[: -5 - n_outs], refs[-5 - n_outs : -2 - n_outs]
    outs, (w_all, sems) = refs[-2 - n_outs : -2], refs[-2:]
    req = lax.axis_index("req")
    outer = lax.axis_index("blk") // TEAM
    _, pair, core = place()
    member = pair * 2 + core
    rows = own.shape[0]
    width = outs[0].shape[1]
    direct = depth % LANES == 0
    places = []
    for i, piece in enumerate(weights):
        from_req = req ^ (i // 2)
        for n in range(n_out - 1 if i % 2 else 1):
            from_outer = lax.rem(outer + n_out - n - i % 2, n_out)
            row, column = starts[i]
            part = piece.at[pl.ds(row + n * tall, depth), column : column + width]
            places.append((part, from_req * n_out + from_outer))
    if not direct:
        run([
            pltpu.make_async_copy(piece, w_all.at[aligned(index, depth), :], sems.at[n])
            for n, (piece, index) in enumerate(places)
        ])
    half = HD // 2
    gain = gain_ref[...]
    if is_kv:
        gain = jnp.where(core == 0, gain, 1.0)
    for out, steps in zip(outs, [(0, 1, 2, 3)] if is_kv else [(1, 3), (0, 2)]):

        def token_rows(k, start, size):
            if k != 1:
                return (own, None, far, far_near)[k][:, pl.ds(start, size)]
            blocks = []
            for n in range(size // LANES):
                first = pl.multiple_of(first_row + (start // LANES + n) * rows, 16)
                blocks.append(near[pl.ds(first, rows), :])
            return jnp.concatenate(blocks, 1)

        def team_rows(start, size):
            return jnp.concatenate([token_rows(k, start, size) for k in steps], 0)

        cosine, sine = (
            jnp.concatenate([ref[aligned(member ^ k, rows), :] for k in steps], 0) for ref in (cos_ref, sin_ref)
        )
        if is_kv:
            cosine = jnp.where(core == 0, cosine, 1.0)
            sine = jnp.where(core == 0, sine, 0.0)
        if direct:
            product = 0.0
            for piece, index in places:
                x = team_rows(pl.multiple_of(index * depth, depth), depth)
                product += jnp.dot(x, piece[...], preferred_element_type=jnp.float32)
        else:
            product = jnp.dot(team_rows(0, w_all.shape[0]), w_all[...], preferred_element_type=jnp.float32)
        for h in range(out.shape[1] // HD):
            head = product[:, h * HD : (h + 1) * HD]
            mean = jnp.mean(head * head, axis=-1, keepdims=True)
            head = head * lax.rsqrt(mean + NORM_EPS) * gain
            front, second = head[:, :half], head[:, half:]
            turned = jnp.concatenate([front * cosine - second * sine, second * cosine + front * sine], 1)
            turned = turned.astype(jnp.bfloat16)
            for n, k in enumerate(steps):
                there = aligned(member ^ k if is_kv else n, rows)
                out[there, h * HD : (h + 1) * HD] = turned[n * rows : (n + 1) * rows]


def attend_kernel(blk_rows, step, store, q_ref, near_ref, piece, length_ref, out):
    _, pair, core = place()
    length = length_ref[0]
    rows = out.shape[0]
    member = (pair * 2 + core) ^ step
    total = store.shape[1]
    quarter = total // 4
    heads = 2 * (out.shape[1] // (2 * HD))
    first = step // 2 * rows
    for j in range(rows // blk_rows):
        block = read_id(piece, piece.shape[0] - ID_ROWS, member * (rows // blk_rows) + j)
        here = slice(first + j * blk_rows, first + (j + 1) * blk_rows)
        there = slice(j * blk_rows, (j + 1) * blk_rows)
        for variant in range(4):
            seen = (variant + 1) * quarter

            @pl.when((block * blk_rows) // quarter == variant)
            def _():
                queries = jnp.concatenate(
                    [ref[here, h * HD : (h + 1) * HD] for ref in (q_ref, near_ref) for h in range(heads // 2)], 0
                )
                shape = (heads * blk_rows, 1)
                query_pos = block * blk_rows + lax.rem(lax.broadcasted_iota(jnp.int32, shape, 0), blk_rows)
                limit = jnp.minimum(query_pos, length - 1)
                key_pos = lax.broadcasted_iota(jnp.int32, (1, seen), 1)
                scores = lax.dot_general(
                    queries,
                    store[0, :seen, :],
                    (((1,), (1,)), ((), ())),
                    preferred_element_type=jnp.float32,
                )
                scores = jnp.where(key_pos <= limit, scores, jnp.finfo(jnp.float32).min)
                weights = jnp.exp(scores - jnp.max(scores, axis=-1, keepdims=True))
                row_sum = jnp.sum(weights, axis=-1, keepdims=True)
                summed = jnp.dot(
                    weights.astype(jnp.bfloat16), store[1, :seen, :], preferred_element_type=jnp.float32
                )
                result = jnp.where(query_pos < length, summed / row_sum, 0.0).astype(jnp.bfloat16)
                for n in range(heads):
                    side = core if n < heads // 2 else 1 - core
                    column = side * (heads // 2) + n % (heads // 2)
                    out[there, aligned(column, HD)] = result[n * blk_rows : (n + 1) * blk_rows]


def live_page(store, table, flat_of, slot, length, blk_rows):
    block = lax.rem(flat_of[slot], table.shape[2])
    page = store[aligned(block, blk_rows), :]
    row = lax.broadcasted_iota(jnp.int32, page.shape, 0)
    return jnp.where(row < length - block * blk_rows, page, jnp.zeros_like(page))


def block_of(pieces, tall, k, j):
    piece, piece_o = pieces
    return read_id(piece_o, k * tall - ID_ROWS, j) if k else read_id(piece, tall - ID_ROWS, j)


def away_kernel(n_out, blk_rows, *refs):
    mine, (piece, piece_o, table, length_ref, away, store, flat_of) = refs[:n_out], refs[n_out:]
    per_piece = mine[0].shape[0] // blk_rows
    for k in range(n_out):
        for j in range(per_piece):
            there = aligned(block_of((piece, piece_o), piece.shape[0], k, j), blk_rows)
            store[there, :] = mine[k][j * blk_rows : (j + 1) * blk_rows, :]
    invert_table(table, flat_of)
    blk = lax.axis_index("blk")
    far = (blk ^ 2) - blk % 2
    slots = away.shape[0] // 2
    for i in range(2 * slots):
        away[i] = live_page(store, table, flat_of, far * slots + i, length_ref[0], blk_rows)


def sort_kernel(n_out, blk_rows, *refs):
    mine, other = refs[:n_out], refs[n_out : 2 * n_out]
    piece, piece_o, store = refs[2 * n_out :]
    _, _, core = place()
    per_piece = mine[0].shape[0] // blk_rows
    for k in range(n_out):
        for j in range(per_piece):
            there = aligned(block_of((piece, piece_o), piece.shape[0], k, j), blk_rows)
            here = slice(j * blk_rows, (j + 1) * blk_rows)
            store[core, there, :] = mine[k][here, :]
            store[1 - core, there, :] = other[k][here, :]


def own_kernel(blk_rows, store, table, length_ref, own, flat_of):
    invert_table(table, flat_of)
    slots = own.shape[0]
    for i in range(slots):
        for half in range(2):
            slot = lax.axis_index("blk") * slots + i
            page = live_page(store.at[half], table, flat_of, slot, length_ref[0], blk_rows)
            own[i, :, half * HD : (half + 1) * HD] = page


def finish_kernel(kept, from_far, own_pages, got, got_near, table, att_out, page_out, flat_of, sems):
    _, pair, core = place()
    invert_table(table, flat_of)
    slots = page_out.shape[0]
    width = kept.shape[1]
    copies = [
        pltpu.make_async_copy(kept, att_out.at[:, aligned(pair, width)], sems.at[0]),
        pltpu.make_async_copy(from_far, att_out.at[:, aligned(1 - pair, width)], sems.at[1]),
    ]
    for copy in copies:
        copy.start()
    for i in range(slots):
        here = lax.div(flat_of[lax.axis_index("blk") * slots + i], table.shape[2]) == pair
        for half in range(2):
            cols = aligned(core if half == 0 else 1 - core, HD)
            there = page_out.at[i, :, cols]
            sem = sems.at[2 + 2 * i + half]
            ours = pltpu.make_async_copy(own_pages.at[i, :, cols], there, sem)
            theirs = pltpu.make_async_copy((got, got_near)[half].at[core * slots + i], there, sem)
            copies.append(ours)

            @pl.when(here)
            def _():
                ours.start()

            @pl.when(jnp.logical_not(here))
            def _():
                theirs.start()

    for copy in copies:
        copy.wait()


def body(tokens, block_ids, lengths, page_table, qkv_weight, q_gain, k_gain):
    n_req, n_blk = lax.axis_size("req"), lax.axis_size("blk")
    n_out = n_blk // TEAM
    bf16 = jnp.bfloat16
    shape = jax.ShapeDtypeStruct
    blk = lax.axis_index("blk")
    member = blk % TEAM

    def in_team(array, k):
        return lax.ppermute(array, "blk", [(i, i ^ k) for i in range(n_blk)])

    def in_req(array, k):
        return lax.ppermute(array, "req", [(i, i ^ k) for i in range(n_req)])

    def across(array, k):
        return lax.ppermute(array, "blk", [(i, (i + TEAM * k) % n_blk) for i in range(n_blk)])

    def sync(*arrays):
        return lax.optimization_barrier(arrays)

    w_rows = qkv_weight.shape[0]
    per_device = block_ids.shape[1]
    own = tokens[0]
    rows = own.shape[0]
    packed_rows = 3 * HD // LANES * w_rows + ID_ROWS
    parts = pl.pallas_call(
        pack_kernel,
        out_shape=[
            shape((packed_rows + (own.size // LANES if k == 1 else 0), LANES), bf16) for k in range(TEAM)
        ],
        in_specs=[pl.BlockSpec(memory_space=pltpu.HBM)] * 3,
        out_specs=[VMEM] * TEAM,
        scratch_shapes=[
            pltpu.VMEM(qkv_weight.shape, bf16),
            pltpu.SMEM(block_ids.shape, jnp.int32),
            pltpu.VMEM(own.shape, bf16),
            pltpu.SemaphoreType.DMA((3,)),
        ],
        compiler_params=params(56),
        name="pack",
    )(qkv_weight, block_ids, own)
    kept_part = pl.pallas_call(
        keep_kernel,
        out_shape=shape(parts[0].shape, bf16),
        in_specs=[VMEM],
        out_specs=VMEM,
        cost_estimate=pl.CostEstimate(flops=10**10, bytes_accessed=MIB, transcendentals=0),
        compiler_params=params(1),
        name="keep",
    )(parts[0])
    got = [kept_part] + [in_team(parts[k], k) for k in range(1, TEAM)]
    kv, q, w = pl.pallas_call(
        team_kernel,
        out_shape=[
            shape((TEAM * w_rows + ID_ROWS, HD), bf16),
            shape((TEAM * w_rows, 2 * HD), bf16),
            shape((TEAM * w_rows, 3 * HD), bf16),
        ],
        in_specs=[VMEM] * TEAM,
        out_specs=[VMEM] * 3,
        compiler_params=params(2),
        name="team",
    )(*got)

    def from_others(piece):
        got = [across(piece, k) for k in range(1, n_out)]
        return got[0] if len(got) == 1 else jnp.concatenate(got, 0)

    kv, q, w, own = sync(kv, q, w, own)
    kv_o, w_x, w_y = from_others(kv), in_req(w, 1), in_req(w, 2)
    q_o, far = from_others(q), in_team(own, 2)

    blk_rows = rows // per_device
    half = HD // 2
    inverse = np.float64(ROPE_BASE) ** (-2.0 * np.arange(half) / HD)
    tables = []
    for positions in (np.arange(per_device * n_blk) * blk_rows, np.arange(blk_rows)):
        angles = positions[:, None] * inverse[None, :]
        tables += [np.cos(angles).astype(np.float32), np.sin(angles).astype(np.float32)]
    cosine, sine = pl.pallas_call(
        angle_kernel,
        out_shape=[shape((TEAM * rows, half), jnp.float32)] * 2,
        in_specs=[VMEM] * 5,
        out_specs=[VMEM] * 2,
        cost_estimate=pl.CostEstimate(flops=10**10, bytes_accessed=40 * 10**6, transcendentals=0),
        compiler_params=params(2),
        name="angles",
    )(kv, *tables)
    slot_count = page_table.shape[1] * page_table.shape[2] // n_blk

    kv_o, w_x, w_y = sync(kv_o, w_x, w_y)
    others = kv_o.shape[0]
    kv_o_x, q_x = pl.pallas_call(
        regroup_kernel,
        out_shape=[shape((others + w_x.shape[0], HD), bf16), shape((w_x.shape[0], 2 * HD), bf16)],
        in_specs=[VMEM] * 2,
        out_specs=[VMEM] * 2,
        compiler_params=params(1),
        name="regroup",
    )(kv_o, w_x)
    kv_ox, kv_oy_d, kv_od = in_req(kv_o, 1), in_req(kv_o_x, 2), in_req(kv_o, 3)
    kv_ox, kv_oy_d, kv_od, q_o, far, cosine, sine = sync(kv_ox, kv_oy_d, kv_od, q_o, far, cosine, sine)
    far_near = in_team(far, 1)
    q_ox, q_oy = in_req(q_o, 1), in_req(q_o, 2)
    kv_weight = [(kv, 0, 0), (kv_o, 0, 0), (w_x, 0, 0), (kv_ox, 0, 0)]
    kv_weight += [(w_y, 0, 0), (kv_oy_d, 0, 0), (kv_oy_d, others, 0), (kv_od, 0, 0)]

    def project(weight, is_kv, gain):
        starts = [part[1:] for part in weight]
        weight = [part[0] for part in weight]
        width = weight[1].shape[1]
        step = weight[1].shape[0] // (n_out - 1)
        depth = own.shape[1]
        n_outs = 1 if is_kv else 2
        return pl.pallas_call(
            functools.partial(project_kernel, n_out, TEAM * w_rows, step, starts, packed_rows, is_kv),
            out_shape=[shape((TEAM * rows // n_outs, width), bf16)] * n_outs,
            in_specs=[VMEM] * (7 + len(weight)),
            out_specs=[VMEM] * n_outs,
            scratch_shapes=[
                pltpu.VMEM((depth, width) if w_rows * TEAM % LANES else (ID_ROWS, LANES), bf16),
                pltpu.SemaphoreType.DMA((n_req * n_out,)),
            ],
            cost_estimate=pl.CostEstimate(
                flops=(0 if is_kv else 0), bytes_accessed=MIB, transcendentals=0
            ),
            compiler_params=params(4 if w_rows * TEAM % LANES == 0 else 12),
            name="project_kv" if is_kv else "project_q",
        )(own, got[1], far, far_near, *weight, gain[None, :], cosine, sine)

    (made,) = project(kv_weight, True, k_gain)
    q_ox, q_oy, q_x = sync(q_ox, q_oy, q_x)
    q_od, q_d = in_req(q_oy, 1), in_req(q_x, 2)
    q_weight = [(q, 0, 0), (q_o, 0, 0), (w_x, 0, HD), (q_ox, 0, 0)]
    q_weight += [(w_y, 0, HD), (q_oy, 0, 0), (q_d, 0, 0), (q_od, 0, 0)]
    mine = [made] + [across(made, k) for k in range(1, n_out)]
    other = [in_team(part, 1) for part in mine]

    total = TEAM * rows * n_out
    store_mib = -(-2 * total * HD * 2 // MIB)
    page_shape = shape((slot_count, blk_rows, 2 * HD), bf16)
    flat_of = pltpu.SMEM((page_table.size,), jnp.int32)
    away_half = pl.pallas_call(
        functools.partial(away_kernel, n_out, blk_rows),
        out_shape=shape((2 * slot_count, blk_rows, HD), bf16),
        in_specs=[VMEM] * (n_out + 2) + [SMEM] * 2,
        out_specs=VMEM,
        scratch_shapes=[pltpu.VMEM((total, HD), bf16), flat_of],
        cost_estimate=pl.CostEstimate(flops=0, bytes_accessed=MIB, transcendentals=0),
        compiler_params=params(store_mib + 1),
        name="away",
    )(*mine, kv, kv_o, page_table, lengths)
    got_half = in_team(away_half, 2)
    away_half, q_od, q_d = sync(away_half, q_od, q_d)
    q_weight[-2:] = [(q_d, 0, 0), (q_od, 0, 0)]

    to_near, queries = project(q_weight, False, q_gain)
    from_near = in_team(to_near, 1)

    store = pl.pallas_call(
        functools.partial(sort_kernel, n_out, blk_rows),
        out_shape=shape((2, total, HD), bf16),
        in_specs=[VMEM] * (2 * n_out + 2),
        out_specs=VMEM,
        cost_estimate=pl.CostEstimate(flops=10**10, bytes_accessed=MIB, transcendentals=0),
        compiler_params=params(store_mib + 1),
        name="sort",
    )(*mine, *other, kv, kv_o)

    def attend(step):
        return pl.pallas_call(
            functools.partial(attend_kernel, blk_rows, step),
            out_shape=shape((rows, H // 2 * HD), bf16),
            in_specs=[VMEM] * 4 + [SMEM],
            out_specs=VMEM,
            cost_estimate=pl.CostEstimate(
                flops=0, bytes_accessed=MIB, transcendentals=0
            ),
            compiler_params=params(store_mib + 2 + 3 * total // 1024),
            name="attend",
        )(store, queries, from_near, kv, lengths)

    from_far = in_team(attend(2), 2)
    kept = attend(0)
    got_half, kept = sync(got_half, kept)
    got_near = in_team(got_half, 1)
    own_pages = pl.pallas_call(
        functools.partial(own_kernel, blk_rows),
        out_shape=page_shape,
        in_specs=[VMEM] + [SMEM] * 2,
        out_specs=VMEM,
        scratch_shapes=[flat_of],
        compiler_params=params(store_mib + 1),
        name="own",
    )(store, page_table, lengths)

    attended, pages = pl.pallas_call(
        finish_kernel,
        out_shape=[shape((rows, H * HD), bf16), page_shape],
        in_specs=[ANY] * 5 + [SMEM],
        out_specs=[ANY] * 2,
        scratch_shapes=[flat_of, pltpu.SemaphoreType.DMA((2 + 2 * slot_count,))],
        compiler_params=params(1),
        name="finish",
    )(kept, from_far, own_pages, got_half, got_near, page_table)
    return attended[None], pages[None]


def solution(mesh):
    in_specs = (
        P("req", "blk", None),
        P("req", "blk"),
        P("req"),
        P("req", None, None),
        P(("req", "blk"), None),
        P(),
        P(),
    )
    out_specs = (P("req", "blk", None), P("req", "blk", None, None))
    return jax.shard_map(body, mesh=mesh, in_specs=in_specs, out_specs=out_specs, check_vma=False)
```

```python
import functools

import jax
import jax.numpy as jnp
import numpy as np
from jax import lax
from jax.experimental import pallas as pl
from jax.experimental.pallas import tpu as pltpu
from jax.sharding import PartitionSpec as P

H = 8
KVH = 2
HD = 256
TEAM = 4
ID_ROWS = 16
LANES = 128
ROPE_BASE = 1000000.0
NORM_EPS = 1e-06
MIB = 1024 * 1024

ANY = pl.BlockSpec(memory_space=pl.ANY)
VMEM = pl.BlockSpec(memory_space=pltpu.VMEM)
SMEM = pl.BlockSpec(memory_space=pltpu.SMEM)


def params(mib):
    return pltpu.CompilerParams(vmem_limit_bytes=mib * MIB)


def place():
    blk = lax.axis_index("blk")
    return lax.axis_index("req"), (blk // 2) % 2, blk % 2


def run(copies):
    for copy in copies:
        copy.start()
    for copy in copies:
        copy.wait()


def aligned(index, size):
    return pl.ds(pl.multiple_of(index * size, size), size)


def q_start(pair, core):
    return pl.multiple_of((pair * 2 + core) * 2 * HD, 2 * HD)


def kv_start(pair, core):
    return pl.multiple_of(H * HD + core * KVH * HD + pair * HD, HD)


def pack_kernel(w_hbm, ids_hbm, tokens_hbm, *refs):
    outs, (w_ref, ids_ref, tokens_ref, sems) = refs[:TEAM], refs[TEAM:]
    run([
        pltpu.make_async_copy(source, there, sems.at[n])
        for n, (source, there) in enumerate(((w_hbm, w_ref), (ids_hbm, ids_ref), (tokens_hbm, tokens_ref)))
    ])
    _, pair, core = place()
    member = pair * 2 + core
    rows = w_ref.shape[0]
    per_device = ids_ref.shape[1]
    lane = lax.broadcasted_iota(jnp.int32, (ID_ROWS, LANES), 1) - member * per_device
    ids = jnp.zeros((ID_ROWS, LANES), jnp.int32)
    for j in range(per_device):
        ids = jnp.where(lane == j, ids_ref[0, j], ids)
    ids = ids.astype(jnp.float32).astype(jnp.bfloat16)
    blocks = 3 * HD // LANES
    for k in range(TEAM):
        to_pair, to_core = pair ^ (k // 2), core ^ (k % 2)
        for n in range(blocks):
            if n < HD // LANES:
                start = pl.multiple_of(kv_start(to_pair, to_core) + n * LANES, LANES)
            else:
                start = pl.multiple_of(q_start(to_pair, to_core) + n * LANES - HD, LANES)
            outs[k][n * rows : (n + 1) * rows, :] = w_ref[:, pl.ds(start, LANES)]
        outs[k][blocks * rows : blocks * rows + ID_ROWS, :] = ids
    token_rows = tokens_ref.shape[0]
    for n in range(tokens_ref.shape[1] // LANES):
        first = blocks * rows + ID_ROWS + n * token_rows
        outs[1][first : first + token_rows, :] = tokens_ref[:, n * LANES : (n + 1) * LANES]


def read_id(piece, row, n):
    ids = piece[row : row + ID_ROWS, :LANES].astype(jnp.float32)[:1]
    if isinstance(n, int):
        return ids[0, n].astype(jnp.int32)
    lane = lax.broadcasted_iota(jnp.int32, ids.shape, 1)
    return jnp.sum(jnp.where(lane == n, ids, 0.0)).astype(jnp.int32)


def angle_kernel(piece, first_cos, first_sin, off_cos, off_sin, cos_out, sin_out):
    blk_rows = off_cos.shape[0]
    for n in range(cos_out.shape[0] // blk_rows):
        block = pl.ds(read_id(piece, piece.shape[0] - ID_ROWS, n), 1)
        here = slice(n * blk_rows, (n + 1) * blk_rows)
        cosine, sine = first_cos[block, :], first_sin[block, :]
        cos_out[here, :] = cosine * off_cos[...] - sine * off_sin[...]
        sin_out[here, :] = sine * off_cos[...] + cosine * off_sin[...]


def invert_table(table, flat_of):
    per_head = table.shape[2]
    for head in range(table.shape[1]):

        @pl.loop(0, per_head)
        def _(block):
            flat_of[table[0, head, block]] = head * per_head + block


def keep_kernel(part, out):
    out[...] = part[...]


def team_kernel(*refs):
    _, pair, core = place()
    parts, (kv_out, q_out, whole) = refs[:TEAM], refs[TEAM:]
    rows = q_out.shape[0] // TEAM
    member = pair * 2 + core
    for k in range(TEAM):
        here = aligned(member ^ k, rows)
        for n in range(3 * HD // LANES):
            out = kv_out if n < HD // LANES else q_out
            first = n * LANES if n < HD // LANES else n * LANES - HD
            part = parts[k][n * rows : (n + 1) * rows, :]
            out[here, first : first + LANES] = part
            whole[here, n * LANES : (n + 1) * LANES] = part
    first = 3 * HD // LANES * rows
    below = [part[first : first + ID_ROWS, :].astype(jnp.float32) for part in parts]
    ids = sum(below[1:], below[0]).astype(jnp.bfloat16)
    kv_out[TEAM * rows :, :] = jnp.concatenate([ids] * (HD // LANES), 1)


def regroup_kernel(kv_o, w_x, kv_out, q_out):
    rows = kv_o.shape[0]
    kv_out[:rows, :] = kv_o[...]
    kv_out[rows:, :] = w_x[:, :HD]
    q_out[...] = w_x[:, HD:]


def project_kernel(n_out, depth, tall, starts, first_row, is_kv, own, near, far, far_near, *refs):
    n_outs = 1 if is_kv else 2
    weights, (gain_ref, cos_ref, sin_ref) = refs[: -5 - n_outs], refs[-5 - n_outs : -2 - n_outs]
    outs, (w_all, sems) = refs[-2 - n_outs : -2], refs[-2:]
    req = lax.axis_index("req")
    outer = lax.axis_index("blk") // TEAM
    _, pair, core = place()
    member = pair * 2 + core
    rows = own.shape[0]
    width = outs[0].shape[1]
    direct = depth % LANES == 0
    places = []
    for i, piece in enumerate(weights):
        from_req = req ^ (i // 2)
        for n in range(n_out - 1 if i % 2 else 1):
            from_outer = lax.rem(outer + n_out - n - i % 2, n_out)
            row, column = starts[i]
            part = piece.at[pl.ds(row + n * tall, depth), column : column + width]
            places.append((part, from_req * n_out + from_outer))
    if not direct:
        run([
            pltpu.make_async_copy(piece, w_all.at[aligned(index, depth), :], sems.at[n])
            for n, (piece, index) in enumerate(places)
        ])
    half = HD // 2
    gain = gain_ref[...]
    if is_kv:
        gain = jnp.where(core == 0, gain, 1.0)
    for out, steps in zip(outs, [(0, 1, 2, 3)] if is_kv else [(1, 3), (0, 2)]):

        def token_rows(k, start, size):
            if k != 1:
                return (own, None, far, far_near)[k][:, pl.ds(start, size)]
            blocks = []
            for n in range(size // LANES):
                first = pl.multiple_of(first_row + (start // LANES + n) * rows, 16)
                blocks.append(near[pl.ds(first, rows), :])
            return jnp.concatenate(blocks, 1)

        def team_rows(start, size):
            return jnp.concatenate([token_rows(k, start, size) for k in steps], 0)

        cosine, sine = (
            jnp.concatenate([ref[aligned(member ^ k, rows), :] for k in steps], 0) for ref in (cos_ref, sin_ref)
        )
        if is_kv:
            cosine = jnp.where(core == 0, cosine, 1.0)
            sine = jnp.where(core == 0, sine, 0.0)
        if direct:
            product = 0.0
            for piece, index in places:
                x = team_rows(pl.multiple_of(index * depth, depth), depth)
                product += jnp.dot(x, piece[...], preferred_element_type=jnp.float32)
        else:
            product = jnp.dot(team_rows(0, w_all.shape[0]), w_all[...], preferred_element_type=jnp.float32)
        for h in range(out.shape[1] // HD):
            head = product[:, h * HD : (h + 1) * HD]
            mean = jnp.mean(head * head, axis=-1, keepdims=True)
            head = head * lax.rsqrt(mean + NORM_EPS) * gain
            front, second = head[:, :half], head[:, half:]
            turned = jnp.concatenate([front * cosine - second * sine, second * cosine + front * sine], 1)
            turned = turned.astype(jnp.bfloat16)
            for n, k in enumerate(steps):
                there = aligned(member ^ k if is_kv else n, rows)
                out[there, h * HD : (h + 1) * HD] = turned[n * rows : (n + 1) * rows]


def attend_kernel(blk_rows, step, store, q_ref, near_ref, piece, length_ref, out):
    _, pair, core = place()
    length = length_ref[0]
    rows = out.shape[0]
    member = (pair * 2 + core) ^ step
    total = store.shape[1]
    quarter = total // 4
    heads = 2 * (out.shape[1] // (2 * HD))
    first = step // 2 * rows
    for j in range(rows // blk_rows):
        block = read_id(piece, piece.shape[0] - ID_ROWS, member * (rows // blk_rows) + j)
        here = slice(first + j * blk_rows, first + (j + 1) * blk_rows)
        there = slice(j * blk_rows, (j + 1) * blk_rows)
        for variant in range(4):
            seen = (variant + 1) * quarter

            @pl.when((block * blk_rows) // quarter == variant)
            def _():
                queries = jnp.concatenate(
                    [ref[here, h * HD : (h + 1) * HD] for ref in (q_ref, near_ref) for h in range(heads // 2)], 0
                )
                shape = (heads * blk_rows, 1)
                query_pos = block * blk_rows + lax.rem(lax.broadcasted_iota(jnp.int32, shape, 0), blk_rows)
                limit = jnp.minimum(query_pos, length - 1)
                key_pos = lax.broadcasted_iota(jnp.int32, (1, seen), 1)
                scores = lax.dot_general(
                    queries,
                    store[0, :seen, :],
                    (((1,), (1,)), ((), ())),
                    preferred_element_type=jnp.float32,
                )
                scores = jnp.where(key_pos <= limit, scores, jnp.finfo(jnp.float32).min)
                weights = jnp.exp(scores - jnp.max(scores, axis=-1, keepdims=True))
                row_sum = jnp.sum(weights, axis=-1, keepdims=True)
                summed = jnp.dot(
                    weights.astype(jnp.bfloat16), store[1, :seen, :], preferred_element_type=jnp.float32
                )
                result = jnp.where(query_pos < length, summed / row_sum, 0.0).astype(jnp.bfloat16)
                for n in range(heads):
                    side = core if n < heads // 2 else 1 - core
                    column = side * (heads // 2) + n % (heads // 2)
                    out[there, aligned(column, HD)] = result[n * blk_rows : (n + 1) * blk_rows]


def live_page(store, table, flat_of, slot, length, blk_rows):
    block = lax.rem(flat_of[slot], table.shape[2])
    page = store[aligned(block, blk_rows), :]
    row = lax.broadcasted_iota(jnp.int32, page.shape, 0)
    return jnp.where(row < length - block * blk_rows, page, jnp.zeros_like(page))


def block_of(pieces, tall, k, j):
    piece, piece_o = pieces
    return read_id(piece_o, k * tall - ID_ROWS, j) if k else read_id(piece, tall - ID_ROWS, j)


def away_kernel(n_out, blk_rows, *refs):
    mine, (piece, piece_o, table, length_ref, away, store, flat_of) = refs[:n_out], refs[n_out:]
    per_piece = mine[0].shape[0] // blk_rows
    for k in range(n_out):
        for j in range(per_piece):
            there = aligned(block_of((piece, piece_o), piece.shape[0], k, j), blk_rows)
            store[there, :] = mine[k][j * blk_rows : (j + 1) * blk_rows, :]
    invert_table(table, flat_of)
    blk = lax.axis_index("blk")
    far = (blk ^ 2) - blk % 2
    slots = away.shape[0] // 2
    for i in range(2 * slots):
        away[i] = live_page(store, table, flat_of, far * slots + i, length_ref[0], blk_rows)


def sort_kernel(n_out, blk_rows, *refs):
    mine, other = refs[:n_out], refs[n_out : 2 * n_out]
    piece, piece_o, store = refs[2 * n_out :]
    _, _, core = place()
    per_piece = mine[0].shape[0] // blk_rows
    for k in range(n_out):
        for j in range(per_piece):
            there = aligned(block_of((piece, piece_o), piece.shape[0], k, j), blk_rows)
            here = slice(j * blk_rows, (j + 1) * blk_rows)
            store[core, there, :] = mine[k][here, :]
            store[1 - core, there, :] = other[k][here, :]


def own_kernel(blk_rows, store, table, length_ref, own, flat_of):
    invert_table(table, flat_of)
    slots = own.shape[0]
    for i in range(slots):
        for half in range(2):
            slot = lax.axis_index("blk") * slots + i
            page = live_page(store.at[half], table, flat_of, slot, length_ref[0], blk_rows)
            own[i, :, half * HD : (half + 1) * HD] = page


def finish_kernel(kept, from_far, own_pages, got, got_near, table, att_out, page_out, flat_of, sems):
    _, pair, core = place()
    invert_table(table, flat_of)
    slots = page_out.shape[0]
    width = kept.shape[1]
    copies = [
        pltpu.make_async_copy(kept, att_out.at[:, aligned(pair, width)], sems.at[0]),
        pltpu.make_async_copy(from_far, att_out.at[:, aligned(1 - pair, width)], sems.at[1]),
    ]
    for copy in copies:
        copy.start()
    for i in range(slots):
        here = lax.div(flat_of[lax.axis_index("blk") * slots + i], table.shape[2]) == pair
        for half in range(2):
            cols = aligned(core if half == 0 else 1 - core, HD)
            there = page_out.at[i, :, cols]
            sem = sems.at[2 + 2 * i + half]
            ours = pltpu.make_async_copy(own_pages.at[i, :, cols], there, sem)
            theirs = pltpu.make_async_copy((got, got_near)[half].at[core * slots + i], there, sem)
            copies.append(ours)

            @pl.when(here)
            def _():
                ours.start()

            @pl.when(jnp.logical_not(here))
            def _():
                theirs.start()

    for copy in copies:
        copy.wait()


def body(tokens, block_ids, lengths, page_table, qkv_weight, q_gain, k_gain):
    n_req, n_blk = lax.axis_size("req"), lax.axis_size("blk")
    n_out = n_blk // TEAM
    bf16 = jnp.bfloat16
    shape = jax.ShapeDtypeStruct
    blk = lax.axis_index("blk")
    member = blk % TEAM

    def in_team(array, k):
        return lax.ppermute(array, "blk", [(i, i ^ k) for i in range(n_blk)])

    def in_req(array, k):
        return lax.ppermute(array, "req", [(i, i ^ k) for i in range(n_req)])

    def across(array, k):
        return lax.ppermute(array, "blk", [(i, (i + TEAM * k) % n_blk) for i in range(n_blk)])

    def sync(*arrays):
        return lax.optimization_barrier(arrays)

    w_rows = qkv_weight.shape[0]
    per_device = block_ids.shape[1]
    own = tokens[0]
    rows = own.shape[0]
    packed_rows = 3 * HD // LANES * w_rows + ID_ROWS
    parts = pl.pallas_call(
        pack_kernel,
        out_shape=[
            shape((packed_rows + (own.size // LANES if k == 1 else 0), LANES), bf16) for k in range(TEAM)
        ],
        in_specs=[pl.BlockSpec(memory_space=pltpu.HBM)] * 3,
        out_specs=[VMEM] * TEAM,
        scratch_shapes=[
            pltpu.VMEM(qkv_weight.shape, bf16),
            pltpu.SMEM(block_ids.shape, jnp.int32),
            pltpu.VMEM(own.shape, bf16),
            pltpu.SemaphoreType.DMA((3,)),
        ],
        compiler_params=params(56),
        name="pack",
    )(qkv_weight, block_ids, own)
    kept_part = pl.pallas_call(
        keep_kernel,
        out_shape=shape(parts[0].shape, bf16),
        in_specs=[VMEM],
        out_specs=VMEM,
        cost_estimate=pl.CostEstimate(flops=10**10, bytes_accessed=MIB, transcendentals=0),
        compiler_params=params(1),
        name="keep",
    )(parts[0])
    got = [kept_part] + [in_team(parts[k], k) for k in range(1, TEAM)]
    kv, q, w = pl.pallas_call(
        team_kernel,
        out_shape=[
            shape((TEAM * w_rows + ID_ROWS, HD), bf16),
            shape((TEAM * w_rows, 2 * HD), bf16),
            shape((TEAM * w_rows, 3 * HD), bf16),
        ],
        in_specs=[VMEM] * TEAM,
        out_specs=[VMEM] * 3,
        compiler_params=params(2),
        name="team",
    )(*got)

    def from_others(piece):
        got = [across(piece, k) for k in range(1, n_out)]
        return got[0] if len(got) == 1 else jnp.concatenate(got, 0)

    kv, q, w, own = sync(kv, q, w, own)
    kv_o, w_x, w_y = from_others(kv), in_req(w, 1), in_req(w, 2)
    q_o, far = from_others(q), in_team(own, 2)

    blk_rows = rows // per_device
    half = HD // 2
    inverse = np.float64(ROPE_BASE) ** (-2.0 * np.arange(half) / HD)
    tables = []
    for positions in (np.arange(per_device * n_blk) * blk_rows, np.arange(blk_rows)):
        angles = positions[:, None] * inverse[None, :]
        tables += [np.cos(angles).astype(np.float32), np.sin(angles).astype(np.float32)]
    cosine, sine = pl.pallas_call(
        angle_kernel,
        out_shape=[shape((TEAM * rows, half), jnp.float32)] * 2,
        in_specs=[VMEM] * 5,
        out_specs=[VMEM] * 2,
        cost_estimate=pl.CostEstimate(flops=10**10, bytes_accessed=40 * 10**6, transcendentals=0),
        compiler_params=params(2),
        name="angles",
    )(kv, *tables)
    slot_count = page_table.shape[1] * page_table.shape[2] // n_blk

    kv_o, w_x, w_y = sync(kv_o, w_x, w_y)
    others = kv_o.shape[0]
    kv_o_x, q_x = pl.pallas_call(
        regroup_kernel,
        out_shape=[shape((others + w_x.shape[0], HD), bf16), shape((w_x.shape[0], 2 * HD), bf16)],
        in_specs=[VMEM] * 2,
        out_specs=[VMEM] * 2,
        compiler_params=params(1),
        name="regroup",
    )(kv_o, w_x)
    kv_ox, kv_oy_d, kv_od = in_req(kv_o, 1), in_req(kv_o_x, 2), in_req(kv_o, 3)
    kv_ox, kv_oy_d, kv_od, q_o, far, cosine, sine = sync(kv_ox, kv_oy_d, kv_od, q_o, far, cosine, sine)
    far_near = in_team(far, 1)
    q_ox, q_oy = in_req(q_o, 1), in_req(q_o, 2)
    kv_weight = [(kv, 0, 0), (kv_o, 0, 0), (w_x, 0, 0), (kv_ox, 0, 0)]
    kv_weight += [(w_y, 0, 0), (kv_oy_d, 0, 0), (kv_oy_d, others, 0), (kv_od, 0, 0)]

    def project(weight, is_kv, gain):
        starts = [part[1:] for part in weight]
        weight = [part[0] for part in weight]
        width = weight[1].shape[1]
        step = weight[1].shape[0] // (n_out - 1)
        depth = own.shape[1]
        n_outs = 1 if is_kv else 2
        return pl.pallas_call(
            functools.partial(project_kernel, n_out, TEAM * w_rows, step, starts, packed_rows, is_kv),
            out_shape=[shape((TEAM * rows // n_outs, width), bf16)] * n_outs,
            in_specs=[VMEM] * (7 + len(weight)),
            out_specs=[VMEM] * n_outs,
            scratch_shapes=[
                pltpu.VMEM((depth, width) if w_rows * TEAM % LANES else (ID_ROWS, LANES), bf16),
                pltpu.SemaphoreType.DMA((n_req * n_out,)),
            ],
            cost_estimate=pl.CostEstimate(
                flops=(0 if is_kv else 4 * 10**9), bytes_accessed=MIB, transcendentals=0
            ),
            compiler_params=params(4 if w_rows * TEAM % LANES == 0 else 12),
            name="project_kv" if is_kv else "project_q",
        )(own, got[1], far, far_near, *weight, gain[None, :], cosine, sine)

    (made,) = project(kv_weight, True, k_gain)
    q_ox, q_oy, q_x, _ = sync(q_ox, q_oy, q_x, made)
    q_od, q_d = in_req(q_oy, 1), in_req(q_x, 2)
    q_weight = [(q, 0, 0), (q_o, 0, 0), (w_x, 0, HD), (q_ox, 0, 0)]
    q_weight += [(w_y, 0, HD), (q_oy, 0, 0), (q_d, 0, 0), (q_od, 0, 0)]
    mine = [made] + [across(made, k) for k in range(1, n_out)]
    other = [in_team(part, 1) for part in mine]

    total = TEAM * rows * n_out
    store_mib = -(-2 * total * HD * 2 // MIB)
    page_shape = shape((slot_count, blk_rows, 2 * HD), bf16)
    flat_of = pltpu.SMEM((page_table.size,), jnp.int32)
    away_half = pl.pallas_call(
        functools.partial(away_kernel, n_out, blk_rows),
        out_shape=shape((2 * slot_count, blk_rows, HD), bf16),
        in_specs=[VMEM] * (n_out + 2) + [SMEM] * 2,
        out_specs=VMEM,
        scratch_shapes=[pltpu.VMEM((total, HD), bf16), flat_of],
        cost_estimate=pl.CostEstimate(flops=0, bytes_accessed=MIB, transcendentals=0),
        compiler_params=params(store_mib + 1),
        name="away",
    )(*mine, kv, kv_o, page_table, lengths)
    got_half = in_team(away_half, 2)
    away_half, q_od, q_d = sync(away_half, q_od, q_d)
    q_weight[-2:] = [(q_d, 0, 0), (q_od, 0, 0)]

    to_near, queries = project(q_weight, False, q_gain)
    from_near = in_team(to_near, 1)

    store = pl.pallas_call(
        functools.partial(sort_kernel, n_out, blk_rows),
        out_shape=shape((2, total, HD), bf16),
        in_specs=[VMEM] * (2 * n_out + 2),
        out_specs=VMEM,
        cost_estimate=pl.CostEstimate(flops=10**10, bytes_accessed=MIB, transcendentals=0),
        compiler_params=params(store_mib + 1),
        name="sort",
    )(*mine, *other, kv, kv_o)

    def attend(step):
        return pl.pallas_call(
            functools.partial(attend_kernel, blk_rows, step),
            out_shape=shape((rows, H // 2 * HD), bf16),
            in_specs=[VMEM] * 4 + [SMEM],
            out_specs=VMEM,
            cost_estimate=pl.CostEstimate(
                flops=0, bytes_accessed=MIB, transcendentals=0
            ),
            compiler_params=params(store_mib + 2 + 3 * total // 1024),
            name="attend",
        )(store, queries, from_near, kv, lengths)

    from_far = in_team(attend(2), 2)
    kept = attend(0)
    got_half, kept = sync(got_half, kept)
    got_near = in_team(got_half, 1)
    own_pages = pl.pallas_call(
        functools.partial(own_kernel, blk_rows),
        out_shape=page_shape,
        in_specs=[VMEM] + [SMEM] * 2,
        out_specs=VMEM,
        scratch_shapes=[flat_of],
        compiler_params=params(store_mib + 1),
        name="own",
    )(store, page_table, lengths)

    attended, pages = pl.pallas_call(
        finish_kernel,
        out_shape=[shape((rows, H * HD), bf16), page_shape],
        in_specs=[ANY] * 5 + [SMEM],
        out_specs=[ANY] * 2,
        scratch_shapes=[flat_of, pltpu.SemaphoreType.DMA((2 + 2 * slot_count,))],
        compiler_params=params(1),
        name="finish",
    )(kept, from_far, own_pages, got_half, got_near, page_table)
    return attended[None], pages[None]


def solution(mesh):
    in_specs = (
        P("req", "blk", None),
        P("req", "blk"),
        P("req"),
        P("req", None, None),
        P(("req", "blk"), None),
        P(),
        P(),
    )
    out_specs = (P("req", "blk", None), P("req", "blk", None, None))
    return jax.shard_map(body, mesh=mesh, in_specs=in_specs, out_specs=out_specs, check_vma=False)
```
